128 devices in a mesh: fsdp: 4 (over z), ctx: 8 (over y, x_hi), tp: 4 (over x_lo, core).
Axes of the slice: x: 4 (x_hi: 2, x_lo: 2; x = x_hi * 2 + x_lo), y: 4, z: 4, core: 2. Of those that a mesh axis runs over, the one named last changes fastest.
Arguments:
- inputs: bfloat16 [8192, 1024], P(('fsdp', 'ctx')), may hold values from -6 to 6
- cotangent: bfloat16 [8192, 1024], P(('fsdp', 'ctx')), may hold values from -6 to 6
- lengths: int32 [4, 4], P('fsdp'), may hold values from 1 to 2048, as said below
- expert_ids: int32 [8192, 8], P(('fsdp', 'ctx')), may hold values from 0 to 31, all different within a row; in each aligned block of 256 rows (0 to 255, 256 to 511, ...) at most 128 rows name the same one
- attn_gain: bfloat16 [1024], P('fsdp'), may hold values from 0.5 to 1.5
- w_query: bfloat16 [1024, 1024], P('fsdp', 'tp'), may hold values from -0.1875 to 0.1875
- key_weight: bfloat16 [1024, 512], P('fsdp', 'tp'), may hold values from -0.1875 to 0.1875
- value_weight: bfloat16 [1024, 512], P('fsdp', 'tp'), may hold values from -0.1875 to 0.1875
- w_output: bfloat16 [1024, 1024], P('fsdp', 'tp'), may hold values from -2 to 2
- ffn_gain: bfloat16 [1024], P('fsdp'), may hold values from 0.5 to 1.5
- w_router: bfloat16 [1024, 32], P('fsdp'), may hold values from -0.09375 to 0.09375
- w_gate: bfloat16 [1024, 32, 512], P('fsdp', None, 'tp'), may hold values from -0.1875 to 0.1875
- w_up: bfloat16 [1024, 32, 512], P('fsdp', None, 'tp'), may hold values from -0.1875 to 0.1875
- w_down: bfloat16 [1024, 32, 512], P('fsdp', None, 'tp'), may hold values from -4 to 4
Outputs:
- output: bfloat16 [8192, 1024], P(('fsdp', 'ctx'))
- input_grad: bfloat16 [8192, 1024], P(('fsdp', 'ctx'))
- grad_attn_gain: float32 [1024], P('fsdp')
- grad_query: float32 [1024, 1024], P('fsdp', 'tp')
- grad_key: float32 [1024, 512], P('fsdp', 'tp')
- grad_value: float32 [1024, 512], P('fsdp', 'tp')
- grad_output: float32 [1024, 1024], P('fsdp', 'tp')
- grad_ffn_gain: float32 [1024], P('fsdp')
- grad_router: float32 [1024, 32], P('fsdp')
- grad_gate: float32 [1024, 32, 512], P('fsdp', None, 'tp')
- grad_up: float32 [1024, 32, 512], P('fsdp', None, 'tp')
- grad_down: float32 [1024, 32, 512], P('fsdp', None, 'tp')
The draws below stay inside these ranges and needn't reach their ends.
Inputs may be any that keep to these rules, and one draw needn't show every extreme that they name: Each row's 4 lengths sum to 2048. `expert_ids`: each row names 8 different experts; the rows of one device name no expert more than 128 times, and in some device's rows one expert is named exactly 128 times.
All inputs are finite; a program needn't handle non-finite values.
Results may differ from the reference program's by a relative error of at most 0.03.
Values may be sent and summed in bfloat16 or wider, within the bound.
A program may use at most 192 MiB of HBM per device.

```python
import math
import jax
import jax.numpy as jnp
import numpy as np
from jax import lax

MODEL_DIM = 1024
QUERY_HEADS = 16
KEY_VALUE_HEADS = 8
HEAD_SIZE = 64
EXPERTS = 32
TOPK = 8
FF = 512
NSEG = 4
PACK_TOKENS = 2048
ROWS = 256
TOKENS = 8192
CAP = 128
N_FSDP = 4


def draw_lengths(key, part):
    key = jax.random.fold_in(key, 11)
    key_place, key_short = jax.random.split(key)
    place = jax.random.randint(key_place, (N_FSDP, 1), 0, NSEG)
    shorts = jax.random.randint(key_short, (N_FSDP, NSEG), 1, ROWS // 4 + 1)
    slots = jnp.arange(NSEG)[None, :]
    shorts = jnp.where(slots == (place + 1) % NSEG, 1, shorts)
    shorts = jnp.where(slots == place, 0, shorts)
    longest = PACK_TOKENS - jnp.sum(shorts, axis=1, keepdims=True)
    return jnp.where(slots == place, longest, shorts).astype(jnp.int32)


def strengthened(entries, key, source, target, blocks, factor):
    def block_of(position):
        return (jnp.arange(entries.shape[position]) // (entries.shape[position] // blocks)).reshape((-1,) + (1,) * (entries.ndim - 1 - position))

    near = jax.random.permutation(key, blocks)[block_of(target)]
    other_side = (block_of(target) + blocks // 2) % blocks
    return jnp.where((block_of(source) == near) | (block_of(source) == other_side), factor * entries, entries)


def steps_of(rng, shape, shards, smallest, largest):
    def one(axis_at, parts):
        draws = jax.random.uniform(jax.random.fold_in(jax.random.fold_in(rng, 6), axis_at), (parts,), jnp.float32, smallest / len(shards), largest / len(shards))
        return jnp.repeat(jnp.exp(draws), shape[axis_at] // parts).reshape((-1,) + (1,) * (len(shape) - axis_at - 1))

    factor_of = one(*shards[0])
    for cut in shards[1:]:
        factor_of = factor_of * one(*cut)
    return factor_of


def shared_out(own_key, own, number, rows, number_of, top, limit, slope):
    ranking = jax.random.permutation(own_key, number_of)
    crowded, usual = load_shares(number_of, rows * top, limit, slope, True), load_shares(number_of, rows * top, limit, slope, False)
    places = jnp.arange(number_of)

    def named(sizes, turn):
        used = int((sizes > 0).sum())
        fixed = max(1, used // 4)
        moved = fixed + (places - fixed + turn * (used - fixed)) % max(1, number_of - fixed)
        return jnp.zeros((number_of,), jnp.int32).at[ranking[jnp.where(places < fixed, places, moved)]].set(jnp.asarray(sizes, jnp.int32))

    sizes = jnp.where(number % 4 == 0, named(crowded, number // 4), named(usual, number - number // 4 - 1))
    mixed = jax.random.permutation(jax.random.fold_in(own, 3), number_of)
    donor, taker = mixed[0:number_of // 2 * 2:2], mixed[1:number_of // 2 * 2:2]
    room = jnp.minimum(sizes[donor] - 1, limit - sizes[taker]) // 2
    room = jnp.where((donor == ranking[0]) | (taker == ranking[0]) | (sizes[taker] == 0), 0, jnp.maximum(room, 0))
    moved = jax.random.randint(jax.random.fold_in(own, 4), (number_of // 2,), 0, 1 << 20) % (room + 1)
    sizes = sizes.at[donor].add(-moved).at[taker].add(moved)
    labels = jnp.searchsorted(jnp.cumsum(sizes), jnp.arange(rows * top), side="right").astype(jnp.int32)
    listing = labels.reshape(top, rows).T
    listing = listing[jax.random.permutation(jax.random.fold_in(own, 1), rows)]
    turn = jax.random.randint(jax.random.fold_in(own, 2), (rows, 1), 0, top)
    return jnp.take_along_axis(listing, (jnp.arange(top)[None, :] + turn) % top, axis=1)


def load_shares(amount, total, limit, lean, full):
    weights = [(1 << 20) // math.isqrt(grade ** lean) + 1 for grade in range(1, amount + 1)]
    largest = limit if full else min(limit, max(-(-total // amount), total * weights[0] // sum(weights)))
    least = 1 if total - largest >= amount - 1 else 0
    given, rest = [largest] + [least] * (amount - 1), total - largest - least * (amount - 1)
    while rest > 0:
        candidates = [i for i in range(1, amount) if given[i] < largest] or [i for i in range(1, amount) if given[i] < limit]
        mass, left = sum([weights[i] for i in candidates]), rest
        for i in candidates:
            extra = min(limit - given[i], max(1, left * weights[i] // mass), rest)
            given[i] = given[i] + extra
            rest = rest - extra
    return np.array(given)


def bell_draw(key, shape, deviation, bound, shards=(), kind=jnp.bfloat16):
    values = jax.random.normal(key, shape, jnp.float32) * deviation
    if len(shards) > 0:
        values = steps_of(key, shape, shards, -0.22, 0.18) * values
    return jnp.clip(values, min=-bound, max=bound).astype(kind)


def heavy_noise(key, extent, spread, reach, pieces, heavy, kind=jnp.bfloat16):
    values = spread * jax.random.normal(key, extent, jnp.float32)
    if pieces:
        values = values * steps_of(key, extent, pieces, -0.22, 0.18)
    return jnp.clip(strengthened(values, jax.random.fold_in(key, 3), *heavy), -reach, reach).astype(kind)


def setup_inputs(seed: int = 0) -> dict:
    key_list = jax.random.split(jax.random.key(seed), 15)
    inputs = heavy_noise(key_list[0], (TOKENS, MODEL_DIM), 1.0, 6.0, ((0, 32),), (0, 1, 32, 2.75))
    cotangent = bell_draw(key_list[1], (TOKENS, MODEL_DIM), 1.0, 6.0, ((0, 32),))
    lengths = draw_lengths(jax.random.fold_in(key_list[14], 71), 0)
    expert_ids_keys = jax.random.split(jax.random.fold_in(key_list[3], 1), TOKENS // ROWS)
    expert_ids_turns = jax.random.permutation(jax.random.fold_in(key_list[3], 3), TOKENS // ROWS)
    expert_ids = jax.vmap(lambda own, number: shared_out(jax.random.fold_in(key_list[3], 2), own, number, ROWS, EXPERTS, TOPK, CAP, 1))(expert_ids_keys, expert_ids_turns).reshape((TOKENS, TOPK))
    attn_gain = jnp.clip(1.0 + 0.1 * jax.random.normal(key_list[4], (MODEL_DIM,), jnp.float32), 0.5, 1.5).astype(jnp.bfloat16)
    w_query = bell_draw(key_list[5], (MODEL_DIM, QUERY_HEADS * HEAD_SIZE), MODEL_DIM ** -0.5, 0.1875, ((0, 4), (1, 4)))
    key_weight = bell_draw(key_list[6], (MODEL_DIM, KEY_VALUE_HEADS * HEAD_SIZE), MODEL_DIM ** -0.5, 0.1875, ((0, 4), (1, 4)))
    value_weight = bell_draw(key_list[7], (MODEL_DIM, KEY_VALUE_HEADS * HEAD_SIZE), MODEL_DIM ** -0.5, 0.1875, ((0, 4), (1, 4)))
    w_output = bell_draw(key_list[8], (MODEL_DIM, QUERY_HEADS * HEAD_SIZE), 8 ** -0.5, 2.0, ((0, 4), (1, 4)))
    ffn_gain = jnp.clip(1.0 + 0.1 * jax.random.normal(key_list[9], (MODEL_DIM,), jnp.float32), 0.5, 1.5).astype(jnp.bfloat16)
    w_router = bell_draw(key_list[10], (MODEL_DIM, EXPERTS), (0.5 * MODEL_DIM ** -0.5), 0.09375, ((0, 4),))
    w_gate = bell_draw(key_list[11], (MODEL_DIM, EXPERTS, FF), MODEL_DIM ** -0.5, 0.1875, ((0, 4), (2, 4)))
    w_up = bell_draw(key_list[12], (MODEL_DIM, EXPERTS, FF), MODEL_DIM ** -0.5, 0.1875, ((0, 4), (2, 4)))
    w_down = bell_draw(key_list[13], (MODEL_DIM, EXPERTS, FF), 2 ** -0.5, 4.0, ((0, 4), (2, 4)))
    return {"inputs": inputs, "cotangent": cotangent, "lengths": lengths, "expert_ids": expert_ids, "attn_gain": attn_gain, "w_query": w_query, "key_weight": key_weight, "value_weight": value_weight, "w_output": w_output, "ffn_gain": ffn_gain, "w_router": w_router, "w_gate": w_gate, "w_up": w_up, "w_down": w_down}


norm_eps = 1e-06
rope_base = 10000.0
branch_scale = 0.22
highest = lax.Precision.HIGHEST

@jax.custom_vjp
def lower_precision(v):
    return lax.optimization_barrier(v.astype(jnp.bfloat16)).astype(jnp.float32)

@jax.custom_vjp
def low_back(v):
    return v

def low_keep(v):
    return (lower_precision(v), None)

def low_pass(kept, grad):
    return (grad,)

def back_keep(v):
    return (v, None)

def back_low(kept, grad):
    return (lower_precision(grad),)
lower_precision.defvjp(low_keep, low_pass)
low_back.defvjp(back_keep, back_low)

def doc_places(lengths_row, rows_global):
    seq_ends = jnp.cumsum(lengths_row).astype(jnp.int32)
    passed = (rows_global[:, None] >= seq_ends[None, :]).astype(jnp.int32)
    docs = lax.optimization_barrier(jnp.sum(passed, axis=1)).astype(jnp.int32)
    starts = lax.optimization_barrier(jnp.sum(passed * lengths_row[None, :], axis=1)).astype(jnp.int32)
    return (docs, rows_global - starts)

def rope_tables(places):
    frequencies = jnp.exp(jnp.arange(HEAD_SIZE // 2, dtype=jnp.float32) * (-2.0 * math.log(rope_base) / HEAD_SIZE))
    angles = places.astype(jnp.float32)[:, None] * frequencies[None, :]
    return (jnp.cos(angles)[:, None, :], jnp.sin(angles)[:, None, :])

def apply_rotary(values, cosine_table, sine_table):
    row_count = values.shape[0]
    head_view = values.reshape(row_count, -1, HEAD_SIZE)
    first_half = head_view[..., :HEAD_SIZE // 2]
    second_half = head_view[..., HEAD_SIZE // 2:]
    turned = jnp.concatenate([first_half * cosine_table - second_half * sine_table, second_half * cosine_table + first_half * sine_table], axis=-1)
    return turned.reshape(row_count, -1)

def rms_norm(values, gain_vector):
    return values * lax.rsqrt(lax.optimization_barrier(jnp.mean(values * values, axis=-1, keepdims=True)) + norm_eps) * gain_vector

def silu_of(values):
    return values * jax.nn.sigmoid(values)

def pack_layer(pack_in, pack_lengths, pack_ids, gain_one, query_w, key_w, value_w, output_w, gain_two, router_w, gate_w, up_w, down_w):
    row_index = jnp.arange(PACK_TOKENS, dtype=jnp.int32)
    docs, places = doc_places(pack_lengths, row_index)
    cosine_table, sine_table = rope_tables(places)
    normed_one = lower_precision(rms_norm(pack_in, gain_one))
    query_pre = low_back(jnp.dot(normed_one, query_w, precision=highest))
    key_unrotated = low_back(jnp.dot(normed_one, key_w, precision=highest))
    value_projected = low_back(jnp.dot(normed_one, value_w, precision=highest))
    queries = lower_precision(apply_rotary(query_pre, cosine_table, sine_table))
    key_entries = lower_precision(apply_rotary(key_unrotated, cosine_table, sine_table)).reshape(PACK_TOKENS, KEY_VALUE_HEADS, HEAD_SIZE)
    value_entries = lower_precision(value_projected).reshape(PACK_TOKENS, KEY_VALUE_HEADS, HEAD_SIZE)
    row_tile = min(512, PACK_TOKENS)
    block_count = PACK_TOKENS // row_tile

    def attend_block(block_item):
        query_tile, block_rows, block_docs = block_item
        query_head_rows = query_tile.reshape(row_tile, KEY_VALUE_HEADS, QUERY_HEADS // KEY_VALUE_HEADS, HEAD_SIZE)
        raw_scores = jnp.einsum('rkgd,skd->kgrs', query_head_rows, key_entries, precision=highest)
        scores = low_back(raw_scores * HEAD_SIZE ** (-0.5))
        allowed = (block_docs[:, None] == docs[None, :]) & (row_index[None, :] <= block_rows[:, None])
        masked = jnp.where(allowed, scores, -1e+30)
        shifted_exp = jnp.exp(masked - lax.optimization_barrier(jnp.max(masked, axis=-1, keepdims=True)))
        attn_probs = lower_precision(shifted_exp / lax.optimization_barrier(jnp.sum(shifted_exp, axis=-1, keepdims=True)))
        outcome = jnp.einsum('kgrs,skd->rkgd', attn_probs, value_entries, precision=highest)
        return outcome.reshape(row_tile, QUERY_HEADS * HEAD_SIZE)
    attended = lax.map(jax.checkpoint(attend_block), (queries.reshape(block_count, row_tile, QUERY_HEADS * HEAD_SIZE), row_index.reshape(block_count, row_tile), docs.reshape(block_count, row_tile)))
    attended = lower_precision(low_back(attended.reshape(PACK_TOKENS, QUERY_HEADS * HEAD_SIZE)))
    attn_out = low_back(jnp.dot(attended, output_w.T, precision=highest))
    residual = pack_in + branch_scale * attn_out
    normed_two = lower_precision(rms_norm(residual, gain_two))
    logits = jnp.dot(normed_two, router_w, precision=highest)
    chosen = jnp.any(pack_ids[:, :, None] == jnp.arange(EXPERTS, dtype=jnp.int32)[None, None, :], axis=1)
    route_masked = jnp.where(chosen, logits, -1e+30)
    route_exp = jnp.exp(route_masked - lax.optimization_barrier(jnp.max(route_masked, axis=-1, keepdims=True)))
    gate_probs = route_exp / lax.optimization_barrier(jnp.sum(route_exp, axis=-1, keepdims=True))
    gate_pre = low_back(jnp.einsum('td,def->tef', normed_two, gate_w, precision=highest))
    up_pre = low_back(jnp.einsum('td,def->tef', normed_two, up_w, precision=highest))
    activation = lower_precision(silu_of(gate_pre) * up_pre)
    outputs = low_back(jnp.einsum('tef,def->ted', activation, down_w, precision=highest))
    expert_sum = lax.optimization_barrier(jnp.sum(gate_probs[:, :, None] * outputs, axis=1))
    return residual + branch_scale * expert_sum

def reference(inputs, cotangent, lengths, expert_ids, attn_gain, w_query, key_weight, value_weight, w_output, ffn_gain, w_router, w_gate, w_up, w_down):

    def forward(hidden_all, gain_one, query_w, key_w, value_w, output_w, gain_two, router_w, gate_w, up_w, down_w):

        def one_pack(unused_carry, pack_item):
            pack_in, pack_lengths, pack_ids = pack_item
            result = pack_layer(pack_in, pack_lengths, pack_ids, gain_one, query_w, key_w, value_w, output_w, gain_two, router_w, gate_w, up_w, down_w)
            return (unused_carry, result)
        _, pack_outputs = lax.scan(jax.checkpoint(one_pack), jnp.zeros((), jnp.float32), (hidden_all.reshape(N_FSDP, PACK_TOKENS, MODEL_DIM), lengths, expert_ids.reshape(N_FSDP, PACK_TOKENS, TOPK)))
        return pack_outputs.reshape(TOKENS, MODEL_DIM)
    output, pullback = jax.vjp(forward, inputs.astype(jnp.float32), attn_gain.astype(jnp.float32), w_query.astype(jnp.float32), key_weight.astype(jnp.float32), value_weight.astype(jnp.float32), w_output.astype(jnp.float32), ffn_gain.astype(jnp.float32), w_router.astype(jnp.float32), w_gate.astype(jnp.float32), w_up.astype(jnp.float32), w_down.astype(jnp.float32))
    gradients = pullback(cotangent.astype(jnp.float32))
    return (output.astype(jnp.bfloat16), gradients[0].astype(jnp.bfloat16), gradients[1], gradients[2], gradients[3], gradients[4], gradients[5], gradients[6], gradients[7], gradients[8], gradients[9], gradients[10])
```

```python
import functools
import math

import jax
import jax.numpy as jnp
from jax import lax
from jax.experimental import pallas as pl
from jax.experimental.pallas import tpu as pltpu
from jax.sharding import PartitionSpec as P

HEAD_SIZE = 64
CAP = 128
MESH = pl.DeviceIdType.MESH

norm_eps = 1e-06
rope_base = 10000.0
branch_scale = 0.22
highest = lax.Precision.HIGHEST
bf16 = jnp.bfloat16
f32 = jnp.float32


def exchange_kernel(plan, sizes, *refs):
    count = len(plan)
    ins, outs = refs[:count], refs[count : 2 * count]
    send_sem, recv_sem, self_sem = refs[2 * count :]

    def place(axes, step):
        offsets = []
        for axis in reversed(axes):
            offsets.append(step % sizes[axis])
            step //= sizes[axis]
        coords = {}
        for axis, offset in zip(axes, offsets[::-1]):
            here = lax.axis_index(axis)
            coords[axis] = lax.rem(here + offset, sizes[axis]) if offset else here
        return coords

    def flat(axes, coords):
        index = 0
        for axis in axes:
            index = index * sizes[axis] + coords[axis]
        return index

    groups = {}
    for axes, _ in plan:
        for step in range(1, math.prod(sizes[a] for a in axes)):
            full, rest = {}, step
            for axis in reversed(axes):
                full[axis] = rest % sizes[axis]
                rest //= sizes[axis]
            key = tuple(sorted((a, o) for a, o in full.items() if o))
            groups[key] = (axes, step)
    barrier = pltpu.get_barrier_semaphore()
    for axes, step in groups.values():
        pl.semaphore_signal(barrier, inc=1, device_id=place(axes, step), device_id_type=MESH)
    pl.semaphore_wait(barrier, len(groups))

    copies = []
    for at, (axes, mode) in enumerate(plan):
        mine = flat(axes, place(axes, 0))
        for step in range(1, math.prod(sizes[a] for a in axes)):
            peer = place(axes, step)
            copy = pltpu.make_async_remote_copy(
                src_ref=ins[at] if mode == "g" else ins[at].at[flat(axes, peer)],
                dst_ref=outs[at].at[mine],
                send_sem=send_sem.at[at, step],
                recv_sem=recv_sem.at[at, step],
                device_id=peer,
                device_id_type=MESH,
            )
            copy.start()
            copies.append(copy)
        own = pltpu.make_async_copy(
            ins[at] if mode == "g" else ins[at].at[mine], outs[at].at[mine], self_sem.at[at]
        )
        own.start()
        copies.append(own)
    for copy in copies:
        copy.wait()


def exchange(sizes, collective_id, *items):
    plan = [(axes, mode) for axes, mode, _ in items]
    arrays = [array for _, _, array in items]
    outs = []
    most = 1
    for axes, mode, array in items:
        n = math.prod(sizes[a] for a in axes)
        most = max(most, n)
        shape = (n,) + array.shape if mode == "g" else array.shape
        outs.append(jax.ShapeDtypeStruct(shape, array.dtype))
    count = len(items)
    moved = sum(math.prod(o.shape) * o.dtype.itemsize for o in outs)
    return pl.pallas_call(
        functools.partial(exchange_kernel, plan, sizes),
        out_shape=outs,
        in_specs=[pl.BlockSpec(memory_space=pl.ANY)] * count,
        out_specs=[pl.BlockSpec(memory_space=pl.ANY)] * count,
        scratch_shapes=[
            pltpu.SemaphoreType.DMA((count, most)),
            pltpu.SemaphoreType.DMA((count, most)),
            pltpu.SemaphoreType.DMA((count,)),
        ],
        compiler_params=pltpu.CompilerParams(collective_id=collective_id, has_side_effects=True),
        cost_estimate=pl.CostEstimate(flops=0, bytes_accessed=20 * moved, transcendentals=0),
        name="exchange_%d" % collective_id,
    )(*arrays)


def rope_tables(places):
    frequencies = jnp.exp(
        jnp.arange(HEAD_SIZE // 2, dtype=jnp.float32) * (-2.0 * math.log(rope_base) / HEAD_SIZE)
    )
    angles = places.astype(jnp.float32)[:, None] * frequencies[None, :]
    return (jnp.cos(angles)[:, None, :], jnp.sin(angles)[:, None, :])


def turn(values, cosine_table, sine_table):
    row_count = values.shape[0]
    head_view = values.reshape(row_count, -1, HEAD_SIZE)
    first_half = head_view[..., : HEAD_SIZE // 2]
    second_half = head_view[..., HEAD_SIZE // 2 :]
    turned = jnp.concatenate(
        [
            first_half * cosine_table - second_half * sine_table,
            second_half * cosine_table + first_half * sine_table,
        ],
        axis=-1,
    )
    return turned.reshape(row_count, -1)


def contract_rows(left, right, precision=None):
    return lax.dot_general(
        left, right, (((0,), (0,)), ((), ())), precision=precision, preferred_element_type=f32
    )


def contract_cols(left, right, precision=None):
    return lax.dot_general(
        left, right, (((1,), (1,)), ((), ())), precision=precision, preferred_element_type=f32
    )


def mm(left, right):
    return jnp.dot(left, right, preferred_element_type=f32)


def local(
    sizes,
    inputs,
    cotangent,
    lengths,
    expert_ids,
    attn_gain,
    w_query,
    key_weight,
    value_weight,
    w_output,
    ffn_gain,
    w_router,
    w_gate,
    w_up,
    w_down,
):
    rows, width = inputs.shape
    n_fsdp, n_ctx, n_tp = sizes["fsdp"], sizes["ctx"], sizes["tp"]
    experts = w_router.shape[1]
    depth, _, ff = w_gate.shape
    per_ctx = experts // n_ctx
    send = functools.partial(exchange, sizes)
    ctx_at, tp_at = lax.axis_index("ctx"), lax.axis_index("tp")

    chosen = jnp.any(
        expert_ids[:, :, None] == jnp.arange(experts, dtype=jnp.int32)[None, None, :], axis=1
    )
    mine = jnp.arange(n_ctx, dtype=jnp.int32) * per_ctx + tp_at
    chosen_mine = jnp.any(expert_ids[None, :, :] == mine[:, None, None], axis=2)
    earlier = jnp.arange(rows)[:, None] < jnp.arange(rows)[None, :]
    rank = mm(chosen_mine.astype(bf16), earlier.astype(bf16))
    slots = jnp.arange(CAP, dtype=f32)
    picks = (chosen_mine[:, None, :] & (rank[:, None, :] == slots[None, :, None])).astype(bf16)
    picks_flat = picks.reshape(n_ctx * CAP, rows)
    grads_sent = mm(picks_flat, cotangent).astype(bf16).reshape(n_ctx, CAP, width)

    first = ctx_at * per_ctx
    own_slices = jnp.stack(
        [
            lax.dynamic_slice_in_dim(w, first, per_ctx, 1).transpose(1, 0, 2)
            for w in (w_gate, w_up, w_down)
        ],
        axis=1,
    )
    gains = jnp.concatenate(
        [
            attn_gain.reshape(-1, 128),
            ffn_gain.reshape(-1, 128),
            jnp.zeros((16 - 2 * depth // 128, 128), bf16),
        ],
        axis=0,
    )
    router_pad = jnp.pad(w_router, ((0, 0), (0, 128 - experts)))
    query_w, key_w, value_w, gains_all, router_all, expert_slices, grads_got = send(
        0,
        (("fsdp",), "g", w_query),
        (("fsdp",), "g", key_weight),
        (("fsdp",), "g", value_weight),
        (("fsdp",), "g", gains),
        (("fsdp",), "g", router_pad),
        (("tp",), "a", own_slices),
        (("ctx",), "a", grads_sent),
    )
    query_w = query_w.reshape(width, -1)
    key_w = key_w.reshape(width, -1)
    value_w = value_w.reshape(width, -1)
    lines = depth // 128
    gain_one = gains_all[:, :lines].reshape(width).astype(f32)
    gain_two = gains_all[:, lines : 2 * lines].reshape(width).astype(f32)
    router_w = router_all.reshape(width, 128)[:, :experts]
    grad_rows = grads_got.reshape(n_ctx * CAP, width)

    output_w = lax.all_gather(w_output, "fsdp", axis=0, tiled=True)
    output_full = lax.all_gather(output_w, "tp", axis=1, tiled=True)
    expert_cat = expert_slices.transpose(2, 1, 0, 3).reshape(depth, 3 * n_tp * ff)
    expert_w = lax.all_gather(expert_cat, "fsdp", axis=0, tiled=True)
    hidden_units = n_tp * ff
    gate_up_w, down_w = expert_w[:, : 2 * hidden_units], expert_w[:, 2 * hidden_units :]

    lengths_row = lengths[0]
    query_rows = ctx_at * rows + jnp.arange(rows, dtype=jnp.int32)
    seq_ends = jnp.cumsum(lengths_row)
    passed = (query_rows[:, None] >= seq_ends[None, :]).astype(jnp.int32)
    starts = jnp.sum(passed * lengths_row[None, :], axis=1)
    cosine_table, sine_table = rope_tables(query_rows - starts)
    hidden_in = inputs.astype(f32)
    scale_one = lax.rsqrt(jnp.mean(hidden_in * hidden_in, axis=-1, keepdims=True) + norm_eps)
    normed_one = (hidden_in * scale_one * gain_one).astype(bf16)
    queries = turn(mm(normed_one, query_w), cosine_table, sine_table).astype(bf16)
    keys_local = turn(mm(normed_one, key_w), cosine_table, sine_table).astype(bf16)
    values_local = mm(normed_one, value_w).astype(bf16)
    pairs_local = jnp.concatenate([keys_local, values_local], axis=1)
    pair_width = keys_local.shape[1]
    (pairs_all,) = send(1, (("ctx",), "g", pairs_local))
    total_rows = n_ctx * rows
    pairs_all = pairs_all.reshape(total_rows, 2 * pair_width)
    key_heads = pair_width // HEAD_SIZE
    groups = queries.shape[1] // pair_width
    keys_all = pairs_all[:, :pair_width].reshape(total_rows, key_heads, HEAD_SIZE)
    values_all = pairs_all[:, pair_width:].reshape(total_rows, key_heads, HEAD_SIZE)
    query_head_rows = queries.reshape(rows, key_heads, groups, HEAD_SIZE)
    key_rows = jnp.arange(total_rows, dtype=jnp.int32)
    allowed = (key_rows[None, :] >= starts[:, None]) & (key_rows[None, :] <= query_rows[:, None])

    def masked_scores():
        raw_scores = jnp.einsum(
            "rkgd,skd->kgrs", query_head_rows, keys_all, preferred_element_type=f32
        )
        return jnp.where(allowed, raw_scores * HEAD_SIZE ** (-0.5), -1e30)

    masked = masked_scores()
    row_top = jnp.max(masked, axis=-1, keepdims=True)
    shifted_exp = jnp.exp(masked - row_top)
    row_total = jnp.sum(shifted_exp, axis=-1, keepdims=True)
    attn_probs = shifted_exp / row_total
    log_total = row_top + jnp.log(row_total)
    attended = jnp.einsum(
        "kgrs,skd->rkgd", attn_probs.astype(bf16), values_all, preferred_element_type=f32
    )
    attended = attended.reshape(rows, -1).astype(bf16)
    (attended_all,) = send(2, (("tp",), "g", attended))
    attended_all = attended_all.transpose(1, 0, 2).reshape(rows, -1)
    residual = hidden_in + branch_scale * contract_cols(attended_all, output_full)

    scale_two = lax.rsqrt(jnp.mean(residual * residual, axis=-1, keepdims=True) + norm_eps)
    normed_two = (residual * scale_two * gain_two).astype(bf16)
    logits = mm(normed_two, router_w)
    route_masked = jnp.where(chosen, logits, -1e30)
    route_exp = jnp.exp(route_masked - jnp.max(route_masked, axis=-1, keepdims=True))
    gate_probs = route_exp / jnp.sum(route_exp, axis=-1, keepdims=True)
    probs_mine = lax.dynamic_index_in_dim(
        gate_probs.T.reshape(n_ctx, per_ctx, rows), tp_at, 1, keepdims=False
    )
    probs_sent = jnp.sum(picks.astype(f32) * probs_mine[:, None, :], axis=2)
    rows_sent = mm(picks_flat, normed_two).astype(bf16).reshape(n_ctx, CAP, width)
    rows_got, probs_got = send(
        3,
        (("ctx",), "a", rows_sent),
        (("ctx",), "a", jnp.broadcast_to(probs_sent[:, None, :], (n_ctx, 8, CAP))),
    )

    norm_rows = rows_got.reshape(n_ctx * CAP, width)
    probs_col = probs_got[:, 0, :].reshape(n_ctx * CAP, 1)
    gate_up = mm(norm_rows, gate_up_w)
    gate_pre, up_pre = gate_up[:, :hidden_units], gate_up[:, hidden_units:]
    down_back = mm(grad_rows, down_w)
    sigmoid_gate = jax.nn.sigmoid(gate_pre)
    silu_gate = gate_pre * sigmoid_gate
    activation = silu_gate * up_pre
    gate_grad_rows = branch_scale * jnp.sum(activation * down_back, axis=1)
    act_grad = (branch_scale * probs_col) * down_back
    gate_in = act_grad * up_pre * sigmoid_gate * (1.0 + gate_pre * (1.0 - sigmoid_gate))
    both_in = jnp.concatenate([gate_in, act_grad * silu_gate], axis=1).astype(bf16)
    weighted = (probs_col * activation).astype(bf16)
    mixed = contract_cols(weighted, down_w).astype(bf16)
    norm_grad = contract_cols(both_in, gate_up_w).astype(bf16)
    gate_grad_rows = jnp.broadcast_to(gate_grad_rows.reshape(n_ctx, 1, CAP), (n_ctx, 8, CAP))
    grad_gate_up = contract_rows(norm_rows, both_in)
    grad_down = contract_rows(grad_rows, weighted) * branch_scale
    expert_grad = jnp.concatenate([grad_gate_up, grad_down], axis=1).astype(bf16)

    norm_grad_got, mixed_got, gate_grad_got = send(
        4,
        (("ctx",), "a", norm_grad.reshape(n_ctx, CAP, width)),
        (("ctx",), "a", mixed.reshape(n_ctx, CAP, width)),
        (("ctx",), "a", gate_grad_rows),
    )

    expert_grad = lax.psum_scatter(expert_grad, "fsdp", scatter_dimension=0, tiled=True)
    expert_grad = expert_grad.reshape(depth, 3, n_tp, ff).transpose(2, 1, 0, 3)
    pieces = [lax.dynamic_index_in_dim(expert_grad, tp_at, 0, keepdims=False)]
    for step in range(1, n_tp):
        piece = lax.dynamic_index_in_dim(
            expert_grad, lax.rem(tp_at + step, n_tp), 0, keepdims=False
        )
        pieces.append(lax.ppermute(piece, "tp", [(s, (s + step) % n_tp) for s in range(n_tp)]))
    pieces = jnp.stack(pieces)
    pieces = jnp.take(pieces, lax.rem(tp_at - jnp.arange(n_tp) + n_tp, n_tp), axis=0)
    expert_all = lax.all_gather(pieces, "ctx", axis=0, tiled=True)
    expert_all = expert_all.transpose(1, 2, 0, 3).astype(f32)

    norm_grad_part = contract_rows(picks_flat, norm_grad_got.reshape(n_ctx * CAP, width))
    mixed_part = contract_rows(picks_flat, mixed_got.reshape(n_ctx * CAP, width)).astype(bf16)
    gate_grad_part = jnp.sum(picks.astype(f32) * gate_grad_got[:, 0, :, None], axis=1)
    norm_grad_parts, gate_grad_parts = send(
        5, (("tp",), "g", norm_grad_part.astype(bf16)), (("tp",), "g", gate_grad_part)
    )
    gate_grads = gate_grad_parts.transpose(2, 1, 0).reshape(rows, experts)
    route_grad = gate_probs * (
        gate_grads - jnp.sum(gate_probs * gate_grads, axis=-1, keepdims=True)
    )
    grad_router = contract_rows(normed_two.astype(f32), route_grad, highest)
    router_back = contract_cols(route_grad, router_w.astype(f32), highest)
    out_grad = cotangent.astype(f32)
    normed_grad = jnp.sum(norm_grad_parts.astype(f32), axis=0) + router_back
    weighted_two = normed_grad * gain_two
    grad_ffn_gain = jnp.sum(normed_grad * residual * scale_two, axis=0)
    residual_grad = (
        out_grad
        + scale_two * weighted_two
        - residual * scale_two**3 * jnp.mean(weighted_two * residual, axis=-1, keepdims=True)
    )
    attn_in = (branch_scale * residual_grad).astype(bf16)
    grad_output = contract_rows(attn_in, attended)
    attended_grad = mm(attn_in, output_w).astype(bf16)

    grad_heads = attended_grad.reshape(rows, key_heads, groups, HEAD_SIZE)
    attn_probs = jnp.exp(masked_scores() - log_total)
    value_grad_all = jnp.einsum(
        "kgrs,rkgd->skd", attn_probs.astype(bf16), grad_heads, preferred_element_type=f32
    )
    prob_grad = jnp.einsum("rkgd,skd->kgrs", grad_heads, values_all, preferred_element_type=f32)
    score_grad = (
        attn_probs * (prob_grad - jnp.sum(attn_probs * prob_grad, axis=-1, keepdims=True))
    ).astype(bf16)
    query_grad_rot = jnp.einsum(
        "kgrs,skd->rkgd", score_grad, keys_all, preferred_element_type=f32
    ).reshape(rows, -1) * HEAD_SIZE ** (-0.5)
    key_grad_all = jnp.einsum(
        "kgrs,rkgd->skd", score_grad, query_head_rows, preferred_element_type=f32
    ) * HEAD_SIZE ** (-0.5)
    pair_grads = jnp.concatenate(
        [
            key_grad_all.reshape(total_rows, pair_width),
            value_grad_all.reshape(total_rows, pair_width),
        ],
        axis=1,
    ).astype(bf16)
    (pair_got,) = send(6, (("ctx",), "a", pair_grads.reshape(n_ctx, rows, 2 * pair_width)))
    pair_owned = jnp.sum(pair_got.astype(f32), axis=0)
    query_grad = turn(query_grad_rot, cosine_table, -sine_table).astype(bf16)
    key_grad = turn(pair_owned[:, :pair_width], cosine_table, -sine_table).astype(bf16)
    value_grad = pair_owned[:, pair_width:].astype(bf16)
    normed_one_part = (
        contract_cols(query_grad, query_w)
        + contract_cols(key_grad, key_w)
        + contract_cols(value_grad, value_w)
    )
    grad_gain_part = jnp.sum(normed_one_part * hidden_in * scale_one, axis=0)
    grad_query = contract_rows(normed_one, query_grad)
    grad_key = contract_rows(normed_one, key_grad)
    grad_value = contract_rows(normed_one, value_grad)

    n_rows = n_fsdp * n_ctx
    share = width // n_rows
    side = jnp.concatenate(
        [grad_router, grad_ffn_gain[:, None], jnp.zeros((width, 128 - experts - 1), f32)], axis=1
    )
    small = jnp.concatenate([grad_query, grad_key, grad_value, grad_output, side], axis=1)
    small = small.astype(bf16).reshape(n_rows, share, -1)
    gain_chunks = jnp.broadcast_to(
        jnp.pad(grad_gain_part.reshape(n_rows, 1, share), ((0, 0), (0, 0), (0, 128 - share))),
        (n_rows, 8, 128),
    )
    one_parts, mixed_parts, small_got, gain_got = send(
        7,
        (("tp",), "g", normed_one_part.astype(bf16)),
        (("tp",), "g", mixed_part),
        (("fsdp", "ctx"), "a", small),
        (("fsdp", "ctx"), "a", gain_chunks),
    )
    small_sum = jnp.sum(small_got.astype(f32), axis=0).astype(bf16)
    gain_sum = jnp.sum(gain_got, axis=0)
    small_all, gain_all = send(
        8, (("ctx",), "g", small_sum), (("ctx", "tp"), "g", gain_sum)
    )
    small_all = small_all.reshape(depth, -1).astype(f32)
    gain_all = gain_all[:, 0, :share].reshape(n_ctx, n_tp, share)
    grad_attn_gain = jnp.sum(gain_all, axis=1).reshape(depth)

    output = residual + branch_scale * jnp.sum(mixed_parts.astype(f32), axis=0)
    normed_one_grad = jnp.sum(one_parts.astype(f32), axis=0)
    weighted_one = normed_one_grad * gain_one
    input_grad = (
        residual_grad
        + scale_one * weighted_one
        - hidden_in * scale_one**3 * jnp.mean(weighted_one * hidden_in, axis=-1, keepdims=True)
    )
    q_end = queries.shape[1]
    k_end, v_end = q_end + pair_width, q_end + 2 * pair_width
    o_end = v_end + attended.shape[1]
    return (
        output.astype(bf16),
        input_grad.astype(bf16),
        grad_attn_gain,
        small_all[:, :q_end],
        small_all[:, q_end:k_end],
        small_all[:, k_end:v_end],
        small_all[:, v_end:o_end],
        small_all[:, o_end + experts],
        small_all[:, o_end : o_end + experts],
        expert_all[0],
        expert_all[1],
        expert_all[2],
    )


def solution(mesh):
    sizes = dict(mesh.shape)
    return jax.shard_map(
        functools.partial(local, sizes),
        mesh=mesh,
        in_specs=(
            P(("fsdp", "ctx"), None),
            P(("fsdp", "ctx"), None),
            P("fsdp", None),
            P(("fsdp", "ctx"), None),
            P("fsdp"),
            P("fsdp", "tp"),
            P("fsdp", "tp"),
            P("fsdp", "tp"),
            P("fsdp", "tp"),
            P("fsdp"),
            P("fsdp", None),
            P("fsdp", None, "tp"),
            P("fsdp", None, "tp"),
            P("fsdp", None, "tp"),
        ),
        out_specs=(
            P(("fsdp", "ctx"), None),
            P(("fsdp", "ctx"), None),
            P("fsdp"),
            P("fsdp", "tp"),
            P("fsdp", "tp"),
            P("fsdp", "tp"),
            P("fsdp", "tp"),
            P("fsdp"),
            P("fsdp", None),
            P("fsdp", None, "tp"),
            P("fsdp", None, "tp"),
            P("fsdp", None, "tp"),
        ),
        check_vma=False,
    )
```

```python
import functools
import math

import jax
import jax.numpy as jnp
from jax import lax
from jax.experimental import pallas as pl
from jax.experimental.pallas import tpu as pltpu
from jax.sharding import PartitionSpec as P

HEAD_SIZE = 64
CAP = 128
MESH = pl.DeviceIdType.MESH

norm_eps = 1e-06
rope_base = 10000.0
branch_scale = 0.22
highest = lax.Precision.HIGHEST
bf16 = jnp.bfloat16
f32 = jnp.float32


def exchange_kernel(plan, sizes, *refs):
    count = len(plan)
    ins, outs = refs[:count], refs[count : 2 * count]
    send_sem, recv_sem, self_sem = refs[2 * count :]

    def place(axes, step):
        offsets = []
        for axis in reversed(axes):
            offsets.append(step % sizes[axis])
            step //= sizes[axis]
        coords = {}
        for axis, offset in zip(axes, offsets[::-1]):
            here = lax.axis_index(axis)
            coords[axis] = lax.rem(here + offset, sizes[axis]) if offset else here
        return coords

    def flat(axes, coords):
        index = 0
        for axis in axes:
            index = index * sizes[axis] + coords[axis]
        return index

    groups = {}
    for axes, _ in plan:
        for step in range(1, math.prod(sizes[a] for a in axes)):
            full, rest = {}, step
            for axis in reversed(axes):
                full[axis] = rest % sizes[axis]
                rest //= sizes[axis]
            key = tuple(sorted((a, o) for a, o in full.items() if o))
            groups[key] = (axes, step)
    barrier = pltpu.get_barrier_semaphore()
    for axes, step in groups.values():
        pl.semaphore_signal(barrier, inc=1, device_id=place(axes, step), device_id_type=MESH)
    pl.semaphore_wait(barrier, len(groups))

    copies = []
    for at, (axes, mode) in enumerate(plan):
        mine = flat(axes, place(axes, 0))
        for step in range(1, math.prod(sizes[a] for a in axes)):
            if mode in "fb":
                peer = place(axes, step if mode == "f" else sizes[axes[0]] - step)
                source, slot = ins[at].at[step], step
            else:
                peer = place(axes, step)
                source = ins[at] if mode == "g" else ins[at].at[flat(axes, peer)]
                slot = mine
            copy = pltpu.make_async_remote_copy(
                src_ref=source,
                dst_ref=outs[at].at[slot],
                send_sem=send_sem.at[at, step],
                recv_sem=recv_sem.at[at, step],
                device_id=peer,
                device_id_type=MESH,
            )
            copy.start()
            copies.append(copy)
        if mode in "fb":
            mine = 0
        own = pltpu.make_async_copy(
            ins[at] if mode == "g" else ins[at].at[mine], outs[at].at[mine], self_sem.at[at]
        )
        own.start()
        copies.append(own)
    for copy in copies:
        copy.wait()


def exchange(sizes, collective_id, *items):
    plan = [(axes, mode) for axes, mode, _ in items]
    arrays = [array for _, _, array in items]
    outs = []
    most = 1
    for axes, mode, array in items:
        n = math.prod(sizes[a] for a in axes)
        most = max(most, n)
        shape = (n,) + array.shape if mode == "g" else array.shape
        outs.append(jax.ShapeDtypeStruct(shape, array.dtype))
    count = len(items)
    moved = sum(math.prod(o.shape) * o.dtype.itemsize for o in outs)
    return pl.pallas_call(
        functools.partial(exchange_kernel, plan, sizes),
        out_shape=outs,
        in_specs=[pl.BlockSpec(memory_space=pl.ANY)] * count,
        out_specs=[pl.BlockSpec(memory_space=pl.ANY)] * count,
        scratch_shapes=[
            pltpu.SemaphoreType.DMA((count, most)),
            pltpu.SemaphoreType.DMA((count, most)),
            pltpu.SemaphoreType.DMA((count,)),
        ],
        compiler_params=pltpu.CompilerParams(collective_id=collective_id, has_side_effects=True),
        cost_estimate=pl.CostEstimate(flops=0, bytes_accessed=20 * moved, transcendentals=0),
        name="exchange_%d" % collective_id,
    )(*arrays)


def spread_kernel(n_ctx, n_tp, pieces_ref, *out_refs):
    experts = n_ctx * n_tp
    tp_at = lax.axis_index("tp")
    depth = pieces_ref.shape[2]
    for which, out_ref in enumerate(out_refs):
        for place in range(experts):
            step = place % n_tp
            expert = place - step + lax.rem(tp_at + n_tp - step, n_tp)
            out_ref[pl.ds(expert, depth, stride=experts), :] = pieces_ref[place, which].astype(f32)


def spread(pieces, n_ctx, n_tp):
    experts, count, depth, ff = pieces.shape
    block = 64
    outs = pl.pallas_call(
        functools.partial(spread_kernel, n_ctx, n_tp),
        grid=(depth // block,),
        out_shape=[jax.ShapeDtypeStruct((depth * experts, ff), f32)] * count,
        in_specs=[pl.BlockSpec((experts, count, block, ff), lambda i: (0, 0, i, 0))],
        out_specs=[pl.BlockSpec((block * experts, ff), lambda i: (i, 0))] * count,
        compiler_params=pltpu.CompilerParams(vmem_limit_bytes=32 * 1024 * 1024),
        name="spread",
    )(pieces)
    return [out.reshape(depth, experts, ff) for out in outs]


def rope_tables(places):
    frequencies = jnp.exp(
        jnp.arange(HEAD_SIZE // 2, dtype=jnp.float32) * (-2.0 * math.log(rope_base) / HEAD_SIZE)
    )
    angles = places.astype(jnp.float32)[:, None] * frequencies[None, :]
    return (jnp.cos(angles)[:, None, :], jnp.sin(angles)[:, None, :])


def turn(values, cosine_table, sine_table):
    row_count = values.shape[0]
    head_view = values.reshape(row_count, -1, HEAD_SIZE)
    first_half = head_view[..., : HEAD_SIZE // 2]
    second_half = head_view[..., HEAD_SIZE // 2 :]
    turned = jnp.concatenate(
        [
            first_half * cosine_table - second_half * sine_table,
            second_half * cosine_table + first_half * sine_table,
        ],
        axis=-1,
    )
    return turned.reshape(row_count, -1)


def contract_rows(left, right, precision=None):
    return lax.dot_general(
        left, right, (((0,), (0,)), ((), ())), precision=precision, preferred_element_type=f32
    )


def contract_cols(left, right, precision=None):
    return lax.dot_general(
        left, right, (((1,), (1,)), ((), ())), precision=precision, preferred_element_type=f32
    )


def mm(left, right):
    return jnp.dot(left, right, preferred_element_type=f32)


def local(
    sizes,
    inputs,
    cotangent,
    lengths,
    expert_ids,
    attn_gain,
    w_query,
    key_weight,
    value_weight,
    w_output,
    ffn_gain,
    w_router,
    w_gate,
    w_up,
    w_down,
):
    rows, width = inputs.shape
    n_fsdp, n_ctx, n_tp = sizes["fsdp"], sizes["ctx"], sizes["tp"]
    experts = w_router.shape[1]
    depth, _, ff = w_gate.shape
    per_ctx = experts // n_ctx
    send = functools.partial(exchange, sizes)
    ctx_at, tp_at = lax.axis_index("ctx"), lax.axis_index("tp")

    chosen = jnp.any(
        expert_ids[:, :, None] == jnp.arange(experts, dtype=jnp.int32)[None, None, :], axis=1
    )
    ctx_order = lax.rem(ctx_at + jnp.arange(n_ctx, dtype=jnp.int32), n_ctx)
    mine = ctx_order * per_ctx + tp_at
    chosen_mine = jnp.any(expert_ids[None, :, :] == mine[:, None, None], axis=2)
    earlier = jnp.arange(rows)[:, None] < jnp.arange(rows)[None, :]
    rank = mm(chosen_mine.astype(bf16), earlier.astype(bf16))
    slots = jnp.arange(CAP, dtype=f32)
    picks = (chosen_mine[:, None, :] & (rank[:, None, :] == slots[None, :, None])).astype(bf16)
    picks_flat = picks.reshape(n_ctx * CAP, rows)

    def shifted(chunks, axis, direction):
        n = chunks.shape[0]
        return jnp.stack(
            [chunks[0]]
            + [
                lax.ppermute(chunks[k], axis, [(s, (s + direction * k) % n) for s in range(n)])
                for k in range(1, n)
            ]
        )

    first = ctx_at * per_ctx
    tp_order = lax.rem(tp_at + jnp.arange(n_tp, dtype=jnp.int32), n_tp)
    own_slices = jnp.stack(
        [
            lax.dynamic_slice_in_dim(w, first, per_ctx, 1).transpose(1, 0, 2)
            for w in (w_gate, w_up, w_down)
        ],
        axis=1,
    )
    gains = jnp.concatenate(
        [
            attn_gain.reshape(-1, 128),
            ffn_gain.reshape(-1, 128),
            jnp.zeros((16 - 2 * depth // 128, 128), bf16),
        ],
        axis=0,
    )
    router_pad = jnp.pad(w_router, ((0, 0), (0, 128 - experts)))
    grads_sent = mm(picks_flat, cotangent).astype(bf16).reshape(n_ctx, CAP, width)
    query_w, key_w, value_w, output_w, gains_all, router_all, expert_slices, grad_rows = send(
        0,
        (("fsdp",), "g", w_query),
        (("fsdp",), "g", key_weight),
        (("fsdp",), "g", value_weight),
        (("fsdp",), "g", w_output),
        (("fsdp",), "g", gains),
        (("fsdp",), "g", router_pad),
        (("tp",), "a", own_slices),
        (("ctx",), "f", grads_sent),
    )
    query_w = query_w.reshape(width, -1)
    key_w = key_w.reshape(width, -1)
    value_w = value_w.reshape(width, -1)
    output_w = output_w.reshape(width, -1)
    lines = depth // 128
    gain_one = gains_all[:, :lines].reshape(width).astype(f32)
    gain_two = gains_all[:, lines : 2 * lines].reshape(width).astype(f32)
    router_w = router_all.reshape(width, 128)[:, :experts]

    grad_rows = grad_rows.reshape(n_ctx * CAP, width)

    output_full = lax.all_gather(output_w, "tp", axis=1, tiled=True)
    expert_cat = expert_slices.transpose(2, 1, 0, 3).reshape(depth, 3 * n_tp * ff)
    expert_w = lax.all_gather(expert_cat, "fsdp", axis=0, tiled=True)
    hidden_units = n_tp * ff
    gate_up_w, down_w = expert_w[:, : 2 * hidden_units], expert_w[:, 2 * hidden_units :]

    lengths_row = lengths[0]
    query_rows = ctx_at * rows + jnp.arange(rows, dtype=jnp.int32)
    seq_ends = jnp.cumsum(lengths_row)
    passed = (query_rows[:, None] >= seq_ends[None, :]).astype(jnp.int32)
    starts = jnp.sum(passed * lengths_row[None, :], axis=1)
    cosine_table, sine_table = rope_tables(query_rows - starts)
    hidden_in = inputs.astype(f32)
    scale_one = lax.rsqrt(jnp.mean(hidden_in * hidden_in, axis=-1, keepdims=True) + norm_eps)
    normed_one = (hidden_in * scale_one * gain_one).astype(bf16)
    queries = turn(mm(normed_one, query_w), cosine_table, sine_table).astype(bf16)
    keys_local = turn(mm(normed_one, key_w), cosine_table, sine_table).astype(bf16)
    values_local = mm(normed_one, value_w).astype(bf16)
    pairs_local = jnp.concatenate([keys_local, values_local], axis=1)
    pair_width = keys_local.shape[1]
    (pairs_all,) = send(1, (("ctx",), "g", pairs_local))
    total_rows = n_ctx * rows
    pairs_all = pairs_all.reshape(total_rows, 2 * pair_width)
    key_heads = pair_width // HEAD_SIZE
    groups = queries.shape[1] // pair_width
    keys_all = pairs_all[:, :pair_width].reshape(total_rows, key_heads, HEAD_SIZE)
    values_all = pairs_all[:, pair_width:].reshape(total_rows, key_heads, HEAD_SIZE)
    query_head_rows = queries.reshape(rows, key_heads, groups, HEAD_SIZE)
    key_rows = jnp.arange(total_rows, dtype=jnp.int32)
    allowed = (key_rows[None, :] >= starts[:, None]) & (key_rows[None, :] <= query_rows[:, None])

    def masked_scores():
        raw_scores = jnp.einsum(
            "rkgd,skd->kgrs", query_head_rows, keys_all, preferred_element_type=f32
        )
        return jnp.where(allowed, raw_scores * HEAD_SIZE ** (-0.5), -1e30)

    masked = masked_scores()
    row_top = jnp.max(masked, axis=-1, keepdims=True)
    shifted_exp = jnp.exp(masked - row_top)
    row_total = jnp.sum(shifted_exp, axis=-1, keepdims=True)
    attn_probs = shifted_exp / row_total
    log_total = row_top + jnp.log(row_total)
    attended = jnp.einsum(
        "kgrs,skd->rkgd", attn_probs.astype(bf16), values_all, preferred_element_type=f32
    )
    attended = attended.reshape(rows, -1).astype(bf16)
    (attended_all,) = send(2, (("tp",), "g", attended))
    attended_all = attended_all.transpose(1, 0, 2).reshape(rows, -1)
    residual = hidden_in + branch_scale * contract_cols(attended_all, output_full)

    scale_two = lax.rsqrt(jnp.mean(residual * residual, axis=-1, keepdims=True) + norm_eps)
    normed_two = (residual * scale_two * gain_two).astype(bf16)
    logits = mm(normed_two, router_w)
    route_masked = jnp.where(chosen, logits, -1e30)
    route_exp = jnp.exp(route_masked - jnp.max(route_masked, axis=-1, keepdims=True))
    gate_probs = route_exp / jnp.sum(route_exp, axis=-1, keepdims=True)
    probs_mine = lax.dynamic_index_in_dim(
        gate_probs.T.reshape(n_ctx, per_ctx, rows), tp_at, 1, keepdims=False
    )
    probs_mine = jnp.take(probs_mine, ctx_order, axis=0)
    probs_sent = jnp.sum(picks.astype(f32) * probs_mine[:, None, :], axis=2)
    rows_sent = mm(picks_flat, normed_two).astype(bf16).reshape(n_ctx, CAP, width)
    rows_got, probs_got = send(
        3,
        (("ctx",), "f", rows_sent),
        (("ctx",), "f", jnp.broadcast_to(probs_sent[:, None, :], (n_ctx, 8, CAP))),
    )

    norm_rows = rows_got.reshape(n_ctx * CAP, width)
    probs_col = probs_got[:, 0, :].reshape(n_ctx * CAP, 1)
    gate_up = mm(norm_rows, gate_up_w)
    gate_pre, up_pre = gate_up[:, :hidden_units], gate_up[:, hidden_units:]
    down_back = mm(grad_rows, down_w)
    sigmoid_gate = jax.nn.sigmoid(gate_pre)
    silu_gate = gate_pre * sigmoid_gate
    activation = silu_gate * up_pre
    gate_grad_rows = branch_scale * jnp.sum(activation * down_back, axis=1)
    act_grad = (branch_scale * probs_col) * down_back
    gate_in = act_grad * up_pre * sigmoid_gate * (1.0 + gate_pre * (1.0 - sigmoid_gate))
    both_in = jnp.concatenate([gate_in, act_grad * silu_gate], axis=1).astype(bf16)
    weighted = (probs_col * activation).astype(bf16)
    mixed = contract_cols(weighted, down_w).astype(bf16).reshape(n_ctx, CAP, width)
    norm_grad = contract_cols(both_in, gate_up_w).astype(bf16)
    gate_grad_rows = jnp.broadcast_to(gate_grad_rows.reshape(n_ctx, 1, CAP), (n_ctx, 8, CAP))
    grad_gate_up = contract_rows(norm_rows, both_in)
    grad_down = contract_rows(grad_rows, weighted) * branch_scale
    expert_grad = jnp.concatenate([grad_gate_up, grad_down], axis=1).astype(bf16)
    expert_grad = lax.psum_scatter(expert_grad, "fsdp", scatter_dimension=0, tiled=True)

    norm_grad_got, gate_grad_got, mixed_got = send(
        4,
        (("ctx",), "b", norm_grad.reshape(n_ctx, CAP, width)),
        (("ctx",), "b", gate_grad_rows),
        (("ctx",), "b", mixed),
    )

    quarter = rows // n_tp
    norm_grad_part = contract_rows(picks_flat, norm_grad_got.reshape(n_ctx * CAP, width))
    gate_grad_part = jnp.sum(picks.astype(f32) * gate_grad_got[:, 0, :, None], axis=1)
    norm_grad_parts, gate_grad_parts = send(
        5,
        (("tp",), "a", norm_grad_part.astype(bf16).reshape(n_tp, quarter, width)),
        (("tp",), "g", gate_grad_part),
    )

    expert_grad, _ = lax.optimization_barrier((expert_grad, gate_grad_parts))
    expert_grad = expert_grad.reshape(depth, 3, n_tp, ff).transpose(2, 1, 0, 3)
    pieces = shifted(jnp.take(expert_grad, tp_order, axis=0), "tp", 1)
    expert_all = lax.all_gather(pieces, "ctx", axis=0, tiled=True)

    def quarter_of(array):
        return lax.dynamic_slice_in_dim(array, tp_at * quarter, quarter, 0)

    back_order = lax.rem(jnp.arange(n_ctx, dtype=jnp.int32) + n_ctx - ctx_at, n_ctx)
    gate_grads = jnp.take(gate_grad_parts, back_order, axis=1)
    gate_grads = gate_grads.transpose(2, 1, 0).reshape(rows, experts)
    route_grad = gate_probs * (
        gate_grads - jnp.sum(gate_probs * gate_grads, axis=-1, keepdims=True)
    )
    grad_router = contract_rows(normed_two.astype(f32), route_grad, highest)
    router_back = contract_cols(quarter_of(route_grad), router_w.astype(f32), highest)
    normed_grad = jnp.sum(norm_grad_parts.astype(f32), axis=0) + router_back
    weighted_two = normed_grad * gain_two
    residual_own, scale_two_own = quarter_of(residual), quarter_of(scale_two)
    grad_ffn_part = jnp.sum(normed_grad * residual_own * scale_two_own, axis=0)
    residual_grad = (
        quarter_of(cotangent).astype(f32)
        + scale_two_own * weighted_two
        - residual_own
        * scale_two_own**3
        * jnp.mean(weighted_two * residual_own, axis=-1, keepdims=True)
    )
    (attn_in,) = send(6, (("tp",), "g", (branch_scale * residual_grad).astype(bf16)))
    attn_in = attn_in.reshape(rows, width)
    grad_output = contract_rows(attn_in, attended)
    attended_grad = mm(attn_in, output_w).astype(bf16)

    grad_heads = attended_grad.reshape(rows, key_heads, groups, HEAD_SIZE)
    attn_probs = jnp.exp(masked_scores() - log_total)
    value_grad_all = jnp.einsum(
        "kgrs,rkgd->skd", attn_probs.astype(bf16), grad_heads, preferred_element_type=f32
    )
    prob_grad = jnp.einsum("rkgd,skd->kgrs", grad_heads, values_all, preferred_element_type=f32)
    score_grad = (
        attn_probs * (prob_grad - jnp.sum(attn_probs * prob_grad, axis=-1, keepdims=True))
    ).astype(bf16)
    query_grad_rot = jnp.einsum(
        "kgrs,skd->rkgd", score_grad, keys_all, preferred_element_type=f32
    ).reshape(rows, -1) * HEAD_SIZE ** (-0.5)
    key_grad_all = jnp.einsum(
        "kgrs,rkgd->skd", score_grad, query_head_rows, preferred_element_type=f32
    ) * HEAD_SIZE ** (-0.5)
    pair_grads = jnp.concatenate(
        [
            key_grad_all.reshape(total_rows, pair_width),
            value_grad_all.reshape(total_rows, pair_width),
        ],
        axis=1,
    ).astype(bf16)
    (pair_got,) = send(7, (("ctx",), "a", pair_grads.reshape(n_ctx, rows, 2 * pair_width)))
    pair_owned = jnp.sum(pair_got.astype(f32), axis=0)
    query_grad = turn(query_grad_rot, cosine_table, -sine_table).astype(bf16)
    key_grad = turn(pair_owned[:, :pair_width], cosine_table, -sine_table).astype(bf16)
    value_grad = pair_owned[:, pair_width:].astype(bf16)
    normed_one_part = (
        contract_cols(query_grad, query_w)
        + contract_cols(key_grad, key_w)
        + contract_cols(value_grad, value_w)
    )
    grad_gain_part = jnp.sum(normed_one_part * hidden_in * scale_one, axis=0)
    grad_query = contract_rows(normed_one, query_grad)
    grad_key = contract_rows(normed_one, key_grad)
    grad_value = contract_rows(normed_one, value_grad)
    mixed_part = contract_rows(picks_flat, mixed_got.reshape(n_ctx * CAP, width)).astype(bf16)

    n_rows = n_fsdp * n_ctx
    share = width // n_rows
    side = jnp.pad(grad_router, ((0, 0), (0, 128 - experts)))
    small = jnp.concatenate([grad_query, grad_key, grad_value, grad_output, side], axis=1)
    small = small.astype(bf16).reshape(n_rows, share, -1)
    gain_parts = jnp.stack([grad_gain_part, grad_ffn_part]).reshape(2, n_rows, share)
    gain_chunks = jnp.pad(gain_parts.transpose(1, 0, 2), ((0, 0), (0, 6), (0, 128 - share)))
    one_parts, mixed_parts, small_got, gain_got = send(
        8,
        (("tp",), "a", normed_one_part.astype(bf16).reshape(n_tp, quarter, width)),
        (("tp",), "a", mixed_part.reshape(n_tp, quarter, width)),
        (("fsdp", "ctx"), "a", small),
        (("fsdp", "ctx"), "a", gain_chunks),
    )
    small_sum = jnp.sum(small_got.astype(f32), axis=0).astype(bf16)
    gain_sum = jnp.sum(gain_got, axis=0)
    output = residual_own + branch_scale * jnp.sum(mixed_parts.astype(f32), axis=0)
    normed_one_grad = jnp.sum(one_parts.astype(f32), axis=0)
    weighted_one = normed_one_grad * gain_one
    hidden_own, scale_one_own = quarter_of(hidden_in), quarter_of(scale_one)
    input_grad = (
        residual_grad
        + scale_one_own * weighted_one
        - hidden_own
        * scale_one_own**3
        * jnp.mean(weighted_one * hidden_own, axis=-1, keepdims=True)
    )
    small_all, gain_all, output, input_grad = send(
        9,
        (("ctx",), "g", small_sum),
        (("ctx", "tp"), "g", gain_sum),
        (("tp",), "g", output.astype(bf16)),
        (("tp",), "g", input_grad.astype(bf16)),
    )
    small_all = small_all.reshape(depth, -1).astype(f32)
    gain_all = jnp.sum(gain_all[:, :2, :share].reshape(n_ctx, n_tp, 2, share), axis=1)
    gain_all = gain_all.transpose(1, 0, 2).reshape(2, depth)
    grad_gate, grad_up, grad_down = spread(expert_all, n_ctx, n_tp)
    q_end = queries.shape[1]
    k_end, v_end = q_end + pair_width, q_end + 2 * pair_width
    o_end = v_end + attended.shape[1]
    return (
        output.reshape(rows, width),
        input_grad.reshape(rows, width),
        gain_all[0],
        small_all[:, :q_end],
        small_all[:, q_end:k_end],
        small_all[:, k_end:v_end],
        small_all[:, v_end:o_end],
        gain_all[1],
        small_all[:, o_end : o_end + experts],
        grad_gate,
        grad_up,
        grad_down,
    )


def solution(mesh):
    sizes = dict(mesh.shape)
    return jax.shard_map(
        functools.partial(local, sizes),
        mesh=mesh,
        in_specs=(
            P(("fsdp", "ctx"), None),
            P(("fsdp", "ctx"), None),
            P("fsdp", None),
            P(("fsdp", "ctx"), None),
            P("fsdp"),
            P("fsdp", "tp"),
            P("fsdp", "tp"),
            P("fsdp", "tp"),
            P("fsdp", "tp"),
            P("fsdp"),
            P("fsdp", None),
            P("fsdp", None, "tp"),
            P("fsdp", None, "tp"),
            P("fsdp", None, "tp"),
        ),
        out_specs=(
            P(("fsdp", "ctx"), None),
            P(("fsdp", "ctx"), None),
            P("fsdp"),
            P("fsdp", "tp"),
            P("fsdp", "tp"),
            P("fsdp", "tp"),
            P("fsdp", "tp"),
            P("fsdp"),
            P("fsdp", None),
            P("fsdp", None, "tp"),
            P("fsdp", None, "tp"),
            P("fsdp", None, "tp"),
        ),
        check_vma=False,
    )
```

```python
import functools
import math

import jax
import jax.numpy as jnp
from jax import lax
from jax.experimental import pallas as pl
from jax.experimental.pallas import tpu as pltpu
from jax.sharding import PartitionSpec as P

HEAD_SIZE = 64
CAP = 128
MESH = pl.DeviceIdType.MESH

norm_eps = 1e-06
rope_base = 10000.0
branch_scale = 0.22
highest = lax.Precision.HIGHEST
bf16 = jnp.bfloat16
f32 = jnp.float32


def exchange_kernel(plan, sizes, *refs):
    count = len(plan)
    ins, outs = refs[:count], refs[count : 2 * count]
    send_sem, recv_sem, self_sem = refs[2 * count :]

    def place(axes, step):
        offsets = []
        for axis in reversed(axes):
            offsets.append(step % sizes[axis])
            step //= sizes[axis]
        coords = {}
        for axis, offset in zip(axes, offsets[::-1]):
            here = lax.axis_index(axis)
            coords[axis] = lax.rem(here + offset, sizes[axis]) if offset else here
        return coords

    def flat(axes, coords):
        index = 0
        for axis in axes:
            index = index * sizes[axis] + coords[axis]
        return index

    groups = {}
    for axes, _ in plan:
        for step in range(1, math.prod(sizes[a] for a in axes)):
            full, rest = {}, step
            for axis in reversed(axes):
                full[axis] = rest % sizes[axis]
                rest //= sizes[axis]
            key = tuple(sorted((a, o) for a, o in full.items() if o))
            groups[key] = (axes, step)
    barrier = pltpu.get_barrier_semaphore()
    for axes, step in groups.values():
        pl.semaphore_signal(barrier, inc=1, device_id=place(axes, step), device_id_type=MESH)
    pl.semaphore_wait(barrier, len(groups))

    copies = []
    for at, (axes, mode) in enumerate(plan):
        mine = flat(axes, place(axes, 0))
        for step in range(1, math.prod(sizes[a] for a in axes)):
            if mode in "fb":
                peer = place(axes, step if mode == "f" else sizes[axes[0]] - step)
                source, slot = ins[at].at[step], step
            else:
                peer = place(axes, step)
                source = ins[at] if mode == "g" else ins[at].at[flat(axes, peer)]
                slot = mine
            copy = pltpu.make_async_remote_copy(
                src_ref=source,
                dst_ref=outs[at].at[slot],
                send_sem=send_sem.at[at, step],
                recv_sem=recv_sem.at[at, step],
                device_id=peer,
                device_id_type=MESH,
            )
            copy.start()
            copies.append(copy)
        if mode in "fb":
            mine = 0
        own = pltpu.make_async_copy(
            ins[at] if mode == "g" else ins[at].at[mine], outs[at].at[mine], self_sem.at[at]
        )
        own.start()
        copies.append(own)
    for copy in copies:
        copy.wait()


def exchange(sizes, collective_id, *items):
    plan = [(axes, mode) for axes, mode, _ in items]
    arrays = [array for _, _, array in items]
    outs = []
    most = 1
    for axes, mode, array in items:
        n = math.prod(sizes[a] for a in axes)
        most = max(most, n)
        shape = (n,) + array.shape if mode == "g" else array.shape
        outs.append(jax.ShapeDtypeStruct(shape, array.dtype))
    count = len(items)
    moved = sum(math.prod(o.shape) * o.dtype.itemsize for o in outs)
    return pl.pallas_call(
        functools.partial(exchange_kernel, plan, sizes),
        out_shape=outs,
        in_specs=[pl.BlockSpec(memory_space=pl.ANY)] * count,
        out_specs=[pl.BlockSpec(memory_space=pl.ANY)] * count,
        scratch_shapes=[
            pltpu.SemaphoreType.DMA((count, most)),
            pltpu.SemaphoreType.DMA((count, most)),
            pltpu.SemaphoreType.DMA((count,)),
        ],
        compiler_params=pltpu.CompilerParams(collective_id=collective_id, has_side_effects=True),
        cost_estimate=pl.CostEstimate(flops=0, bytes_accessed=20 * moved, transcendentals=0),
        name="exchange_%d" % collective_id,
    )(*arrays)


def spread_kernel(n_ctx, n_tp, pieces_ref, *out_refs):
    experts = n_ctx * n_tp
    tp_at = lax.axis_index("tp")
    depth = pieces_ref.shape[2]
    for which, out_ref in enumerate(out_refs):
        for place in range(experts):
            step = place % n_tp
            expert = place - step + lax.rem(tp_at + n_tp - step, n_tp)
            out_ref[pl.ds(expert, depth, stride=experts), :] = pieces_ref[place, which].astype(f32)


def spread(pieces, n_ctx, n_tp):
    experts, count, depth, ff = pieces.shape
    block = 64
    outs = pl.pallas_call(
        functools.partial(spread_kernel, n_ctx, n_tp),
        grid=(depth // block,),
        out_shape=[jax.ShapeDtypeStruct((depth * experts, ff), f32)] * count,
        in_specs=[pl.BlockSpec((experts, count, block, ff), lambda i: (0, 0, i, 0))],
        out_specs=[pl.BlockSpec((block * experts, ff), lambda i: (i, 0))] * count,
        compiler_params=pltpu.CompilerParams(vmem_limit_bytes=32 * 1024 * 1024),
        name="spread",
    )(pieces)
    return [out.reshape(depth, experts, ff) for out in outs]


def expert_kernel(
    n,
    rows_ref,
    probs_ref,
    grads_ref,
    w_ref,
    norm_got,
    mixed_got,
    gate_got,
    wgrad_ref,
    norm_buf,
    probs_buf,
    both_buf,
    weighted_buf,
    back_buf,
    mixed_buf,
    gate_buf,
    send_sems,
    recv_sems,
):
    me = lax.axis_index("ctx")
    hidden = w_ref.shape[1] // 3

    def chunk(ref, k):
        return ref.at[pl.ds(pl.multiple_of(k * CAP, CAP), CAP)]

    def copy(which, k, source, target, place):
        return pltpu.make_async_remote_copy(
            src_ref=source,
            dst_ref=target,
            send_sem=send_sems.at[which, k],
            recv_sem=recv_sems.at[which, k],
            device_id={"ctx": lax.rem(place, n)},
            device_id_type=MESH,
        )

    def out_copies(k):
        return (
            copy(0, k, chunk(rows_ref, k), chunk(norm_buf, k), me + k),
            copy(1, k, probs_ref.at[k], probs_buf.at[k], me + k),
        )

    def back_copies(k):
        place = me + n - k
        return (
            copy(2, k, chunk(back_buf, k), chunk(norm_got, k), place),
            copy(3, k, gate_buf.at[k], gate_got.at[k], place),
            copy(4, k, chunk(mixed_buf, k), chunk(mixed_got, k), place),
        )

    barrier = pltpu.get_barrier_semaphore()
    for k in range(1, n):
        pl.semaphore_signal(
            barrier, inc=1, device_id={"ctx": lax.rem(me + k, n)}, device_id_type=MESH
        )
    pl.semaphore_wait(barrier, n - 1)
    for k in range(1, n):
        for item in out_copies(k):
            item.start()
    norm_buf[:CAP] = rows_ref[:CAP]
    probs_buf[0] = probs_ref[0]
    same = lax.broadcasted_iota(jnp.int32, (CAP, CAP), 0) == lax.broadcasted_iota(
        jnp.int32, (CAP, CAP), 1
    )

    def pair(j, carry):
        for k in (2 * j, 2 * j + 1):

            @pl.when(k > 0)
            def _():
                for item in out_copies(k):
                    item.wait_recv()

        here = pl.ds(pl.multiple_of(j * 2 * CAP, 2 * CAP), 2 * CAP)
        gate_up = mm(norm_buf[here, :], w_ref[:, : 2 * hidden])
        down_back = mm(grads_ref[here, :], w_ref[:, 2 * hidden :])
        probs = jnp.concatenate(
            [
                jnp.sum(jnp.where(same, probs_buf[k][:1, :], 0.0), axis=1, keepdims=True)
                for k in (2 * j, 2 * j + 1)
            ],
            axis=0,
        )
        gate_pre, up_pre = gate_up[:, :hidden], gate_up[:, hidden:]
        sig = jax.nn.sigmoid(gate_pre)
        silu = gate_pre * sig
        activation = silu * up_pre
        gate_grad = branch_scale * jnp.sum(activation * down_back, axis=1, keepdims=True)
        act_grad = (branch_scale * probs) * down_back
        both_buf[here, :hidden] = (
            act_grad * up_pre * sig * (1.0 + gate_pre * (1.0 - sig))
        ).astype(bf16)
        both_buf[here, hidden:] = (act_grad * silu).astype(bf16)
        weighted_buf[here, :] = (probs * activation).astype(bf16)
        back_buf[here, :] = contract_cols(both_buf[here, :], w_ref[:, : 2 * hidden]).astype(bf16)
        for i in range(2):
            line = jnp.sum(
                jnp.where(same, gate_grad[i * CAP : (i + 1) * CAP], 0.0), axis=0, keepdims=True
            )
            gate_buf[2 * j + i] = jnp.broadcast_to(line, (8, CAP))
        mixed_buf[here, :] = contract_cols(weighted_buf[here, :], w_ref[:, 2 * hidden :]).astype(
            bf16
        )
        for k in (2 * j, 2 * j + 1):

            @pl.when(k > 0)
            def _():
                for item in back_copies(k):
                    item.start()

        return carry

    lax.fori_loop(0, n // 2, pair, 0)
    norm_got[:CAP] = back_buf[:CAP]
    mixed_got[:CAP] = mixed_buf[:CAP]
    gate_got[0] = gate_buf[0]

    width = w_ref.shape[0]
    part = 256

    def weight_grads(j, carry):
        here = pl.ds(pl.multiple_of(j * part, part), part)
        wgrad_ref[here, : 2 * hidden] = contract_rows(norm_buf[:, here], both_buf[...]).astype(bf16)
        wgrad_ref[here, 2 * hidden :] = (
            contract_rows(grads_ref[:, here], weighted_buf[...]) * branch_scale
        ).astype(bf16)
        return carry

    lax.fori_loop(0, width // part, weight_grads, 0)
    for k in range(1, n):
        for item in out_copies(k):
            item.wait_send()
        for item in back_copies(k):
            item.wait()


def expert_of_place(sizes, rows_sent, probs_sent, grad_rows, expert_w):
    n = sizes["ctx"]
    total, width = rows_sent.shape
    columns = expert_w.shape[1]
    hidden = columns // 3
    like = jax.ShapeDtypeStruct
    vmem = pl.BlockSpec(memory_space=pltpu.VMEM)
    return pl.pallas_call(
        functools.partial(expert_kernel, n),
        out_shape=[
            like((total, width), bf16),
            like((total, width), bf16),
            like(probs_sent.shape, f32),
            like((width, columns), bf16),
        ],
        in_specs=[vmem] * 4,
        out_specs=[vmem] * 4,
        scratch_shapes=[
            pltpu.VMEM((total, width), bf16),
            pltpu.VMEM(probs_sent.shape, f32),
            pltpu.VMEM((total, 2 * hidden), bf16),
            pltpu.VMEM((total, hidden), bf16),
            pltpu.VMEM((total, width), bf16),
            pltpu.VMEM((total, width), bf16),
            pltpu.VMEM(probs_sent.shape, f32),
            pltpu.SemaphoreType.DMA((5, n)),
            pltpu.SemaphoreType.DMA((5, n)),
        ],
        compiler_params=pltpu.CompilerParams(
            collective_id=3, has_side_effects=True, vmem_limit_bytes=48 * 1024 * 1024
        ),
        cost_estimate=pl.CostEstimate(
            flops=6 * 2 * total * width * hidden * 3, bytes_accessed=100 << 20, transcendentals=0
        ),
        name="expert_of_place",
    )(rows_sent, probs_sent, grad_rows, expert_w)


def rope_tables(places):
    frequencies = jnp.exp(
        jnp.arange(HEAD_SIZE // 2, dtype=jnp.float32) * (-2.0 * math.log(rope_base) / HEAD_SIZE)
    )
    angles = places.astype(jnp.float32)[:, None] * frequencies[None, :]
    return (jnp.cos(angles)[:, None, :], jnp.sin(angles)[:, None, :])


def turn(values, cosine_table, sine_table):
    row_count = values.shape[0]
    head_view = values.reshape(row_count, -1, HEAD_SIZE)
    first_half = head_view[..., : HEAD_SIZE // 2]
    second_half = head_view[..., HEAD_SIZE // 2 :]
    turned = jnp.concatenate(
        [
            first_half * cosine_table - second_half * sine_table,
            second_half * cosine_table + first_half * sine_table,
        ],
        axis=-1,
    )
    return turned.reshape(row_count, -1)


def contract_rows(left, right, precision=None):
    return lax.dot_general(
        left, right, (((0,), (0,)), ((), ())), precision=precision, preferred_element_type=f32
    )


def contract_cols(left, right, precision=None):
    return lax.dot_general(
        left, right, (((1,), (1,)), ((), ())), precision=precision, preferred_element_type=f32
    )


def mm(left, right):
    return jnp.dot(left, right, preferred_element_type=f32)


def local(
    sizes,
    inputs,
    cotangent,
    lengths,
    expert_ids,
    attn_gain,
    w_query,
    key_weight,
    value_weight,
    w_output,
    ffn_gain,
    w_router,
    w_gate,
    w_up,
    w_down,
):
    rows, width = inputs.shape
    n_fsdp, n_ctx, n_tp = sizes["fsdp"], sizes["ctx"], sizes["tp"]
    experts = w_router.shape[1]
    depth, _, ff = w_gate.shape
    per_ctx = experts // n_ctx
    send = functools.partial(exchange, sizes)
    ctx_at, tp_at = lax.axis_index("ctx"), lax.axis_index("tp")

    chosen = jnp.any(
        expert_ids[:, :, None] == jnp.arange(experts, dtype=jnp.int32)[None, None, :], axis=1
    )
    ctx_order = lax.rem(ctx_at + jnp.arange(n_ctx, dtype=jnp.int32), n_ctx)
    mine = ctx_order * per_ctx + tp_at
    chosen_mine = jnp.any(expert_ids[None, :, :] == mine[:, None, None], axis=2)
    earlier = jnp.arange(rows)[:, None] < jnp.arange(rows)[None, :]
    rank = mm(chosen_mine.astype(bf16), earlier.astype(bf16))
    slots = jnp.arange(CAP, dtype=f32)
    picks = (chosen_mine[:, None, :] & (rank[:, None, :] == slots[None, :, None])).astype(bf16)
    picks_flat = picks.reshape(n_ctx * CAP, rows)

    def shifted(chunks, axis, direction):
        n = chunks.shape[0]
        return jnp.stack(
            [chunks[0]]
            + [
                lax.ppermute(chunks[k], axis, [(s, (s + direction * k) % n) for s in range(n)])
                for k in range(1, n)
            ]
        )

    first = ctx_at * per_ctx
    tp_order = lax.rem(tp_at + jnp.arange(n_tp, dtype=jnp.int32), n_tp)
    own_slices = jnp.stack(
        [
            lax.dynamic_slice_in_dim(w, first, per_ctx, 1).transpose(1, 0, 2)
            for w in (w_gate, w_up, w_down)
        ],
        axis=1,
    )
    gains = jnp.concatenate(
        [
            attn_gain.reshape(-1, 128),
            ffn_gain.reshape(-1, 128),
            jnp.zeros((16 - 2 * depth // 128, 128), bf16),
        ],
        axis=0,
    )
    router_pad = jnp.pad(w_router, ((0, 0), (0, 128 - experts)))
    grads_sent = mm(picks_flat, cotangent).astype(bf16).reshape(n_ctx, CAP, width)
    query_w, key_w, value_w, output_w, gains_all, router_all, expert_slices, grad_rows = send(
        0,
        (("fsdp",), "g", w_query),
        (("fsdp",), "g", key_weight),
        (("fsdp",), "g", value_weight),
        (("fsdp",), "g", w_output),
        (("fsdp",), "g", gains),
        (("fsdp",), "g", router_pad),
        (("tp",), "a", own_slices),
        (("ctx",), "f", grads_sent),
    )
    query_w = query_w.reshape(width, -1)
    key_w = key_w.reshape(width, -1)
    value_w = value_w.reshape(width, -1)
    output_w = output_w.reshape(width, -1)
    lines = depth // 128
    gain_one = gains_all[:, :lines].reshape(width).astype(f32)
    gain_two = gains_all[:, lines : 2 * lines].reshape(width).astype(f32)
    router_w = router_all.reshape(width, 128)[:, :experts]

    grad_rows = grad_rows.reshape(n_ctx * CAP, width)

    output_full = lax.all_gather(output_w, "tp", axis=1, tiled=True)
    expert_cat = expert_slices.transpose(2, 1, 0, 3).reshape(depth, 3 * n_tp * ff)
    expert_w = lax.all_gather(expert_cat, "fsdp", axis=0, tiled=True)

    lengths_row = lengths[0]
    query_rows = ctx_at * rows + jnp.arange(rows, dtype=jnp.int32)
    seq_ends = jnp.cumsum(lengths_row)
    passed = (query_rows[:, None] >= seq_ends[None, :]).astype(jnp.int32)
    starts = jnp.sum(passed * lengths_row[None, :], axis=1)
    cosine_table, sine_table = rope_tables(query_rows - starts)
    hidden_in = inputs.astype(f32)
    scale_one = lax.rsqrt(jnp.mean(hidden_in * hidden_in, axis=-1, keepdims=True) + norm_eps)
    normed_one = (hidden_in * scale_one * gain_one).astype(bf16)
    queries = turn(mm(normed_one, query_w), cosine_table, sine_table).astype(bf16)
    keys_local = turn(mm(normed_one, key_w), cosine_table, sine_table).astype(bf16)
    values_local = mm(normed_one, value_w).astype(bf16)
    pairs_local = jnp.concatenate([keys_local, values_local], axis=1)
    pair_width = keys_local.shape[1]
    (pairs_all,) = send(1, (("ctx",), "g", pairs_local))
    total_rows = n_ctx * rows
    pairs_all = pairs_all.reshape(total_rows, 2 * pair_width)
    key_heads = pair_width // HEAD_SIZE
    groups = queries.shape[1] // pair_width
    keys_all = pairs_all[:, :pair_width].reshape(total_rows, key_heads, HEAD_SIZE)
    values_all = pairs_all[:, pair_width:].reshape(total_rows, key_heads, HEAD_SIZE)
    query_head_rows = queries.reshape(rows, key_heads, groups, HEAD_SIZE)
    key_rows = jnp.arange(total_rows, dtype=jnp.int32)
    allowed = (key_rows[None, :] >= starts[:, None]) & (key_rows[None, :] <= query_rows[:, None])

    def masked_scores():
        raw_scores = jnp.einsum(
            "rkgd,skd->kgrs", query_head_rows, keys_all, preferred_element_type=f32
        )
        return jnp.where(allowed, raw_scores * HEAD_SIZE ** (-0.5), -1e30)

    masked = masked_scores()
    row_top = jnp.max(masked, axis=-1, keepdims=True)
    shifted_exp = jnp.exp(masked - row_top)
    row_total = jnp.sum(shifted_exp, axis=-1, keepdims=True)
    attn_probs = shifted_exp / row_total
    log_total = row_top + jnp.log(row_total)
    attended = jnp.einsum(
        "kgrs,skd->rkgd", attn_probs.astype(bf16), values_all, preferred_element_type=f32
    )
    attended = attended.reshape(rows, -1).astype(bf16)
    (attended_all,) = send(2, (("tp",), "g", attended))
    attended_all = attended_all.transpose(1, 0, 2).reshape(rows, -1)
    residual = hidden_in + branch_scale * contract_cols(attended_all, output_full)

    scale_two = lax.rsqrt(jnp.mean(residual * residual, axis=-1, keepdims=True) + norm_eps)
    normed_two = (residual * scale_two * gain_two).astype(bf16)
    logits = mm(normed_two, router_w)
    route_masked = jnp.where(chosen, logits, -1e30)
    route_exp = jnp.exp(route_masked - jnp.max(route_masked, axis=-1, keepdims=True))
    gate_probs = route_exp / jnp.sum(route_exp, axis=-1, keepdims=True)
    probs_mine = lax.dynamic_index_in_dim(
        gate_probs.T.reshape(n_ctx, per_ctx, rows), tp_at, 1, keepdims=False
    )
    probs_mine = jnp.take(probs_mine, ctx_order, axis=0)
    probs_sent = jnp.sum(picks.astype(f32) * probs_mine[:, None, :], axis=2)
    rows_sent = mm(picks_flat, normed_two).astype(bf16)
    probs_sent = jnp.broadcast_to(probs_sent[:, None, :], (n_ctx, 8, CAP))
    norm_grad_got, mixed_got, gate_grad_got, expert_grad = expert_of_place(
        sizes, rows_sent, probs_sent, grad_rows, expert_w
    )
    expert_grad = lax.psum_scatter(expert_grad, "fsdp", scatter_dimension=0, tiled=True)

    quarter = rows // n_tp
    norm_grad_part = contract_rows(picks_flat, norm_grad_got)
    gate_grad_part = jnp.sum(picks.astype(f32) * gate_grad_got[:, 0, :, None], axis=1)
    norm_grad_parts, gate_grad_parts = send(
        5,
        (("tp",), "a", norm_grad_part.astype(bf16).reshape(n_tp, quarter, width)),
        (("tp",), "g", gate_grad_part),
    )

    def quarter_of(array):
        return lax.dynamic_slice_in_dim(array, tp_at * quarter, quarter, 0)

    back_order = lax.rem(jnp.arange(n_ctx, dtype=jnp.int32) + n_ctx - ctx_at, n_ctx)
    gate_grads = jnp.take(gate_grad_parts, back_order, axis=1)
    gate_grads = gate_grads.transpose(2, 1, 0).reshape(rows, experts)
    route_grad = gate_probs * (
        gate_grads - jnp.sum(gate_probs * gate_grads, axis=-1, keepdims=True)
    )
    grad_router = contract_rows(normed_two.astype(f32), route_grad, highest)
    router_back = contract_cols(quarter_of(route_grad), router_w.astype(f32), highest)
    normed_grad = jnp.sum(norm_grad_parts.astype(f32), axis=0) + router_back
    weighted_two = normed_grad * gain_two
    residual_own, scale_two_own = quarter_of(residual), quarter_of(scale_two)
    grad_ffn_part = jnp.sum(normed_grad * residual_own * scale_two_own, axis=0)
    residual_grad = (
        quarter_of(cotangent).astype(f32)
        + scale_two_own * weighted_two
        - residual_own
        * scale_two_own**3
        * jnp.mean(weighted_two * residual_own, axis=-1, keepdims=True)
    )
    (attn_in,) = send(6, (("tp",), "g", (branch_scale * residual_grad).astype(bf16)))
    attn_in = attn_in.reshape(rows, width)

    expert_grad, _ = lax.optimization_barrier((expert_grad, attn_in))
    expert_grad = expert_grad.reshape(depth, 3, n_tp, ff).transpose(2, 1, 0, 3)
    pieces = shifted(jnp.take(expert_grad, tp_order, axis=0), "tp", 1)
    expert_all = lax.all_gather(pieces, "ctx", axis=0, tiled=True)

    grad_output = contract_rows(attn_in, attended)
    attended_grad = mm(attn_in, output_w).astype(bf16)

    grad_heads = attended_grad.reshape(rows, key_heads, groups, HEAD_SIZE)
    attn_probs = jnp.exp(masked_scores() - log_total)
    value_grad_all = jnp.einsum(
        "kgrs,rkgd->skd", attn_probs.astype(bf16), grad_heads, preferred_element_type=f32
    )
    prob_grad = jnp.einsum("rkgd,skd->kgrs", grad_heads, values_all, preferred_element_type=f32)
    score_grad = (
        attn_probs * (prob_grad - jnp.sum(attn_probs * prob_grad, axis=-1, keepdims=True))
    ).astype(bf16)
    query_grad_rot = jnp.einsum(
        "kgrs,skd->rkgd", score_grad, keys_all, preferred_element_type=f32
    ).reshape(rows, -1) * HEAD_SIZE ** (-0.5)
    key_grad_all = jnp.einsum(
        "kgrs,rkgd->skd", score_grad, query_head_rows, preferred_element_type=f32
    ) * HEAD_SIZE ** (-0.5)
    pair_grads = jnp.concatenate(
        [
            key_grad_all.reshape(total_rows, pair_width),
            value_grad_all.reshape(total_rows, pair_width),
        ],
        axis=1,
    ).astype(bf16)
    (pair_got,) = send(7, (("ctx",), "a", pair_grads.reshape(n_ctx, rows, 2 * pair_width)))
    pair_owned = jnp.sum(pair_got.astype(f32), axis=0)
    query_grad = turn(query_grad_rot, cosine_table, -sine_table).astype(bf16)
    key_grad = turn(pair_owned[:, :pair_width], cosine_table, -sine_table).astype(bf16)
    value_grad = pair_owned[:, pair_width:].astype(bf16)
    normed_one_part = (
        contract_cols(query_grad, query_w)
        + contract_cols(key_grad, key_w)
        + contract_cols(value_grad, value_w)
    )
    grad_gain_part = jnp.sum(normed_one_part * hidden_in * scale_one, axis=0)
    grad_query = contract_rows(normed_one, query_grad)
    grad_key = contract_rows(normed_one, key_grad)
    grad_value = contract_rows(normed_one, value_grad)
    mixed_part = contract_rows(picks_flat, mixed_got).astype(bf16)

    n_rows = n_fsdp * n_ctx
    share = width // n_rows
    side = jnp.pad(grad_router, ((0, 0), (0, 128 - experts)))
    small = jnp.concatenate([grad_query, grad_key, grad_value, grad_output, side], axis=1)
    small = small.astype(bf16).reshape(n_rows, share, -1)
    gain_parts = jnp.stack([grad_gain_part, grad_ffn_part]).reshape(2, n_rows, share)
    gain_chunks = jnp.pad(gain_parts.transpose(1, 0, 2), ((0, 0), (0, 6), (0, 128 - share)))
    one_parts, mixed_parts, small_got, gain_got = send(
        8,
        (("tp",), "a", normed_one_part.astype(bf16).reshape(n_tp, quarter, width)),
        (("tp",), "a", mixed_part.reshape(n_tp, quarter, width)),
        (("fsdp", "ctx"), "a", small),
        (("fsdp", "ctx"), "a", gain_chunks),
    )
    small_sum = jnp.sum(small_got.astype(f32), axis=0).astype(bf16)
    gain_sum = jnp.sum(gain_got, axis=0)
    output = residual_own + branch_scale * jnp.sum(mixed_parts.astype(f32), axis=0)
    normed_one_grad = jnp.sum(one_parts.astype(f32), axis=0)
    weighted_one = normed_one_grad * gain_one
    hidden_own, scale_one_own = quarter_of(hidden_in), quarter_of(scale_one)
    input_grad = (
        residual_grad
        + scale_one_own * weighted_one
        - hidden_own
        * scale_one_own**3
        * jnp.mean(weighted_one * hidden_own, axis=-1, keepdims=True)
    )
    small_all, gain_all, output, input_grad = send(
        9,
        (("ctx",), "g", small_sum),
        (("ctx", "tp"), "g", gain_sum),
        (("tp",), "g", output.astype(bf16)),
        (("tp",), "g", input_grad.astype(bf16)),
    )
    small_all = small_all.reshape(depth, -1).astype(f32)
    gain_all = jnp.sum(gain_all[:, :2, :share].reshape(n_ctx, n_tp, 2, share), axis=1)
    gain_all = gain_all.transpose(1, 0, 2).reshape(2, depth)
    grad_gate, grad_up, grad_down = spread(expert_all, n_ctx, n_tp)
    q_end = queries.shape[1]
    k_end, v_end = q_end + pair_width, q_end + 2 * pair_width
    o_end = v_end + attended.shape[1]
    return (
        output.reshape(rows, width),
        input_grad.reshape(rows, width),
        gain_all[0],
        small_all[:, :q_end],
        small_all[:, q_end:k_end],
        small_all[:, k_end:v_end],
        small_all[:, v_end:o_end],
        gain_all[1],
        small_all[:, o_end : o_end + experts],
        grad_gate,
        grad_up,
        grad_down,
    )


def solution(mesh):
    sizes = dict(mesh.shape)
    return jax.shard_map(
        functools.partial(local, sizes),
        mesh=mesh,
        in_specs=(
            P(("fsdp", "ctx"), None),
            P(("fsdp", "ctx"), None),
            P("fsdp", None),
            P(("fsdp", "ctx"), None),
            P("fsdp"),
            P("fsdp", "tp"),
            P("fsdp", "tp"),
            P("fsdp", "tp"),
            P("fsdp", "tp"),
            P("fsdp"),
            P("fsdp", None),
            P("fsdp", None, "tp"),
            P("fsdp", None, "tp"),
            P("fsdp", None, "tp"),
        ),
        out_specs=(
            P(("fsdp", "ctx"), None),
            P(("fsdp", "ctx"), None),
            P("fsdp"),
            P("fsdp", "tp"),
            P("fsdp", "tp"),
            P("fsdp", "tp"),
            P("fsdp", "tp"),
            P("fsdp"),
            P("fsdp", None),
            P("fsdp", None, "tp"),
            P("fsdp", None, "tp"),
            P("fsdp", None, "tp"),
        ),
        check_vma=False,
    )
```

```python
import functools
import math

import jax
import jax.numpy as jnp
from jax import lax
from jax.experimental import pallas as pl
from jax.experimental.pallas import tpu as pltpu
from jax.sharding import PartitionSpec as P

HEAD_SIZE = 64
CAP = 128
MESH = pl.DeviceIdType.MESH

norm_eps = 1e-06
rope_base = 10000.0
branch_scale = 0.22
highest = lax.Precision.HIGHEST
bf16 = jnp.bfloat16
f32 = jnp.float32


def exchange_kernel(plan, sizes, *refs):
    count = len(plan)
    ins, outs = refs[:count], refs[count : 2 * count]
    send_sem, recv_sem, self_sem = refs[2 * count :]

    def place(axes, step):
        offsets = []
        for axis in reversed(axes):
            offsets.append(step % sizes[axis])
            step //= sizes[axis]
        coords = {}
        for axis, offset in zip(axes, offsets[::-1]):
            here = lax.axis_index(axis)
            coords[axis] = lax.rem(here + offset, sizes[axis]) if offset else here
        return coords

    def flat(axes, coords):
        index = 0
        for axis in axes:
            index = index * sizes[axis] + coords[axis]
        return index

    groups = {}
    for axes, _ in plan:
        for step in range(1, math.prod(sizes[a] for a in axes)):
            full, rest = {}, step
            for axis in reversed(axes):
                full[axis] = rest % sizes[axis]
                rest //= sizes[axis]
            key = tuple(sorted((a, o) for a, o in full.items() if o))
            groups[key] = (axes, step)
    barrier = pltpu.get_barrier_semaphore()
    for axes, step in groups.values():
        pl.semaphore_signal(barrier, inc=1, device_id=place(axes, step), device_id_type=MESH)
    pl.semaphore_wait(barrier, len(groups))

    copies = []
    for at, (axes, mode) in enumerate(plan):
        mine = flat(axes, place(axes, 0))
        for step in range(1, math.prod(sizes[a] for a in axes)):
            if mode in "fb":
                peer = place(axes, step if mode == "f" else sizes[axes[0]] - step)
                source, slot = ins[at].at[step], step
            else:
                peer = place(axes, step)
                source = ins[at] if mode == "g" else ins[at].at[flat(axes, peer)]
                slot = mine
            copy = pltpu.make_async_remote_copy(
                src_ref=source,
                dst_ref=outs[at].at[slot],
                send_sem=send_sem.at[at, step],
                recv_sem=recv_sem.at[at, step],
                device_id=peer,
                device_id_type=MESH,
            )
            copy.start()
            copies.append(copy)
        if mode in "fb":
            mine = 0
        own = pltpu.make_async_copy(
            ins[at] if mode == "g" else ins[at].at[mine], outs[at].at[mine], self_sem.at[at]
        )
        own.start()
        copies.append(own)
    for copy in copies:
        copy.wait()


def exchange(sizes, collective_id, *items):
    plan = [(axes, mode) for axes, mode, _ in items]
    arrays = [array for _, _, array in items]
    outs = []
    most = 1
    for axes, mode, array in items:
        n = math.prod(sizes[a] for a in axes)
        most = max(most, n)
        shape = (n,) + array.shape if mode == "g" else array.shape
        outs.append(jax.ShapeDtypeStruct(shape, array.dtype))
    count = len(items)
    moved = sum(math.prod(o.shape) * o.dtype.itemsize for o in outs)
    return pl.pallas_call(
        functools.partial(exchange_kernel, plan, sizes),
        out_shape=outs,
        in_specs=[pl.BlockSpec(memory_space=pl.ANY)] * count,
        out_specs=[pl.BlockSpec(memory_space=pl.ANY)] * count,
        scratch_shapes=[
            pltpu.SemaphoreType.DMA((count, most)),
            pltpu.SemaphoreType.DMA((count, most)),
            pltpu.SemaphoreType.DMA((count,)),
        ],
        compiler_params=pltpu.CompilerParams(collective_id=collective_id, has_side_effects=True),
        cost_estimate=pl.CostEstimate(flops=0, bytes_accessed=20 * moved, transcendentals=0),
        name="exchange_%d" % collective_id,
    )(*arrays)


def spread_kernel(pieces_ref, *out_refs):
    experts = pieces_ref.shape[0]
    depth = pieces_ref.shape[2]
    for which, out_ref in enumerate(out_refs):
        for expert in range(experts):
            out_ref[pl.ds(expert, depth, stride=experts), :] = pieces_ref[expert, which].astype(f32)


def spread(pieces):
    experts, count, depth, ff = pieces.shape
    block = 64
    outs = pl.pallas_call(
        spread_kernel,
        grid=(depth // block,),
        out_shape=[jax.ShapeDtypeStruct((depth * experts, ff), f32)] * count,
        in_specs=[pl.BlockSpec((experts, count, block, ff), lambda i: (0, 0, i, 0))],
        out_specs=[pl.BlockSpec((block * experts, ff), lambda i: (i, 0))] * count,
        compiler_params=pltpu.CompilerParams(vmem_limit_bytes=32 * 1024 * 1024),
        name="spread",
    )(pieces)
    return [out.reshape(depth, experts, ff) for out in outs]


def expert_kernel(
    n,
    part,
    rows_ref,
    probs_ref,
    grads_ref,
    w_ref,
    norm_got,
    mixed_got,
    gate_got,
    wgrad_ref,
    norm_buf,
    probs_buf,
    both_buf,
    weighted_buf,
    back_buf,
    mixed_buf,
    gate_buf,
    send_sems,
    recv_sems,
):
    me = lax.axis_index("ctx")
    hidden = w_ref.shape[1] // 3

    def chunk(ref, k):
        return ref.at[pl.ds(pl.multiple_of(k * CAP, CAP), CAP)]

    def copy(which, k, source, target, place):
        return pltpu.make_async_remote_copy(
            src_ref=source,
            dst_ref=target,
            send_sem=send_sems.at[which, k],
            recv_sem=recv_sems.at[which, k],
            device_id={"ctx": lax.rem(place, n)},
            device_id_type=MESH,
        )

    def out_copies(k):
        return (
            copy(0, k, chunk(rows_ref, k), chunk(norm_buf, k), me + k),
            copy(1, k, probs_ref.at[k], probs_buf.at[k], me + k),
        )

    def back_copies(k):
        place = me + n - k
        return (
            copy(2, k, chunk(back_buf, k), chunk(norm_got, k), place),
            copy(3, k, gate_buf.at[k], gate_got.at[k], place),
            copy(4, k, chunk(mixed_buf, k), chunk(mixed_got, k), place),
        )

    barrier = pltpu.get_barrier_semaphore()
    for k in range(1, n):
        pl.semaphore_signal(
            barrier, inc=1, device_id={"ctx": lax.rem(me + k, n)}, device_id_type=MESH
        )
    pl.semaphore_wait(barrier, n - 1)
    for k in range(1, 4):
        for item in out_copies(k):
            item.start()
    norm_buf[:CAP] = rows_ref[:CAP]
    probs_buf[0] = probs_ref[0]
    same = lax.broadcasted_iota(jnp.int32, (CAP, CAP), 0) == lax.broadcasted_iota(
        jnp.int32, (CAP, CAP), 1
    )

    def pair(j, carry):
        @pl.when(j < n // 2 - 2)
        def _():
            for k in (2 * j + 4, 2 * j + 5):
                for item in out_copies(k):
                    item.start()

        for k in (2 * j, 2 * j + 1):

            @pl.when(k > 0)
            def _():
                for item in out_copies(k):
                    item.wait_recv()

        here = pl.ds(pl.multiple_of(j * 2 * CAP, 2 * CAP), 2 * CAP)
        gate_up = mm(norm_buf[here, :], w_ref[:, : 2 * hidden])
        down_back = mm(grads_ref[here, :], w_ref[:, 2 * hidden :])
        probs = jnp.concatenate(
            [
                jnp.sum(jnp.where(same, probs_buf[k][:1, :], 0.0), axis=1, keepdims=True)
                for k in (2 * j, 2 * j + 1)
            ],
            axis=0,
        )
        gate_pre, up_pre = gate_up[:, :hidden], gate_up[:, hidden:]
        sig = jax.nn.sigmoid(gate_pre)
        silu = gate_pre * sig
        activation = silu * up_pre
        gate_grad = branch_scale * jnp.sum(activation * down_back, axis=1, keepdims=True)
        act_grad = (branch_scale * probs) * down_back
        both_buf[here, :hidden] = (
            act_grad * up_pre * sig * (1.0 + gate_pre * (1.0 - sig))
        ).astype(bf16)
        both_buf[here, hidden:] = (act_grad * silu).astype(bf16)
        weighted_buf[here, :] = (probs * activation).astype(bf16)
        back_buf[here, :] = contract_cols(both_buf[here, :], w_ref[:, : 2 * hidden]).astype(bf16)
        for i in range(2):
            line = jnp.sum(
                jnp.where(same, gate_grad[i * CAP : (i + 1) * CAP], 0.0), axis=0, keepdims=True
            )
            gate_buf[2 * j + i] = jnp.broadcast_to(line, (8, CAP))
        mixed_buf[here, :] = contract_cols(weighted_buf[here, :], w_ref[:, 2 * hidden :]).astype(
            bf16
        )
        for k in (2 * j, 2 * j + 1):

            @pl.when(k > 0)
            def _():
                for item in back_copies(k):
                    item.start()

        return carry

    lax.fori_loop(0, n // 2, pair, 0)
    norm_got[:CAP] = back_buf[:CAP]
    mixed_got[:CAP] = mixed_buf[:CAP]
    gate_got[0] = gate_buf[0]

    width, slim = w_ref.shape[0], wgrad_ref.shape[1]

    def weight_grads(j, carry):
        here = pl.ds(pl.multiple_of(j * part, part), part)
        gate_up = contract_rows(norm_buf[:, here], both_buf[...]).astype(bf16)
        down = (contract_rows(grads_ref[:, here], weighted_buf[...]) * branch_scale).astype(bf16)
        for piece in range(hidden // slim):
            for which in range(3):
                row = (j * (hidden // slim) + piece) * 3 + which
                at = pl.ds(pl.multiple_of(row * part, part), part)
                if which < 2:
                    start = which * hidden + piece * slim
                    wgrad_ref[at, :] = gate_up[:, start : start + slim]
                else:
                    wgrad_ref[at, :] = down[:, piece * slim : (piece + 1) * slim]
        return carry

    lax.fori_loop(0, width // part, weight_grads, 0)
    for k in range(1, n):
        for item in out_copies(k):
            item.wait_send()
        for item in back_copies(k):
            item.wait()


def expert_of_place(sizes, rows_sent, probs_sent, grad_rows, expert_w):
    n = sizes["ctx"]
    total, width = rows_sent.shape
    columns = expert_w.shape[1]
    hidden = columns // 3
    like = jax.ShapeDtypeStruct
    vmem = pl.BlockSpec(memory_space=pltpu.VMEM)
    return pl.pallas_call(
        functools.partial(expert_kernel, n, width // sizes["fsdp"]),
        out_shape=[
            like((total, width), bf16),
            like((total, width), bf16),
            like(probs_sent.shape, f32),
            like((width * sizes["tp"] * 3, hidden // sizes["tp"]), bf16),
        ],
        in_specs=[vmem] * 4,
        out_specs=[vmem] * 4,
        scratch_shapes=[
            pltpu.VMEM((total, width), bf16),
            pltpu.VMEM(probs_sent.shape, f32),
            pltpu.VMEM((total, 2 * hidden), bf16),
            pltpu.VMEM((total, hidden), bf16),
            pltpu.VMEM((total, width), bf16),
            pltpu.VMEM((total, width), bf16),
            pltpu.VMEM(probs_sent.shape, f32),
            pltpu.SemaphoreType.DMA((5, n)),
            pltpu.SemaphoreType.DMA((5, n)),
        ],
        compiler_params=pltpu.CompilerParams(
            collective_id=3, has_side_effects=True, vmem_limit_bytes=48 * 1024 * 1024
        ),
        cost_estimate=pl.CostEstimate(
            flops=6 * 2 * total * width * hidden * 3, bytes_accessed=100 << 20, transcendentals=0
        ),
        name="expert_of_place",
    )(rows_sent, probs_sent, grad_rows, expert_w)


def rope_tables(places, columns):
    column = jnp.arange(columns, dtype=jnp.int32)
    steps = (column % (HEAD_SIZE // 2)).astype(f32)
    frequencies = jnp.exp(steps * (-2.0 * math.log(rope_base) / HEAD_SIZE))
    angles = places.astype(f32)[:, None] * frequencies[None, :]
    first = (column % HEAD_SIZE < HEAD_SIZE // 2)[None, :]
    sine = jnp.sin(angles)
    return jnp.cos(angles), jnp.where(first, -sine, sine), first


def turn(values, cosine, sine, first):
    half = HEAD_SIZE // 2
    other = jnp.where(first, jnp.roll(values, -half, axis=1), jnp.roll(values, half, axis=1))
    return values * cosine + other * sine


def contract_rows(left, right, precision=None):
    return lax.dot_general(
        left, right, (((0,), (0,)), ((), ())), precision=precision, preferred_element_type=f32
    )


def contract_cols(left, right, precision=None):
    return lax.dot_general(
        left, right, (((1,), (1,)), ((), ())), precision=precision, preferred_element_type=f32
    )


def mm(left, right):
    return jnp.dot(left, right, preferred_element_type=f32)


def local(
    sizes,
    inputs,
    cotangent,
    lengths,
    expert_ids,
    attn_gain,
    w_query,
    key_weight,
    value_weight,
    w_output,
    ffn_gain,
    w_router,
    w_gate,
    w_up,
    w_down,
):
    rows, width = inputs.shape
    n_fsdp, n_ctx, n_tp = sizes["fsdp"], sizes["ctx"], sizes["tp"]
    experts = w_router.shape[1]
    depth, _, ff = w_gate.shape
    per_ctx = experts // n_ctx
    send = functools.partial(exchange, sizes)
    ctx_at, tp_at = lax.axis_index("ctx"), lax.axis_index("tp")

    chosen = jnp.any(
        expert_ids[:, :, None] == jnp.arange(experts, dtype=jnp.int32)[None, None, :], axis=1
    )
    ctx_order = lax.rem(ctx_at + jnp.arange(n_ctx, dtype=jnp.int32), n_ctx)
    mine = ctx_order * per_ctx + tp_at
    chosen_mine = jnp.any(expert_ids[None, :, :] == mine[:, None, None], axis=2)
    earlier = jnp.arange(rows)[:, None] < jnp.arange(rows)[None, :]
    rank = mm(chosen_mine.astype(bf16), earlier.astype(bf16))
    slots = jnp.arange(CAP, dtype=f32)
    picks = (chosen_mine[:, None, :] & (rank[:, None, :] == slots[None, :, None])).astype(bf16)
    picks_flat = picks.reshape(n_ctx * CAP, rows)

    first = ctx_at * per_ctx
    own_slices = jnp.stack(
        [
            lax.dynamic_slice_in_dim(w, first, per_ctx, 1).transpose(1, 0, 2)
            for w in (w_gate, w_up, w_down)
        ],
        axis=1,
    )
    gains = jnp.concatenate(
        [
            attn_gain.reshape(-1, 128),
            ffn_gain.reshape(-1, 128),
            jnp.zeros((16 - 2 * depth // 128, 128), bf16),
        ],
        axis=0,
    )
    router_pad = jnp.pad(w_router, ((0, 0), (0, 128 - experts)))
    grads_sent = mm(picks_flat, cotangent).astype(bf16).reshape(n_ctx, CAP, width)
    qkv_w, output_w, gains_all, router_all, expert_slices, grad_rows = send(
        0,
        (("fsdp",), "g", jnp.concatenate([w_query, key_weight, value_weight], axis=1)),
        (("fsdp",), "g", w_output),
        (("fsdp",), "g", gains),
        (("fsdp",), "g", router_pad),
        (("tp",), "a", own_slices),
        (("ctx",), "f", grads_sent),
    )
    qkv_w = qkv_w.reshape(width, -1)
    output_w = output_w.reshape(width, -1)
    lines = depth // 128
    gain_one = gains_all[:, :lines].reshape(width).astype(f32)
    gain_two = gains_all[:, lines : 2 * lines].reshape(width).astype(f32)
    router_w = router_all.reshape(width, 128)[:, :experts]

    grad_rows = grad_rows.reshape(n_ctx * CAP, width)

    expert_cat = expert_slices.transpose(2, 1, 0, 3).reshape(depth, 3 * n_tp * ff)
    expert_w = lax.all_gather(expert_cat, "fsdp", axis=0, tiled=True)

    lengths_row = lengths[0]
    query_rows = ctx_at * rows + jnp.arange(rows, dtype=jnp.int32)
    seq_ends = jnp.cumsum(lengths_row)
    passed = (query_rows[:, None] >= seq_ends[None, :]).astype(jnp.int32)
    starts = jnp.sum(passed * lengths_row[None, :], axis=1)
    q_end, pair_width = w_query.shape[1], key_weight.shape[1]
    turned = q_end + pair_width
    cosine, sine, first_half = rope_tables(query_rows - starts, turned)
    hidden_in = inputs.astype(f32)
    scale_one = lax.rsqrt(jnp.mean(hidden_in * hidden_in, axis=-1, keepdims=True) + norm_eps)
    normed_one = (hidden_in * scale_one * gain_one).astype(bf16)
    qkv = mm(normed_one, qkv_w)
    queries_keys = turn(qkv[:, :turned], cosine, sine, first_half).astype(bf16)
    queries = queries_keys[:, :q_end]
    pairs_local = jnp.concatenate(
        [queries_keys[:, q_end:], qkv[:, turned:].astype(bf16)], axis=1
    )
    pairs_all, output_all = send(
        1, (("ctx",), "g", pairs_local), (("tp",), "g", output_w)
    )
    total_rows = n_ctx * rows
    pairs_all = pairs_all.reshape(total_rows, 2 * pair_width)
    key_heads = pair_width // HEAD_SIZE
    groups = queries.shape[1] // pair_width
    keys_all = pairs_all[:, :pair_width].reshape(total_rows, key_heads, HEAD_SIZE)
    values_all = pairs_all[:, pair_width:].reshape(total_rows, key_heads, HEAD_SIZE)
    query_head_rows = queries.reshape(rows, key_heads, groups, HEAD_SIZE)
    key_rows = jnp.arange(total_rows, dtype=jnp.int32)
    allowed = (key_rows[None, :] >= starts[:, None]) & (key_rows[None, :] <= query_rows[:, None])

    def masked_scores():
        raw_scores = jnp.einsum(
            "rkgd,skd->kgrs", query_head_rows, keys_all, preferred_element_type=f32
        )
        return jnp.where(allowed, raw_scores * HEAD_SIZE ** (-0.5), -1e30)

    masked = masked_scores()
    row_top = jnp.max(masked, axis=-1, keepdims=True)
    shifted_exp = jnp.exp(masked - row_top)
    row_total = jnp.sum(shifted_exp, axis=-1, keepdims=True)
    attn_probs = shifted_exp / row_total
    log_total = row_top + jnp.log(row_total)
    attended = jnp.einsum(
        "kgrs,skd->rkgd", attn_probs.astype(bf16), values_all, preferred_element_type=f32
    )
    attended = attended.reshape(rows, -1).astype(bf16)
    (attended_all,) = send(2, (("tp",), "g", attended))
    attended_all = attended_all.transpose(1, 0, 2).reshape(rows, -1)
    output_full = output_all.transpose(1, 0, 2).reshape(width, -1)
    residual = hidden_in + branch_scale * contract_cols(attended_all, output_full)

    scale_two = lax.rsqrt(jnp.mean(residual * residual, axis=-1, keepdims=True) + norm_eps)
    normed_two = (residual * scale_two * gain_two).astype(bf16)
    logits = mm(normed_two, router_w)
    route_masked = jnp.where(chosen, logits, -1e30)
    route_exp = jnp.exp(route_masked - jnp.max(route_masked, axis=-1, keepdims=True))
    gate_probs = route_exp / jnp.sum(route_exp, axis=-1, keepdims=True)
    probs_mine = lax.dynamic_index_in_dim(
        gate_probs.T.reshape(n_ctx, per_ctx, rows), tp_at, 1, keepdims=False
    )
    probs_mine = jnp.take(probs_mine, ctx_order, axis=0)
    probs_sent = jnp.sum(picks.astype(f32) * probs_mine[:, None, :], axis=2)
    rows_sent = mm(picks_flat, normed_two).astype(bf16)
    probs_sent = jnp.broadcast_to(probs_sent[:, None, :], (n_ctx, 8, CAP))
    norm_grad_got, mixed_got, gate_grad_got, expert_grad = expert_of_place(
        sizes, rows_sent, probs_sent, grad_rows, expert_w
    )
    expert_grad = lax.psum_scatter(expert_grad, "fsdp", scatter_dimension=0, tiled=True)

    quarter = rows // n_tp
    norm_grad_part = contract_rows(picks_flat, norm_grad_got)
    gate_grad_part = jnp.sum(picks.astype(f32) * gate_grad_got[:, 0, :, None], axis=1)
    norm_grad_parts, gate_grad_parts = send(
        5,
        (("tp",), "a", norm_grad_part.astype(bf16).reshape(n_tp, quarter, width)),
        (("tp",), "g", gate_grad_part),
    )

    def quarter_of(array):
        return lax.dynamic_slice_in_dim(array, tp_at * quarter, quarter, 0)

    back_order = lax.rem(jnp.arange(n_ctx, dtype=jnp.int32) + n_ctx - ctx_at, n_ctx)
    gate_grads = jnp.take(gate_grad_parts, back_order, axis=1)
    gate_grads = gate_grads.transpose(2, 1, 0).reshape(rows, experts)
    route_grad = gate_probs * (
        gate_grads - jnp.sum(gate_probs * gate_grads, axis=-1, keepdims=True)
    )
    grad_router = contract_rows(normed_two.astype(f32), route_grad, highest)
    router_back = contract_cols(quarter_of(route_grad), router_w.astype(f32), highest)
    normed_grad = jnp.sum(norm_grad_parts.astype(f32), axis=0) + router_back
    weighted_two = normed_grad * gain_two
    residual_own, scale_two_own = quarter_of(residual), quarter_of(scale_two)
    grad_ffn_part = jnp.sum(normed_grad * residual_own * scale_two_own, axis=0)
    residual_grad = (
        quarter_of(cotangent).astype(f32)
        + scale_two_own * weighted_two
        - residual_own
        * scale_two_own**3
        * jnp.mean(weighted_two * residual_own, axis=-1, keepdims=True)
    )
    attn_in, pieces = send(
        6,
        (("tp",), "g", (branch_scale * residual_grad).astype(bf16)),
        (("tp",), "a", expert_grad.reshape(n_tp, 3, depth, ff)),
    )
    attn_in = attn_in.reshape(rows, width)

    expert_all = lax.all_gather(pieces, "ctx", axis=0, tiled=True)

    side = jnp.pad(grad_router, ((0, 0), (0, 128 - experts)))
    early = jnp.concatenate([contract_rows(attn_in, attended), side], axis=1).astype(bf16)
    mixed_part = contract_rows(picks_flat, mixed_got).astype(bf16)
    attended_grad = mm(attn_in, output_w).astype(bf16)

    grad_heads = attended_grad.reshape(rows, key_heads, groups, HEAD_SIZE)
    attn_probs = jnp.exp(masked_scores() - log_total)
    value_grad_all = jnp.einsum(
        "kgrs,rkgd->skd", attn_probs.astype(bf16), grad_heads, preferred_element_type=f32
    )
    prob_grad = jnp.einsum("rkgd,skd->kgrs", grad_heads, values_all, preferred_element_type=f32)
    score_grad = (
        attn_probs * (prob_grad - jnp.sum(attn_probs * prob_grad, axis=-1, keepdims=True))
    ).astype(bf16)
    query_grad_rot = jnp.einsum(
        "kgrs,skd->rkgd", score_grad, keys_all, preferred_element_type=f32
    ).reshape(rows, -1) * HEAD_SIZE ** (-0.5)
    key_grad_all = jnp.einsum(
        "kgrs,rkgd->skd", score_grad, query_head_rows, preferred_element_type=f32
    ) * HEAD_SIZE ** (-0.5)
    pair_grads = jnp.concatenate(
        [
            key_grad_all.reshape(total_rows, pair_width),
            value_grad_all.reshape(total_rows, pair_width),
        ],
        axis=1,
    ).astype(bf16)
    pair_got, mixed_parts, early_got = send(
        7,
        (("ctx",), "a", pair_grads.reshape(n_ctx, rows, 2 * pair_width)),
        (("tp",), "a", mixed_part.reshape(n_tp, quarter, width)),
        (("fsdp",), "a", early.reshape(n_fsdp, depth, -1)),
    )
    pair_owned = jnp.sum(pair_got.astype(f32), axis=0)
    turned_back = turn(
        jnp.concatenate([query_grad_rot, pair_owned[:, :pair_width]], axis=1),
        cosine,
        -sine,
        first_half,
    )
    qkv_grad = jnp.concatenate([turned_back, pair_owned[:, pair_width:]], axis=1).astype(bf16)
    normed_one_part = contract_cols(qkv_grad, qkv_w)
    grad_gain_part = jnp.sum(normed_one_part * hidden_in * scale_one, axis=0)
    grad_qkv = contract_rows(normed_one, qkv_grad).astype(bf16)
    output = residual_own + branch_scale * jnp.sum(mixed_parts.astype(f32), axis=0)

    gain_parts = jnp.stack([grad_gain_part, grad_ffn_part]).reshape(2, n_fsdp, depth)
    gain_chunks = jnp.pad(gain_parts.transpose(1, 0, 2), ((0, 0), (0, 6), (0, 0)))
    one_parts, qkv_got, gain_got, output = send(
        8,
        (("tp",), "a", normed_one_part.astype(bf16).reshape(n_tp, quarter, width)),
        (("fsdp",), "a", grad_qkv.reshape(n_fsdp, depth, -1)),
        (("fsdp",), "a", gain_chunks),
        (("tp",), "g", output.astype(bf16)),
    )
    small = jnp.concatenate(
        [
            jnp.sum(qkv_got.astype(f32), axis=0).astype(bf16),
            jnp.sum(early_got.astype(f32), axis=0).astype(bf16),
        ],
        axis=1,
    )
    gain_sum = jnp.sum(gain_got, axis=0)
    normed_one_grad = jnp.sum(one_parts.astype(f32), axis=0)
    weighted_one = normed_one_grad * gain_one
    hidden_own, scale_one_own = quarter_of(hidden_in), quarter_of(scale_one)
    input_grad = (
        residual_grad
        + scale_one_own * weighted_one
        - hidden_own
        * scale_one_own**3
        * jnp.mean(weighted_one * hidden_own, axis=-1, keepdims=True)
    )
    small_got, gain_all, input_grad = send(
        9,
        (("ctx",), "a", small.reshape(n_ctx, depth // n_ctx, -1)),
        (("ctx", "tp"), "g", gain_sum),
        (("tp",), "g", input_grad.astype(bf16)),
    )
    (small_all,) = send(10, (("ctx",), "g", jnp.sum(small_got.astype(f32), axis=0).astype(bf16)))
    small_all = small_all.reshape(depth, -1).astype(f32)
    gain_all = jnp.sum(gain_all, axis=0)
    grad_gate, grad_up, grad_down = spread(expert_all)
    k_end, v_end = q_end + pair_width, q_end + 2 * pair_width
    o_end = v_end + attended.shape[1]
    return (
        output.reshape(rows, width),
        input_grad.reshape(rows, width),
        gain_all[0],
        small_all[:, :q_end],
        small_all[:, q_end:k_end],
        small_all[:, k_end:v_end],
        small_all[:, v_end:o_end],
        gain_all[1],
        small_all[:, o_end : o_end + experts],
        grad_gate,
        grad_up,
        grad_down,
    )


def solution(mesh):
    sizes = dict(mesh.shape)
    return jax.shard_map(
        functools.partial(local, sizes),
        mesh=mesh,
        in_specs=(
            P(("fsdp", "ctx"), None),
            P(("fsdp", "ctx"), None),
            P("fsdp", None),
            P(("fsdp", "ctx"), None),
            P("fsdp"),
            P("fsdp", "tp"),
            P("fsdp", "tp"),
            P("fsdp", "tp"),
            P("fsdp", "tp"),
            P("fsdp"),
            P("fsdp", None),
            P("fsdp", None, "tp"),
            P("fsdp", None, "tp"),
            P("fsdp", None, "tp"),
        ),
        out_specs=(
            P(("fsdp", "ctx"), None),
            P(("fsdp", "ctx"), None),
            P("fsdp"),
            P("fsdp", "tp"),
            P("fsdp", "tp"),
            P("fsdp", "tp"),
            P("fsdp", "tp"),
            P("fsdp"),
            P("fsdp", None),
            P("fsdp", None, "tp"),
            P("fsdp", None, "tp"),
            P("fsdp", None, "tp"),
        ),
        check_vma=False,
    )
```

```python
import functools
import math

import jax
import jax.numpy as jnp
from jax import lax
from jax.experimental import pallas as pl
from jax.experimental.pallas import tpu as pltpu
from jax.sharding import PartitionSpec as P

HEAD_SIZE = 64
CAP = 128
MESH = pl.DeviceIdType.MESH

norm_eps = 1e-06
rope_base = 10000.0
branch_scale = 0.22
highest = lax.Precision.HIGHEST
bf16 = jnp.bfloat16
f32 = jnp.float32


def exchange_kernel(plan, sizes, *refs):
    count = len(plan)
    ins, outs = refs[:count], refs[count : 2 * count]
    send_sem, recv_sem, self_sem = refs[2 * count :]

    def place(axes, step):
        offsets = []
        for axis in reversed(axes):
            offsets.append(step % sizes[axis])
            step //= sizes[axis]
        coords = {}
        for axis, offset in zip(axes, offsets[::-1]):
            here = lax.axis_index(axis)
            coords[axis] = lax.rem(here + offset, sizes[axis]) if offset else here
        return coords

    def flat(axes, coords):
        index = 0
        for axis in axes:
            index = index * sizes[axis] + coords[axis]
        return index

    groups = {}
    for axes, _ in plan:
        for step in range(1, math.prod(sizes[a] for a in axes)):
            full, rest = {}, step
            for axis in reversed(axes):
                full[axis] = rest % sizes[axis]
                rest //= sizes[axis]
            key = tuple(sorted((a, o) for a, o in full.items() if o))
            groups[key] = (axes, step)
    barrier = pltpu.get_barrier_semaphore()
    for axes, step in groups.values():
        pl.semaphore_signal(barrier, inc=1, device_id=place(axes, step), device_id_type=MESH)
    pl.semaphore_wait(barrier, len(groups))

    copies = []
    for at, (axes, mode) in enumerate(plan):
        mine = flat(axes, place(axes, 0))
        for step in range(1, math.prod(sizes[a] for a in axes)):
            if mode in "fb":
                peer = place(axes, step if mode == "f" else sizes[axes[0]] - step)
                source, slot = ins[at].at[step], step
            else:
                peer = place(axes, step)
                source = ins[at] if mode == "g" else ins[at].at[flat(axes, peer)]
                slot = mine
            copy = pltpu.make_async_remote_copy(
                src_ref=source,
                dst_ref=outs[at].at[slot],
                send_sem=send_sem.at[at, step],
                recv_sem=recv_sem.at[at, step],
                device_id=peer,
                device_id_type=MESH,
            )
            copy.start()
            copies.append(copy)
        if mode in "fb":
            mine = 0
        own = pltpu.make_async_copy(
            ins[at] if mode == "g" else ins[at].at[mine], outs[at].at[mine], self_sem.at[at]
        )
        own.start()
        copies.append(own)
    for copy in copies:
        copy.wait()


def exchange(sizes, collective_id, *items):
    plan = [(axes, mode) for axes, mode, _ in items]
    arrays = [array for _, _, array in items]
    outs = []
    most = 1
    for axes, mode, array in items:
        n = math.prod(sizes[a] for a in axes)
        most = max(most, n)
        shape = (n,) + array.shape if mode == "g" else array.shape
        outs.append(jax.ShapeDtypeStruct(shape, array.dtype))
    count = len(items)
    moved = sum(math.prod(o.shape) * o.dtype.itemsize for o in outs)
    return pl.pallas_call(
        functools.partial(exchange_kernel, plan, sizes),
        out_shape=outs,
        in_specs=[pl.BlockSpec(memory_space=pl.ANY)] * count,
        out_specs=[pl.BlockSpec(memory_space=pl.ANY)] * count,
        scratch_shapes=[
            pltpu.SemaphoreType.DMA((count, most)),
            pltpu.SemaphoreType.DMA((count, most)),
            pltpu.SemaphoreType.DMA((count,)),
        ],
        compiler_params=pltpu.CompilerParams(collective_id=collective_id, has_side_effects=True),
        cost_estimate=pl.CostEstimate(flops=0, bytes_accessed=20 * moved, transcendentals=0),
        name="exchange_%d" % collective_id,
    )(*arrays)


def spread_kernel(pieces_ref, *out_refs):
    experts = pieces_ref.shape[0]
    depth = pieces_ref.shape[2]
    for which, out_ref in enumerate(out_refs):
        for expert in range(experts):
            out_ref[pl.ds(expert, depth, stride=experts), :] = pieces_ref[expert, which].astype(f32)


def spread(pieces):
    experts, count, depth, ff = pieces.shape
    block = 64
    outs = pl.pallas_call(
        spread_kernel,
        grid=(depth // block,),
        out_shape=[jax.ShapeDtypeStruct((depth * experts, ff), f32)] * count,
        in_specs=[pl.BlockSpec((experts, count, block, ff), lambda i: (0, 0, i, 0))],
        out_specs=[pl.BlockSpec((block * experts, ff), lambda i: (i, 0))] * count,
        compiler_params=pltpu.CompilerParams(vmem_limit_bytes=32 * 1024 * 1024),
        name="spread",
    )(pieces)
    return [out.reshape(depth, experts, ff) for out in outs]


def expert_kernel(
    n,
    n_fsdp,
    part,
    rows_ref,
    probs_ref,
    grads_ref,
    w_ref,
    norm_got,
    mixed_got,
    gate_got,
    wgrad_ref,
    wgrad_buf,
    wgrad_got,
    norm_buf,
    probs_buf,
    both_buf,
    weighted_buf,
    back_buf,
    mixed_buf,
    gate_buf,
    send_sems,
    recv_sems,
    wgrad_send,
    wgrad_recv,
):
    me, fsdp_at = lax.axis_index("ctx"), lax.axis_index("fsdp")
    hidden = w_ref.shape[1] // 3

    def chunk(ref, k):
        return ref.at[pl.ds(pl.multiple_of(k * CAP, CAP), CAP)]

    def copy(which, k, source, target, place):
        return pltpu.make_async_remote_copy(
            src_ref=source,
            dst_ref=target,
            send_sem=send_sems.at[which, k],
            recv_sem=recv_sems.at[which, k],
            device_id={"ctx": lax.rem(place, n)},
            device_id_type=MESH,
        )

    def out_copies(k):
        return (
            copy(0, k, chunk(rows_ref, k), chunk(norm_buf, k), me + k),
            copy(1, k, probs_ref.at[k], probs_buf.at[k], me + k),
        )

    def back_copies(k):
        place = me + n - k
        return (
            copy(2, k, chunk(back_buf, k), chunk(norm_got, k), place),
            copy(3, k, gate_buf.at[k], gate_got.at[k], place),
            copy(4, k, chunk(mixed_buf, k), chunk(mixed_got, k), place),
        )

    barrier = pltpu.get_barrier_semaphore()
    for k in range(1, n):
        pl.semaphore_signal(
            barrier, inc=1, device_id={"ctx": lax.rem(me + k, n)}, device_id_type=MESH
        )
    for k in range(1, n_fsdp):
        pl.semaphore_signal(
            barrier,
            inc=1,
            device_id={"fsdp": lax.rem(fsdp_at + k, n_fsdp)},
            device_id_type=MESH,
        )
    pl.semaphore_wait(barrier, n - 1 + n_fsdp - 1)
    for k in range(1, 4):
        for item in out_copies(k):
            item.start()
    norm_buf[:CAP] = rows_ref[:CAP]
    probs_buf[0] = probs_ref[0]
    same = lax.broadcasted_iota(jnp.int32, (CAP, CAP), 0) == lax.broadcasted_iota(
        jnp.int32, (CAP, CAP), 1
    )

    def pair(j, carry):
        @pl.when(j < n // 2 - 2)
        def _():
            for k in (2 * j + 4, 2 * j + 5):
                for item in out_copies(k):
                    item.start()

        for k in (2 * j, 2 * j + 1):

            @pl.when(k > 0)
            def _():
                for item in out_copies(k):
                    item.wait_recv()

        here = pl.ds(pl.multiple_of(j * 2 * CAP, 2 * CAP), 2 * CAP)
        gate_up = mm(norm_buf[here, :], w_ref[:, : 2 * hidden])
        down_back = mm(grads_ref[here, :], w_ref[:, 2 * hidden :])
        probs = jnp.concatenate(
            [
                jnp.sum(jnp.where(same, probs_buf[k][:1, :], 0.0), axis=1, keepdims=True)
                for k in (2 * j, 2 * j + 1)
            ],
            axis=0,
        )
        gate_pre, up_pre = gate_up[:, :hidden], gate_up[:, hidden:]
        sig = jax.nn.sigmoid(gate_pre)
        silu = gate_pre * sig
        activation = silu * up_pre
        gate_grad = branch_scale * jnp.sum(activation * down_back, axis=1, keepdims=True)
        act_grad = (branch_scale * probs) * down_back
        both_buf[here, :hidden] = (
            act_grad * up_pre * sig * (1.0 + gate_pre * (1.0 - sig))
        ).astype(bf16)
        both_buf[here, hidden:] = (act_grad * silu).astype(bf16)
        weighted_buf[here, :] = (probs * activation).astype(bf16)
        back_buf[here, :] = contract_cols(both_buf[here, :], w_ref[:, : 2 * hidden]).astype(bf16)
        for i in range(2):
            line = jnp.sum(
                jnp.where(same, gate_grad[i * CAP : (i + 1) * CAP], 0.0), axis=0, keepdims=True
            )
            gate_buf[2 * j + i] = jnp.broadcast_to(line, (8, CAP))
        mixed_buf[here, :] = contract_cols(weighted_buf[here, :], w_ref[:, 2 * hidden :]).astype(
            bf16
        )
        for k in (2 * j, 2 * j + 1):

            @pl.when(k > 0)
            def _():
                for item in back_copies(k):
                    item.start()

        return carry

    lax.fori_loop(0, n // 2, pair, 0)
    norm_got[:CAP] = back_buf[:CAP]
    mixed_got[:CAP] = mixed_buf[:CAP]
    gate_got[0] = gate_buf[0]

    slim = wgrad_ref.shape[1]

    def wgrad_copy(k):
        return pltpu.make_async_remote_copy(
            src_ref=wgrad_buf.at[k],
            dst_ref=wgrad_got.at[k],
            send_sem=wgrad_send.at[k],
            recv_sem=wgrad_recv.at[k],
            device_id={"fsdp": lax.rem(fsdp_at + k, n_fsdp)},
            device_id_type=MESH,
        )

    def weight_grads(j, carry):
        k = lax.rem(j + 1, n_fsdp)
        here = pl.ds(pl.multiple_of(lax.rem(fsdp_at + k, n_fsdp) * part, part), part)
        gate_up = contract_rows(norm_buf[:, here], both_buf[...]).astype(bf16)
        down = (contract_rows(grads_ref[:, here], weighted_buf[...]) * branch_scale).astype(bf16)
        for piece in range(hidden // slim):
            for which in range(3):
                row = (piece * 3 + which) * part
                if which < 2:
                    start = which * hidden + piece * slim
                    wgrad_buf[k, row : row + part, :] = gate_up[:, start : start + slim]
                else:
                    wgrad_buf[k, row : row + part, :] = down[:, piece * slim : (piece + 1) * slim]

        @pl.when(k > 0)
        def _():
            wgrad_copy(k).start()

        return carry

    lax.fori_loop(0, n_fsdp, weight_grads, 0)
    for k in range(1, n_fsdp):
        wgrad_copy(k).wait()

    def summed(j, carry):
        at = pl.ds(pl.multiple_of(j * part, part), part)
        total = wgrad_buf[0, at, :].astype(f32)
        for k in range(1, n_fsdp):
            total += wgrad_got[k, at, :].astype(f32)
        wgrad_ref[at, :] = total.astype(bf16)
        return carry

    lax.fori_loop(0, wgrad_ref.shape[0] // part, summed, 0)
    for k in range(1, n):
        for item in out_copies(k):
            item.wait_send()
        for item in back_copies(k):
            item.wait()


def expert_of_place(sizes, rows_sent, probs_sent, grad_rows, expert_w):
    n = sizes["ctx"]
    total, width = rows_sent.shape
    n_fsdp, n_tp = sizes["fsdp"], sizes["tp"]
    hidden, part = expert_w.shape[1] // 3, width // n_fsdp
    owned = (n_tp * 3 * part, hidden // n_tp)
    like = jax.ShapeDtypeStruct
    vmem = pl.BlockSpec(memory_space=pltpu.VMEM)
    return pl.pallas_call(
        functools.partial(expert_kernel, n, n_fsdp, part),
        out_shape=[
            like((total, width), bf16),
            like((total, width), bf16),
            like(probs_sent.shape, f32),
            like(owned, bf16),
        ],
        in_specs=[vmem] * 4,
        out_specs=[vmem] * 4,
        scratch_shapes=[
            pltpu.VMEM((n_fsdp,) + owned, bf16),
            pltpu.VMEM((n_fsdp,) + owned, bf16),
            pltpu.VMEM((total, width), bf16),
            pltpu.VMEM(probs_sent.shape, f32),
            pltpu.VMEM((total, 2 * hidden), bf16),
            pltpu.VMEM((total, hidden), bf16),
            pltpu.VMEM((total, width), bf16),
            pltpu.VMEM((total, width), bf16),
            pltpu.VMEM(probs_sent.shape, f32),
            pltpu.SemaphoreType.DMA((5, n)),
            pltpu.SemaphoreType.DMA((5, n)),
            pltpu.SemaphoreType.DMA((n_fsdp,)),
            pltpu.SemaphoreType.DMA((n_fsdp,)),
        ],
        compiler_params=pltpu.CompilerParams(
            collective_id=3, has_side_effects=True, vmem_limit_bytes=48 * 1024 * 1024
        ),
        cost_estimate=pl.CostEstimate(
            flops=6 * 2 * total * width * hidden * 3, bytes_accessed=100 << 20, transcendentals=0
        ),
        name="expert_of_place",
    )(rows_sent, probs_sent, grad_rows, expert_w)


def rope_tables(places, columns):
    column = jnp.arange(columns, dtype=jnp.int32)
    steps = (column % (HEAD_SIZE // 2)).astype(f32)
    frequencies = jnp.exp(steps * (-2.0 * math.log(rope_base) / HEAD_SIZE))
    angles = places.astype(f32)[:, None] * frequencies[None, :]
    first = (column % HEAD_SIZE < HEAD_SIZE // 2)[None, :]
    sine = jnp.sin(angles)
    return jnp.cos(angles), jnp.where(first, -sine, sine), first


def turn(values, cosine, sine, first):
    half = HEAD_SIZE // 2
    other = jnp.where(first, jnp.roll(values, -half, axis=1), jnp.roll(values, half, axis=1))
    return values * cosine + other * sine


def contract_rows(left, right, precision=None):
    return lax.dot_general(
        left, right, (((0,), (0,)), ((), ())), precision=precision, preferred_element_type=f32
    )


def contract_cols(left, right, precision=None):
    return lax.dot_general(
        left, right, (((1,), (1,)), ((), ())), precision=precision, preferred_element_type=f32
    )


def mm(left, right):
    return jnp.dot(left, right, preferred_element_type=f32)


def local(
    sizes,
    inputs,
    cotangent,
    lengths,
    expert_ids,
    attn_gain,
    w_query,
    key_weight,
    value_weight,
    w_output,
    ffn_gain,
    w_router,
    w_gate,
    w_up,
    w_down,
):
    rows, width = inputs.shape
    n_fsdp, n_ctx, n_tp = sizes["fsdp"], sizes["ctx"], sizes["tp"]
    experts = w_router.shape[1]
    depth, _, ff = w_gate.shape
    per_ctx = experts // n_ctx
    send = functools.partial(exchange, sizes)
    ctx_at, tp_at = lax.axis_index("ctx"), lax.axis_index("tp")

    chosen = jnp.any(
        expert_ids[:, :, None] == jnp.arange(experts, dtype=jnp.int32)[None, None, :], axis=1
    )
    ctx_order = lax.rem(ctx_at + jnp.arange(n_ctx, dtype=jnp.int32), n_ctx)
    mine = ctx_order * per_ctx + tp_at
    chosen_mine = jnp.any(expert_ids[None, :, :] == mine[:, None, None], axis=2)
    earlier = jnp.arange(rows)[:, None] < jnp.arange(rows)[None, :]
    rank = mm(chosen_mine.astype(bf16), earlier.astype(bf16))
    slots = jnp.arange(CAP, dtype=f32)
    picks = (chosen_mine[:, None, :] & (rank[:, None, :] == slots[None, :, None])).astype(bf16)
    picks_flat = picks.reshape(n_ctx * CAP, rows)

    first = ctx_at * per_ctx
    own_slices = jnp.stack(
        [
            lax.dynamic_slice_in_dim(w, first, per_ctx, 1).transpose(1, 0, 2)
            for w in (w_gate, w_up, w_down)
        ],
        axis=1,
    )
    gains = jnp.concatenate(
        [
            attn_gain.reshape(-1, 128),
            ffn_gain.reshape(-1, 128),
            jnp.zeros((16 - 2 * depth // 128, 128), bf16),
        ],
        axis=0,
    )
    router_pad = jnp.pad(w_router, ((0, 0), (0, 128 - experts)))
    grads_sent = mm(picks_flat, cotangent).astype(bf16).reshape(n_ctx, CAP, width)
    qkv_w, gains_all, router_all, expert_slices, grad_rows = send(
        0,
        (("fsdp",), "g", jnp.concatenate([w_query, key_weight, value_weight], axis=1)),
        (("fsdp",), "g", gains),
        (("fsdp",), "g", router_pad),
        (("tp",), "a", own_slices),
        (("ctx",), "f", grads_sent),
    )
    qkv_w = qkv_w.reshape(width, -1)
    lines = depth // 128
    gain_one = gains_all[:, :lines].reshape(width).astype(f32)
    gain_two = gains_all[:, lines : 2 * lines].reshape(width).astype(f32)
    router_w = router_all.reshape(width, 128)[:, :experts]

    grad_rows = grad_rows.reshape(n_ctx * CAP, width)

    expert_cat = expert_slices.transpose(2, 1, 0, 3).reshape(depth, 3 * n_tp * ff)
    expert_w = lax.all_gather(expert_cat, "fsdp", axis=0, tiled=True)

    lengths_row = lengths[0]
    query_rows = ctx_at * rows + jnp.arange(rows, dtype=jnp.int32)
    seq_ends = jnp.cumsum(lengths_row)
    passed = (query_rows[:, None] >= seq_ends[None, :]).astype(jnp.int32)
    starts = jnp.sum(passed * lengths_row[None, :], axis=1)
    q_end, pair_width = w_query.shape[1], key_weight.shape[1]
    turned = q_end + pair_width
    cosine, sine, first_half = rope_tables(query_rows - starts, turned)
    hidden_in = inputs.astype(f32)
    scale_one = lax.rsqrt(jnp.mean(hidden_in * hidden_in, axis=-1, keepdims=True) + norm_eps)
    normed_one = (hidden_in * scale_one * gain_one).astype(bf16)
    qkv = mm(normed_one, qkv_w)
    queries_keys = turn(qkv[:, :turned], cosine, sine, first_half).astype(bf16)
    queries = queries_keys[:, :q_end]
    pairs_local = jnp.concatenate(
        [queries_keys[:, q_end:], qkv[:, turned:].astype(bf16)], axis=1
    )
    pairs_all, output_w = send(1, (("ctx",), "g", pairs_local), (("fsdp",), "g", w_output))
    output_w = output_w.reshape(width, -1)
    total_rows = n_ctx * rows
    pairs_all = pairs_all.reshape(total_rows, 2 * pair_width)
    key_heads = pair_width // HEAD_SIZE
    groups = queries.shape[1] // pair_width
    keys_all = pairs_all[:, :pair_width].reshape(total_rows, key_heads, HEAD_SIZE)
    values_all = pairs_all[:, pair_width:].reshape(total_rows, key_heads, HEAD_SIZE)
    query_head_rows = queries.reshape(rows, key_heads, groups, HEAD_SIZE)
    key_rows = jnp.arange(total_rows, dtype=jnp.int32)
    allowed = (key_rows[None, :] >= starts[:, None]) & (key_rows[None, :] <= query_rows[:, None])

    def masked_scores():
        raw_scores = jnp.einsum(
            "rkgd,skd->kgrs", query_head_rows, keys_all, preferred_element_type=f32
        )
        return jnp.where(allowed, raw_scores * HEAD_SIZE ** (-0.5), -1e30)

    masked = masked_scores()
    row_top = jnp.max(masked, axis=-1, keepdims=True)
    shifted_exp = jnp.exp(masked - row_top)
    row_total = jnp.sum(shifted_exp, axis=-1, keepdims=True)
    attn_probs = shifted_exp / row_total
    log_total = row_top + jnp.log(row_total)
    attended = jnp.einsum(
        "kgrs,skd->rkgd", attn_probs.astype(bf16), values_all, preferred_element_type=f32
    )
    attended = attended.reshape(rows, -1).astype(bf16)
    quarter = rows // n_tp

    def quarter_of(array):
        return lax.dynamic_slice_in_dim(array, tp_at * quarter, quarter, 0)

    attn_part = contract_cols(attended, output_w).astype(bf16)
    (attn_parts,) = send(2, (("tp",), "a", attn_part.reshape(n_tp, quarter, width)))
    hidden_own, scale_one_own = quarter_of(hidden_in), quarter_of(scale_one)
    residual_own = hidden_own + branch_scale * jnp.sum(attn_parts.astype(f32), axis=0)

    scale_two_own = lax.rsqrt(jnp.mean(residual_own * residual_own, axis=-1, keepdims=True) + norm_eps)
    normed_two_own = (residual_own * scale_two_own * gain_two).astype(bf16)
    (normed_two,) = send(11, (("tp",), "g", normed_two_own))
    normed_two = normed_two.reshape(rows, width)
    logits = mm(normed_two, router_w)
    route_masked = jnp.where(chosen, logits, -1e30)
    route_exp = jnp.exp(route_masked - jnp.max(route_masked, axis=-1, keepdims=True))
    gate_probs = route_exp / jnp.sum(route_exp, axis=-1, keepdims=True)
    probs_mine = lax.dynamic_index_in_dim(
        gate_probs.T.reshape(n_ctx, per_ctx, rows), tp_at, 1, keepdims=False
    )
    probs_mine = jnp.take(probs_mine, ctx_order, axis=0)
    probs_sent = jnp.sum(picks.astype(f32) * probs_mine[:, None, :], axis=2)
    rows_sent = mm(picks_flat, normed_two).astype(bf16)
    probs_sent = jnp.broadcast_to(probs_sent[:, None, :], (n_ctx, 8, CAP))
    norm_grad_got, mixed_got, gate_grad_got, expert_grad = expert_of_place(
        sizes, rows_sent, probs_sent, grad_rows, expert_w
    )

    norm_grad_part = contract_rows(picks_flat, norm_grad_got)
    gate_grad_part = jnp.sum(picks.astype(f32) * gate_grad_got[:, 0, :, None], axis=1)
    norm_grad_parts, gate_grad_parts, pieces = send(
        5,
        (("tp",), "a", norm_grad_part.astype(bf16).reshape(n_tp, quarter, width)),
        (("tp",), "g", gate_grad_part),
        (("tp",), "a", expert_grad.reshape(n_tp, 3, depth, ff)),
    )
    expert_all = lax.all_gather(pieces, "ctx", axis=0, tiled=True)

    back_order = lax.rem(jnp.arange(n_ctx, dtype=jnp.int32) + n_ctx - ctx_at, n_ctx)
    gate_grads = jnp.take(gate_grad_parts, back_order, axis=1)
    gate_grads = gate_grads.transpose(2, 1, 0).reshape(rows, experts)
    route_grad = gate_probs * (
        gate_grads - jnp.sum(gate_probs * gate_grads, axis=-1, keepdims=True)
    )
    grad_router = contract_rows(normed_two.astype(f32), route_grad, highest)
    router_back = contract_cols(quarter_of(route_grad), router_w.astype(f32), highest)
    normed_grad = jnp.sum(norm_grad_parts.astype(f32), axis=0) + router_back
    weighted_two = normed_grad * gain_two
    grad_ffn_part = jnp.sum(normed_grad * residual_own * scale_two_own, axis=0)
    residual_grad = (
        quarter_of(cotangent).astype(f32)
        + scale_two_own * weighted_two
        - residual_own
        * scale_two_own**3
        * jnp.mean(weighted_two * residual_own, axis=-1, keepdims=True)
    )
    (attn_in,) = send(6, (("tp",), "g", (branch_scale * residual_grad).astype(bf16)))
    attn_in = attn_in.reshape(rows, width)

    side = jnp.pad(grad_router, ((0, 0), (0, 128 - experts)))
    early = jnp.concatenate([contract_rows(attn_in, attended), side], axis=1).astype(bf16)
    mixed_part = contract_rows(picks_flat, mixed_got).astype(bf16)
    attended_grad = mm(attn_in, output_w).astype(bf16)

    grad_heads = attended_grad.reshape(rows, key_heads, groups, HEAD_SIZE)
    attn_probs = jnp.exp(masked_scores() - log_total)
    value_grad_all = jnp.einsum(
        "kgrs,rkgd->skd", attn_probs.astype(bf16), grad_heads, preferred_element_type=f32
    )
    prob_grad = jnp.einsum("rkgd,skd->kgrs", grad_heads, values_all, preferred_element_type=f32)
    score_grad = (
        attn_probs * (prob_grad - jnp.sum(attn_probs * prob_grad, axis=-1, keepdims=True))
    ).astype(bf16)
    query_grad_rot = jnp.einsum(
        "kgrs,skd->rkgd", score_grad, keys_all, preferred_element_type=f32
    ).reshape(rows, -1) * HEAD_SIZE ** (-0.5)
    key_grad_all = jnp.einsum(
        "kgrs,rkgd->skd", score_grad, query_head_rows, preferred_element_type=f32
    ) * HEAD_SIZE ** (-0.5)
    pair_grads = jnp.concatenate(
        [
            key_grad_all.reshape(total_rows, pair_width),
            value_grad_all.reshape(total_rows, pair_width),
        ],
        axis=1,
    ).astype(bf16)
    pair_got, mixed_parts, early_got = send(
        7,
        (("ctx",), "a", pair_grads.reshape(n_ctx, rows, 2 * pair_width)),
        (("tp",), "a", mixed_part.reshape(n_tp, quarter, width)),
        (("fsdp",), "a", early.reshape(n_fsdp, depth, -1)),
    )
    pair_owned = jnp.sum(pair_got.astype(f32), axis=0)
    turned_back = turn(
        jnp.concatenate([query_grad_rot, pair_owned[:, :pair_width]], axis=1),
        cosine,
        -sine,
        first_half,
    )
    qkv_grad = jnp.concatenate([turned_back, pair_owned[:, pair_width:]], axis=1).astype(bf16)
    normed_one_part = contract_cols(qkv_grad, qkv_w)
    grad_gain_part = jnp.sum(normed_one_part * hidden_in * scale_one, axis=0)
    grad_qkv = contract_rows(normed_one, qkv_grad).astype(bf16)
    output = residual_own + branch_scale * jnp.sum(mixed_parts.astype(f32), axis=0)

    gain_parts = jnp.stack([grad_gain_part, grad_ffn_part]).reshape(2, n_fsdp, depth)
    gain_chunks = jnp.pad(gain_parts.transpose(1, 0, 2), ((0, 0), (0, 6), (0, 0)))
    one_parts, qkv_got, gain_got, output = send(
        8,
        (("tp",), "a", normed_one_part.astype(bf16).reshape(n_tp, quarter, width)),
        (("fsdp",), "a", grad_qkv.reshape(n_fsdp, depth, -1)),
        (("fsdp",), "a", gain_chunks),
        (("tp",), "g", output.astype(bf16)),
    )
    small = jnp.concatenate(
        [
            jnp.sum(qkv_got.astype(f32), axis=0).astype(bf16),
            jnp.sum(early_got.astype(f32), axis=0).astype(bf16),
        ],
        axis=1,
    )
    gain_sum = jnp.sum(gain_got, axis=0)
    normed_one_grad = jnp.sum(one_parts.astype(f32), axis=0)
    weighted_one = normed_one_grad * gain_one
    input_grad = (
        residual_grad
        + scale_one_own * weighted_one
        - hidden_own
        * scale_one_own**3
        * jnp.mean(weighted_one * hidden_own, axis=-1, keepdims=True)
    )
    small_got, gain_all, input_grad = send(
        9,
        (("ctx",), "a", small.reshape(n_ctx, depth // n_ctx, -1)),
        (("ctx", "tp"), "g", gain_sum),
        (("tp",), "g", input_grad.astype(bf16)),
    )
    (small_all,) = send(10, (("ctx",), "g", jnp.sum(small_got.astype(f32), axis=0).astype(bf16)))
    small_all = small_all.reshape(depth, -1).astype(f32)
    gain_all = jnp.sum(gain_all, axis=0)
    grad_gate, grad_up, grad_down = spread(expert_all)
    k_end, v_end = q_end + pair_width, q_end + 2 * pair_width
    o_end = v_end + attended.shape[1]
    return (
        output.reshape(rows, width),
        input_grad.reshape(rows, width),
        gain_all[0],
        small_all[:, :q_end],
        small_all[:, q_end:k_end],
        small_all[:, k_end:v_end],
        small_all[:, v_end:o_end],
        gain_all[1],
        small_all[:, o_end : o_end + experts],
        grad_gate,
        grad_up,
        grad_down,
    )


def solution(mesh):
    sizes = dict(mesh.shape)
    return jax.shard_map(
        functools.partial(local, sizes),
        mesh=mesh,
        in_specs=(
            P(("fsdp", "ctx"), None),
            P(("fsdp", "ctx"), None),
            P("fsdp", None),
            P(("fsdp", "ctx"), None),
            P("fsdp"),
            P("fsdp", "tp"),
            P("fsdp", "tp"),
            P("fsdp", "tp"),
            P("fsdp", "tp"),
            P("fsdp"),
            P("fsdp", None),
            P("fsdp", None, "tp"),
            P("fsdp", None, "tp"),
            P("fsdp", None, "tp"),
        ),
        out_specs=(
            P(("fsdp", "ctx"), None),
            P(("fsdp", "ctx"), None),
            P("fsdp"),
            P("fsdp", "tp"),
            P("fsdp", "tp"),
            P("fsdp", "tp"),
            P("fsdp", "tp"),
            P("fsdp"),
            P("fsdp", None),
            P("fsdp", None, "tp"),
            P("fsdp", None, "tp"),
            P("fsdp", None, "tp"),
        ),
        check_vma=False,
    )
```

```python
import functools
import math

import jax
import jax.numpy as jnp
from jax import lax
from jax.experimental import pallas as pl
from jax.experimental.pallas import tpu as pltpu
from jax.sharding import PartitionSpec as P

HEAD_SIZE = 64
CAP = 128
MESH = pl.DeviceIdType.MESH

norm_eps = 1e-06
rope_base = 10000.0
branch_scale = 0.22
highest = lax.Precision.HIGHEST
bf16 = jnp.bfloat16
f32 = jnp.float32


def offset(slot, n):
    return slot // 2 + slot % 2 * (n // 2)


def exchange_kernel(plan, sizes, *refs):
    count = len(plan)
    ins, outs = refs[:count], refs[count : 2 * count]
    send_sem, recv_sem, self_sem = refs[2 * count :]

    def place(axes, step):
        offsets = []
        for axis in reversed(axes):
            offsets.append(step % sizes[axis])
            step //= sizes[axis]
        coords = {}
        for axis, offset in zip(axes, offsets[::-1]):
            here = lax.axis_index(axis)
            coords[axis] = lax.rem(here + offset, sizes[axis]) if offset else here
        return coords

    def flat(axes, coords):
        index = 0
        for axis in axes:
            index = index * sizes[axis] + coords[axis]
        return index

    groups = {}
    for axes, _ in plan:
        for step in range(1, math.prod(sizes[a] for a in axes)):
            full, rest = {}, step
            for axis in reversed(axes):
                full[axis] = rest % sizes[axis]
                rest //= sizes[axis]
            key = tuple(sorted((a, o) for a, o in full.items() if o))
            groups[key] = (axes, step)
    barrier = pltpu.get_barrier_semaphore()
    for axes, step in groups.values():
        pl.semaphore_signal(barrier, inc=1, device_id=place(axes, step), device_id_type=MESH)
    pl.semaphore_wait(barrier, len(groups))

    copies = []
    for at, (axes, mode) in enumerate(plan):
        mine = flat(axes, place(axes, 0))
        for step in range(1, math.prod(sizes[a] for a in axes)):
            if mode == "f":
                peer = place(axes, offset(step, sizes[axes[0]]))
                source, slot = ins[at].at[step], step
            else:
                peer = place(axes, step)
                source = ins[at] if mode == "g" else ins[at].at[flat(axes, peer)]
                slot = mine
            copy = pltpu.make_async_remote_copy(
                src_ref=source,
                dst_ref=outs[at].at[slot],
                send_sem=send_sem.at[at, step],
                recv_sem=recv_sem.at[at, step],
                device_id=peer,
                device_id_type=MESH,
            )
            copy.start()
            copies.append(copy)
        if mode == "f":
            mine = 0
        own = pltpu.make_async_copy(
            ins[at] if mode == "g" else ins[at].at[mine], outs[at].at[mine], self_sem.at[at]
        )
        own.start()
        copies.append(own)
    for copy in copies:
        copy.wait()


def exchange(sizes, collective_id, *items):
    plan = [(axes, mode) for axes, mode, _ in items]
    arrays = [array for _, _, array in items]
    outs = []
    most = 1
    for axes, mode, array in items:
        n = math.prod(sizes[a] for a in axes)
        most = max(most, n)
        shape = (n,) + array.shape if mode == "g" else array.shape
        outs.append(jax.ShapeDtypeStruct(shape, array.dtype))
    count = len(items)
    moved = sum(math.prod(o.shape) * o.dtype.itemsize for o in outs)
    return pl.pallas_call(
        functools.partial(exchange_kernel, plan, sizes),
        out_shape=outs,
        in_specs=[pl.BlockSpec(memory_space=pl.ANY)] * count,
        out_specs=[pl.BlockSpec(memory_space=pl.ANY)] * count,
        scratch_shapes=[
            pltpu.SemaphoreType.DMA((count, most)),
            pltpu.SemaphoreType.DMA((count, most)),
            pltpu.SemaphoreType.DMA((count,)),
        ],
        compiler_params=pltpu.CompilerParams(collective_id=collective_id, has_side_effects=True),
        cost_estimate=pl.CostEstimate(flops=0, bytes_accessed=20 * moved, transcendentals=0),
        name="exchange_%d" % collective_id,
    )(*arrays)


def spread_kernel(steps, early_ref, late_ref, *out_refs):
    experts, _, depth, _ = early_ref.shape

    def write(pieces_ref):
        for which, out_ref in enumerate(out_refs):
            for expert in range(experts):
                out_ref[pl.ds(expert, depth, stride=experts), :] = pieces_ref[
                    expert, which
                ].astype(f32)

    @pl.when(pl.program_id(0) < steps)
    def _():
        write(early_ref)

    @pl.when(pl.program_id(0) >= steps)
    def _():
        write(late_ref)


def spread(early, late):
    experts, count, depth, ff = early.shape
    block = 64
    steps = depth // block
    shape = (experts, count, block, ff)
    outs = pl.pallas_call(
        functools.partial(spread_kernel, steps),
        grid=(2 * steps,),
        out_shape=[jax.ShapeDtypeStruct((2 * depth * experts, ff), f32)] * count,
        in_specs=[
            pl.BlockSpec(shape, lambda i: (0, 0, jnp.minimum(i, steps - 1), 0)),
            pl.BlockSpec(shape, lambda i: (0, 0, jnp.maximum(i - steps, 0), 0)),
        ],
        out_specs=[pl.BlockSpec((block * experts, ff), lambda i: (i, 0))] * count,
        compiler_params=pltpu.CompilerParams(vmem_limit_bytes=40 * 1024 * 1024),
        name="spread",
    )(early, late)
    return [out.reshape(2 * depth, experts, ff) for out in outs]


def attention_back_kernel(groups, starts_ref, first_ref, queries_ref, grads_ref, pairs_ref, query_out, pair_out, probs, back):
    rows = queries_ref.shape[0]
    total, both = pairs_ref.shape
    pair_width = both // 2
    block = 512
    blocks = [slice(at, at + block) for at in range(0, total, block)]
    scale = HEAD_SIZE ** (-0.5)
    places = jnp.concatenate([first_ref[0, 0] + lax.broadcasted_iota(jnp.int32, (rows, 1), 0)] * groups, axis=0)
    starts = jnp.concatenate([starts_ref[...]] * groups, axis=0)
    query_parts, key_parts, value_parts = [], [], []
    for head in range(pair_width // HEAD_SIZE):

        def heads_of(ref):
            at = [(head * groups + g) * HEAD_SIZE for g in range(groups)]
            return jnp.concatenate([ref[:, a : a + HEAD_SIZE] for a in at], axis=0)

        queries, grads = heads_of(queries_ref), heads_of(grads_ref)
        own = slice(head * HEAD_SIZE, (head + 1) * HEAD_SIZE)
        own_values = slice(pair_width + own.start, pair_width + own.stop)
        top = jnp.full((rows * groups, 1), -1e30, f32)
        for part in blocks:
            key_rows = part.start + lax.broadcasted_iota(jnp.int32, (1, block), 1)
            allowed = (key_rows >= starts) & (key_rows <= places)
            scores = contract_cols(queries, pairs_ref[part, own]) * scale
            scores = jnp.where(allowed, scores, -1e30)
            probs[:, part] = scores
            top = jnp.maximum(top, jnp.max(scores, axis=1, keepdims=True))
        count = jnp.zeros((rows * groups, 1), f32)
        for part in blocks:
            raised = jnp.exp(probs[:, part] - top)
            probs[:, part] = raised
            count += jnp.sum(raised, axis=1, keepdims=True)
        share = 1.0 / count
        mean = jnp.zeros((rows * groups, 1), f32)
        for part in blocks:
            weights = probs[:, part] * share
            probs[:, part] = weights
            prob_grad = contract_cols(grads, pairs_ref[part, own_values])
            back[:, part] = prob_grad
            mean += jnp.sum(weights * prob_grad, axis=1, keepdims=True)
        query_grad = jnp.zeros((rows * groups, HEAD_SIZE), f32)
        keys_here, values_here = [], []
        for part in blocks:
            weights = probs[:, part]
            score_grad = (weights * (back[:, part] - mean)).astype(bf16)
            query_grad += mm(score_grad, pairs_ref[part, own])
            keys_here.append((contract_rows(score_grad, queries) * scale).astype(bf16))
            values_here.append(contract_rows(weights.astype(bf16), grads).astype(bf16))
        query_grad = query_grad * scale
        query_parts += [query_grad[g * rows : (g + 1) * rows] for g in range(groups)]
        key_parts.append(jnp.concatenate(keys_here, axis=0))
        value_parts.append(jnp.concatenate(values_here, axis=0))
    query_out[...] = jnp.concatenate(query_parts, axis=1)
    pair_out[...] = jnp.concatenate(key_parts + value_parts, axis=1)


def attention_back(starts, first_row, queries, grads, pairs, pair_width):
    rows, q_width = queries.shape
    total = pairs.shape[0]
    groups = q_width // pair_width
    vmem = pl.BlockSpec(memory_space=pltpu.VMEM)
    return pl.pallas_call(
        functools.partial(attention_back_kernel, groups),
        out_shape=[
            jax.ShapeDtypeStruct((rows, q_width), f32),
            jax.ShapeDtypeStruct((total, 2 * pair_width), bf16),
        ],
        in_specs=[vmem, pl.BlockSpec(memory_space=pltpu.SMEM), vmem, vmem, vmem],
        out_specs=[vmem, vmem],
        scratch_shapes=[pltpu.VMEM((rows * groups, total), f32)] * 2,
        compiler_params=pltpu.CompilerParams(vmem_limit_bytes=48 * 1024 * 1024),
        cost_estimate=pl.CostEstimate(
            flops=10 * rows * q_width * total, bytes_accessed=8 << 20, transcendentals=rows * total * 4
        ),
        name="attention_back",
    )(starts.reshape(rows, 1), first_row.reshape(1, 1), queries, grads, pairs)


def expert_kernel(
    n,
    n_fsdp,
    part,
    rows_ref,
    probs_ref,
    grads_ref,
    w_ref,
    norm_got,
    mixed_got,
    gate_got,
    wgrad_ref,
    wgrad_late_ref,
    wgrad_buf,
    wgrad_got,
    norm_buf,
    probs_buf,
    both_buf,
    weighted_buf,
    back_buf,
    mixed_buf,
    gate_buf,
    send_sems,
    recv_sems,
    wgrad_send,
    wgrad_recv,
):
    me, fsdp_at = lax.axis_index("ctx"), lax.axis_index("fsdp")
    hidden = w_ref.shape[1] // 3

    def chunk(ref, k):
        return ref.at[pl.ds(pl.multiple_of(k * CAP, CAP), CAP)]

    def copy(which, k, source, target, place):
        return pltpu.make_async_remote_copy(
            src_ref=source,
            dst_ref=target,
            send_sem=send_sems.at[which, k],
            recv_sem=recv_sems.at[which, k],
            device_id={"ctx": lax.rem(place, n)},
            device_id_type=MESH,
        )

    def out_copies(k):
        place = me + offset(k, n)
        return (
            copy(0, k, chunk(rows_ref, k), chunk(norm_buf, k), place),
            copy(1, k, probs_ref.at[k], probs_buf.at[k], place),
        )

    def back_copies(k):
        place = me + n - offset(k, n)
        return (
            copy(2, k, chunk(back_buf, k), chunk(norm_got, k), place),
            copy(3, k, gate_buf.at[k], gate_got.at[k], place),
            copy(4, k, chunk(mixed_buf, k), chunk(mixed_got, k), place),
        )

    barrier = pltpu.get_barrier_semaphore()
    for k in range(1, n):
        pl.semaphore_signal(
            barrier, inc=1, device_id={"ctx": lax.rem(me + k, n)}, device_id_type=MESH
        )
    for k in range(1, n_fsdp):
        pl.semaphore_signal(
            barrier,
            inc=1,
            device_id={"fsdp": lax.rem(fsdp_at + k, n_fsdp)},
            device_id_type=MESH,
        )
    pl.semaphore_wait(barrier, n - 1 + n_fsdp - 1)
    for k in range(1, 4):
        for item in out_copies(k):
            item.start()
    norm_buf[:CAP] = rows_ref[:CAP]
    probs_buf[0] = probs_ref[0]
    same = lax.broadcasted_iota(jnp.int32, (CAP, CAP), 0) == lax.broadcasted_iota(
        jnp.int32, (CAP, CAP), 1
    )

    def pair(j, carry):
        @pl.when(j < n // 2 - 2)
        def _():
            for k in (2 * j + 4, 2 * j + 5):
                for item in out_copies(k):
                    item.start()

        for k in (2 * j, 2 * j + 1):

            @pl.when(k > 0)
            def _():
                for item in out_copies(k):
                    item.wait_recv()

        here = pl.ds(pl.multiple_of(j * 2 * CAP, 2 * CAP), 2 * CAP)
        gate_up = mm(norm_buf[here, :], w_ref[:, : 2 * hidden])
        down_back = mm(grads_ref[here, :], w_ref[:, 2 * hidden :])
        probs = jnp.concatenate(
            [
                jnp.sum(jnp.where(same, probs_buf[k][:1, :], 0.0), axis=1, keepdims=True)
                for k in (2 * j, 2 * j + 1)
            ],
            axis=0,
        )
        gate_pre, up_pre = gate_up[:, :hidden], gate_up[:, hidden:]
        sig = jax.nn.sigmoid(gate_pre)
        silu = gate_pre * sig
        activation = silu * up_pre
        gate_grad = branch_scale * jnp.sum(activation * down_back, axis=1, keepdims=True)
        act_grad = (branch_scale * probs) * down_back
        both_buf[here, :hidden] = (
            act_grad * up_pre * sig * (1.0 + gate_pre * (1.0 - sig))
        ).astype(bf16)
        both_buf[here, hidden:] = (act_grad * silu).astype(bf16)
        weighted_buf[here, :] = (probs * activation).astype(bf16)
        back_buf[here, :] = contract_cols(both_buf[here, :], w_ref[:, : 2 * hidden]).astype(bf16)
        for i in range(2):
            line = jnp.sum(
                jnp.where(same, gate_grad[i * CAP : (i + 1) * CAP], 0.0), axis=0, keepdims=True
            )
            gate_buf[2 * j + i] = jnp.broadcast_to(line, (8, CAP))
        mixed_buf[here, :] = contract_cols(weighted_buf[here, :], w_ref[:, 2 * hidden :]).astype(
            bf16
        )
        for k in (2 * j, 2 * j + 1):

            @pl.when(k > 0)
            def _():
                for item in back_copies(k):
                    item.start()

        return carry

    lax.fori_loop(0, n // 2, pair, 0)
    norm_got[:CAP] = back_buf[:CAP]
    mixed_got[:CAP] = mixed_buf[:CAP]
    gate_got[0] = gate_buf[0]

    slim = wgrad_ref.shape[1]

    def wgrad_copy(k):
        return pltpu.make_async_remote_copy(
            src_ref=wgrad_buf.at[k],
            dst_ref=wgrad_got.at[k],
            send_sem=wgrad_send.at[k],
            recv_sem=wgrad_recv.at[k],
            device_id={"fsdp": lax.rem(fsdp_at + k, n_fsdp)},
            device_id_type=MESH,
        )

    def weight_grads(j, carry):
        k = lax.rem(j + 1, n_fsdp)
        here = pl.ds(pl.multiple_of(lax.rem(fsdp_at + k, n_fsdp) * part, part), part)
        gate_up = contract_rows(norm_buf[:, here], both_buf[...]).astype(bf16)
        down = (contract_rows(grads_ref[:, here], weighted_buf[...]) * branch_scale).astype(bf16)
        for piece in range(hidden // slim):
            for which in range(3):
                row = (piece * 3 + which) * part
                if which < 2:
                    start = which * hidden + piece * slim
                    wgrad_buf[k, row : row + part, :] = gate_up[:, start : start + slim]
                else:
                    wgrad_buf[k, row : row + part, :] = down[:, piece * slim : (piece + 1) * slim]

        @pl.when(k > 0)
        def _():
            wgrad_copy(k).start()

        return carry

    lax.fori_loop(0, n_fsdp, weight_grads, 0)
    for k in range(1, n_fsdp):
        wgrad_copy(k).wait()

    def summed(j, carry):
        at = pl.ds(pl.multiple_of(j * part, part), part)
        total = wgrad_buf[0, at, :].astype(f32)
        for k in range(1, n_fsdp):
            total += wgrad_got[k, at, :].astype(f32)
        half = part // 2
        to = pl.ds(pl.multiple_of(j * half, half), half)
        wgrad_ref[to, :] = total[:half].astype(bf16)
        wgrad_late_ref[to, :] = total[half:].astype(bf16)
        return carry

    lax.fori_loop(0, wgrad_buf.shape[1] // part, summed, 0)
    for k in range(1, n):
        for item in out_copies(k):
            item.wait_send()
        for item in back_copies(k):
            item.wait()


def expert_of_place(sizes, rows_sent, probs_sent, grad_rows, expert_w):
    n = sizes["ctx"]
    total, width = rows_sent.shape
    n_fsdp, n_tp = sizes["fsdp"], sizes["tp"]
    hidden, part = expert_w.shape[1] // 3, width // n_fsdp
    owned = (n_tp * 3 * part, hidden // n_tp)
    like = jax.ShapeDtypeStruct
    vmem = pl.BlockSpec(memory_space=pltpu.VMEM)
    return pl.pallas_call(
        functools.partial(expert_kernel, n, n_fsdp, part),
        out_shape=[
            like((total, width), bf16),
            like((total, width), bf16),
            like(probs_sent.shape, f32),
            like((owned[0] // 2, owned[1]), bf16),
            like((owned[0] // 2, owned[1]), bf16),
        ],
        in_specs=[vmem] * 4,
        out_specs=[vmem] * 5,
        scratch_shapes=[
            pltpu.VMEM((n_fsdp,) + owned, bf16),
            pltpu.VMEM((n_fsdp,) + owned, bf16),
            pltpu.VMEM((total, width), bf16),
            pltpu.VMEM(probs_sent.shape, f32),
            pltpu.VMEM((total, 2 * hidden), bf16),
            pltpu.VMEM((total, hidden), bf16),
            pltpu.VMEM((total, width), bf16),
            pltpu.VMEM((total, width), bf16),
            pltpu.VMEM(probs_sent.shape, f32),
            pltpu.SemaphoreType.DMA((5, n)),
            pltpu.SemaphoreType.DMA((5, n)),
            pltpu.SemaphoreType.DMA((n_fsdp,)),
            pltpu.SemaphoreType.DMA((n_fsdp,)),
        ],
        compiler_params=pltpu.CompilerParams(
            collective_id=3, has_side_effects=True, vmem_limit_bytes=48 * 1024 * 1024
        ),
        cost_estimate=pl.CostEstimate(
            flops=6 * 2 * total * width * hidden * 3, bytes_accessed=100 << 20, transcendentals=0
        ),
        name="expert_of_place",
    )(rows_sent, probs_sent, grad_rows, expert_w)


def rope_tables(places, columns):
    column = jnp.arange(columns, dtype=jnp.int32)
    steps = (column % (HEAD_SIZE // 2)).astype(f32)
    frequencies = jnp.exp(steps * (-2.0 * math.log(rope_base) / HEAD_SIZE))
    angles = places.astype(f32)[:, None] * frequencies[None, :]
    first = (column % HEAD_SIZE < HEAD_SIZE // 2)[None, :]
    sine = jnp.sin(angles)
    return jnp.cos(angles), jnp.where(first, -sine, sine), first


def turn(values, cosine, sine, first):
    half = HEAD_SIZE // 2
    other = jnp.where(first, jnp.roll(values, -half, axis=1), jnp.roll(values, half, axis=1))
    return values * cosine + other * sine


def contract_rows(left, right, precision=None):
    return lax.dot_general(
        left, right, (((0,), (0,)), ((), ())), precision=precision, preferred_element_type=f32
    )


def contract_cols(left, right, precision=None):
    return lax.dot_general(
        left, right, (((1,), (1,)), ((), ())), precision=precision, preferred_element_type=f32
    )


def mm(left, right):
    return jnp.dot(left, right, preferred_element_type=f32)


def local(
    sizes,
    inputs,
    cotangent,
    lengths,
    expert_ids,
    attn_gain,
    w_query,
    key_weight,
    value_weight,
    w_output,
    ffn_gain,
    w_router,
    w_gate,
    w_up,
    w_down,
):
    rows, width = inputs.shape
    n_fsdp, n_ctx, n_tp = sizes["fsdp"], sizes["ctx"], sizes["tp"]
    experts = w_router.shape[1]
    depth, _, ff = w_gate.shape
    per_ctx = experts // n_ctx
    send = functools.partial(exchange, sizes)
    ctx_at, tp_at = lax.axis_index("ctx"), lax.axis_index("tp")

    chosen = jnp.any(
        expert_ids[:, :, None] == jnp.arange(experts, dtype=jnp.int32)[None, None, :], axis=1
    )
    offsets = [offset(slot, n_ctx) for slot in range(n_ctx)]
    ctx_order = lax.rem(ctx_at + jnp.array(offsets, dtype=jnp.int32), n_ctx)
    mine = ctx_order * per_ctx + tp_at
    chosen_mine = jnp.any(expert_ids[None, :, :] == mine[:, None, None], axis=2)
    earlier = jnp.arange(rows)[:, None] < jnp.arange(rows)[None, :]
    rank = mm(chosen_mine.astype(bf16), earlier.astype(bf16))
    slots = jnp.arange(CAP, dtype=f32)
    picks = (chosen_mine[:, None, :] & (rank[:, None, :] == slots[None, :, None])).astype(bf16)
    picks_flat = picks.reshape(n_ctx * CAP, rows)

    first = ctx_at * per_ctx
    own_slices = jnp.stack(
        [
            lax.dynamic_slice_in_dim(w, first, per_ctx, 1).transpose(1, 0, 2)
            for w in (w_gate, w_up, w_down)
        ],
        axis=1,
    )
    gains = jnp.concatenate(
        [
            attn_gain.reshape(-1, 128),
            ffn_gain.reshape(-1, 128),
            jnp.zeros((16 - 2 * depth // 128, 128), bf16),
        ],
        axis=0,
    )
    router_pad = jnp.pad(w_router, ((0, 0), (0, 128 - experts)))
    grads_sent = mm(picks_flat, cotangent).astype(bf16).reshape(n_ctx, CAP, width)
    qkv_w, gains_all, router_all, expert_slices, grad_rows = send(
        0,
        (("fsdp",), "g", jnp.concatenate([w_query, key_weight, value_weight], axis=1)),
        (("fsdp",), "g", gains),
        (("fsdp",), "g", router_pad),
        (("tp",), "a", own_slices),
        (("ctx",), "f", grads_sent),
    )
    qkv_w = qkv_w.reshape(width, -1)
    lines = depth // 128
    gain_one = gains_all[:, :lines].reshape(width).astype(f32)
    gain_two = gains_all[:, lines : 2 * lines].reshape(width).astype(f32)
    router_w = router_all.reshape(width, 128)[:, :experts]

    grad_rows = grad_rows.reshape(n_ctx * CAP, width)

    expert_cat = expert_slices.transpose(2, 1, 0, 3).reshape(depth, 3 * n_tp * ff)
    expert_w = lax.all_gather(expert_cat, "fsdp", axis=0, tiled=True)

    lengths_row = lengths[0]
    query_rows = ctx_at * rows + jnp.arange(rows, dtype=jnp.int32)
    seq_ends = jnp.cumsum(lengths_row)
    passed = (query_rows[:, None] >= seq_ends[None, :]).astype(jnp.int32)
    starts = jnp.sum(passed * lengths_row[None, :], axis=1)
    q_end, pair_width = w_query.shape[1], key_weight.shape[1]
    turned = q_end + pair_width
    cosine, sine, first_half = rope_tables(query_rows - starts, turned)
    hidden_in = inputs.astype(f32)
    scale_one = lax.rsqrt(jnp.mean(hidden_in * hidden_in, axis=-1, keepdims=True) + norm_eps)
    normed_one = (hidden_in * scale_one * gain_one).astype(bf16)
    qkv = mm(normed_one, qkv_w)
    queries_keys = turn(qkv[:, :turned], cosine, sine, first_half).astype(bf16)
    queries = queries_keys[:, :q_end]
    pairs_local = jnp.concatenate(
        [queries_keys[:, q_end:], qkv[:, turned:].astype(bf16)], axis=1
    )
    pairs_all, output_w = send(1, (("ctx",), "g", pairs_local), (("fsdp",), "g", w_output))
    output_w = output_w.reshape(width, -1)
    total_rows = n_ctx * rows
    pairs_all = pairs_all.reshape(total_rows, 2 * pair_width)
    key_heads = pair_width // HEAD_SIZE
    groups = queries.shape[1] // pair_width
    keys_all = pairs_all[:, :pair_width].reshape(total_rows, key_heads, HEAD_SIZE)
    values_all = pairs_all[:, pair_width:].reshape(total_rows, key_heads, HEAD_SIZE)
    query_head_rows = queries.reshape(rows, key_heads, groups, HEAD_SIZE)
    key_rows = jnp.arange(total_rows, dtype=jnp.int32)
    allowed = (key_rows[None, :] >= starts[:, None]) & (key_rows[None, :] <= query_rows[:, None])

    raw_scores = jnp.einsum("rkgd,skd->kgrs", query_head_rows, keys_all, preferred_element_type=f32)
    masked = jnp.where(allowed, raw_scores * HEAD_SIZE ** (-0.5), -1e30)
    row_top = jnp.max(masked, axis=-1, keepdims=True)
    shifted_exp = jnp.exp(masked - row_top)
    attn_probs = shifted_exp / jnp.sum(shifted_exp, axis=-1, keepdims=True)
    attended = jnp.einsum(
        "kgrs,skd->rkgd", attn_probs.astype(bf16), values_all, preferred_element_type=f32
    )
    attended = attended.reshape(rows, -1).astype(bf16)
    quarter = rows // n_tp

    def quarter_of(array):
        return lax.dynamic_slice_in_dim(array, tp_at * quarter, quarter, 0)

    attn_part = contract_cols(attended, output_w).astype(bf16)
    (attn_parts,) = send(2, (("tp",), "a", attn_part.reshape(n_tp, quarter, width)))
    hidden_own, scale_one_own = quarter_of(hidden_in), quarter_of(scale_one)
    residual_own = hidden_own + branch_scale * jnp.sum(attn_parts.astype(f32), axis=0)

    scale_two_own = lax.rsqrt(jnp.mean(residual_own * residual_own, axis=-1, keepdims=True) + norm_eps)
    normed_two_own = (residual_own * scale_two_own * gain_two).astype(bf16)
    (normed_two,) = send(11, (("tp",), "g", normed_two_own))
    normed_two = normed_two.reshape(rows, width)
    logits = mm(normed_two, router_w)
    route_masked = jnp.where(chosen, logits, -1e30)
    route_exp = jnp.exp(route_masked - jnp.max(route_masked, axis=-1, keepdims=True))
    gate_probs = route_exp / jnp.sum(route_exp, axis=-1, keepdims=True)
    probs_mine = lax.dynamic_index_in_dim(
        gate_probs.T.reshape(n_ctx, per_ctx, rows), tp_at, 1, keepdims=False
    )
    probs_mine = jnp.take(probs_mine, ctx_order, axis=0)
    probs_sent = jnp.sum(picks.astype(f32) * probs_mine[:, None, :], axis=2)
    rows_sent = mm(picks_flat, normed_two).astype(bf16)
    probs_sent = jnp.broadcast_to(probs_sent[:, None, :], (n_ctx, 8, CAP))
    norm_grad_got, mixed_got, gate_grad_got, *expert_grads = expert_of_place(
        sizes, rows_sent, probs_sent, grad_rows, expert_w
    )

    norm_grad_part = contract_rows(picks_flat, norm_grad_got)
    gate_grad_part = jnp.sum(picks.astype(f32) * gate_grad_got[:, 0, :, None], axis=1)
    norm_grad_parts, gate_grad_parts, pieces, late_pieces = send(
        5,
        (("tp",), "a", norm_grad_part.astype(bf16).reshape(n_tp, quarter, width)),
        (("tp",), "g", gate_grad_part),
        *[(("tp",), "a", grad.reshape(n_tp, 3, depth // 2, ff)) for grad in expert_grads],
    )
    expert_all = lax.all_gather(pieces, "ctx", axis=0, tiled=True)

    slot_of = jnp.array([offsets.index(k) for k in range(n_ctx)], dtype=jnp.int32)
    back_order = slot_of[lax.rem(jnp.arange(n_ctx, dtype=jnp.int32) + n_ctx - ctx_at, n_ctx)]
    gate_grads = jnp.take(gate_grad_parts, back_order, axis=1)
    gate_grads = gate_grads.transpose(2, 1, 0).reshape(rows, experts)
    route_grad = gate_probs * (
        gate_grads - jnp.sum(gate_probs * gate_grads, axis=-1, keepdims=True)
    )
    grad_router = contract_rows(normed_two.astype(f32), route_grad, highest)
    router_back = contract_cols(quarter_of(route_grad), router_w.astype(f32), highest)
    normed_grad = jnp.sum(norm_grad_parts.astype(f32), axis=0) + router_back
    weighted_two = normed_grad * gain_two
    grad_ffn_part = jnp.sum(normed_grad * residual_own * scale_two_own, axis=0)
    residual_grad = (
        quarter_of(cotangent).astype(f32)
        + scale_two_own * weighted_two
        - residual_own
        * scale_two_own**3
        * jnp.mean(weighted_two * residual_own, axis=-1, keepdims=True)
    )
    (attn_in,) = send(6, (("tp",), "g", (branch_scale * residual_grad).astype(bf16)))
    attn_in = attn_in.reshape(rows, width)

    side = jnp.pad(grad_router, ((0, 0), (0, 128 - experts)))
    early = jnp.concatenate([contract_rows(attn_in, attended), side], axis=1).astype(bf16)
    mixed_part = contract_rows(picks_flat, mixed_got).astype(bf16)
    attended_grad = mm(attn_in, output_w).astype(bf16)

    query_grad_rot, pair_grads = attention_back(
        starts, ctx_at * rows, queries, attended_grad, pairs_all, pair_width
    )
    pair_got, mixed_parts, early_got = send(
        7,
        (("ctx",), "a", pair_grads.reshape(n_ctx, rows, 2 * pair_width)),
        (("tp",), "a", mixed_part.reshape(n_tp, quarter, width)),
        (("fsdp",), "a", early.reshape(n_fsdp, depth, -1)),
    )
    late_pieces, pair_got = lax.optimization_barrier((late_pieces, pair_got))
    late_all = lax.all_gather(late_pieces, "ctx", axis=0, tiled=True)
    pair_owned = jnp.sum(pair_got.astype(f32), axis=0)
    turned_back = turn(
        jnp.concatenate([query_grad_rot, pair_owned[:, :pair_width]], axis=1),
        cosine,
        -sine,
        first_half,
    )
    qkv_grad = jnp.concatenate([turned_back, pair_owned[:, pair_width:]], axis=1).astype(bf16)
    normed_one_part = contract_cols(qkv_grad, qkv_w)
    grad_gain_part = jnp.sum(normed_one_part * hidden_in * scale_one, axis=0)
    grad_qkv = contract_rows(normed_one, qkv_grad).astype(bf16)
    output = residual_own + branch_scale * jnp.sum(mixed_parts.astype(f32), axis=0)

    gain_parts = jnp.stack([grad_gain_part, grad_ffn_part]).reshape(2, n_fsdp, depth)
    gain_chunks = jnp.pad(gain_parts.transpose(1, 0, 2), ((0, 0), (0, 6), (0, 0)))
    one_parts, qkv_got, gain_got, output = send(
        8,
        (("tp",), "a", normed_one_part.astype(bf16).reshape(n_tp, quarter, width)),
        (("fsdp",), "a", grad_qkv.reshape(n_fsdp, depth, -1)),
        (("fsdp",), "a", gain_chunks),
        (("tp",), "g", output.astype(bf16)),
    )
    small = jnp.concatenate(
        [
            jnp.sum(qkv_got.astype(f32), axis=0).astype(bf16),
            jnp.sum(early_got.astype(f32), axis=0).astype(bf16),
        ],
        axis=1,
    )
    gain_sum = jnp.sum(gain_got, axis=0)
    normed_one_grad = jnp.sum(one_parts.astype(f32), axis=0)
    weighted_one = normed_one_grad * gain_one
    input_grad = (
        residual_grad
        + scale_one_own * weighted_one
        - hidden_own
        * scale_one_own**3
        * jnp.mean(weighted_one * hidden_own, axis=-1, keepdims=True)
    )
    small_got, gain_all, input_grad = send(
        9,
        (("ctx",), "a", small.reshape(n_ctx, depth // n_ctx, -1)),
        (("ctx", "tp"), "g", gain_sum),
        (("tp",), "g", input_grad.astype(bf16)),
    )
    (small_all,) = send(10, (("ctx",), "g", jnp.sum(small_got.astype(f32), axis=0).astype(bf16)))
    small_all = small_all.reshape(depth, -1).astype(f32)
    gain_all = jnp.sum(gain_all, axis=0)
    grad_gate, grad_up, grad_down = spread(expert_all, late_all)
    k_end, v_end = q_end + pair_width, q_end + 2 * pair_width
    o_end = v_end + attended.shape[1]
    return (
        output.reshape(rows, width),
        input_grad.reshape(rows, width),
        gain_all[0],
        small_all[:, :q_end],
        small_all[:, q_end:k_end],
        small_all[:, k_end:v_end],
        small_all[:, v_end:o_end],
        gain_all[1],
        small_all[:, o_end : o_end + experts],
        grad_gate,
        grad_up,
        grad_down,
    )


def solution(mesh):
    sizes = dict(mesh.shape)
    return jax.shard_map(
        functools.partial(local, sizes),
        mesh=mesh,
        in_specs=(
            P(("fsdp", "ctx"), None),
            P(("fsdp", "ctx"), None),
            P("fsdp", None),
            P(("fsdp", "ctx"), None),
            P("fsdp"),
            P("fsdp", "tp"),
            P("fsdp", "tp"),
            P("fsdp", "tp"),
            P("fsdp", "tp"),
            P("fsdp"),
            P("fsdp", None),
            P("fsdp", None, "tp"),
            P("fsdp", None, "tp"),
            P("fsdp", None, "tp"),
        ),
        out_specs=(
            P(("fsdp", "ctx"), None),
            P(("fsdp", "ctx"), None),
            P("fsdp"),
            P("fsdp", "tp"),
            P("fsdp", "tp"),
            P("fsdp", "tp"),
            P("fsdp", "tp"),
            P("fsdp"),
            P("fsdp", None),
            P("fsdp", None, "tp"),
            P("fsdp", None, "tp"),
            P("fsdp", None, "tp"),
        ),
        check_vma=False,
    )
```

```python
import functools
import math

import jax
import jax.numpy as jnp
from jax import lax
from jax.experimental import pallas as pl
from jax.experimental.pallas import tpu as pltpu
from jax.sharding import PartitionSpec as P

HEAD_SIZE = 64
CAP = 128
MESH = pl.DeviceIdType.MESH

norm_eps = 1e-06
rope_base = 10000.0
branch_scale = 0.22
highest = lax.Precision.HIGHEST
bf16 = jnp.bfloat16
f32 = jnp.float32


def offset(slot, n):
    return slot // 2 + slot % 2 * (n // 2)


def exchange_kernel(plan, sizes, *refs):
    count = len(plan)
    ins, outs = refs[:count], refs[count : 2 * count]
    send_sem, recv_sem, self_sem = refs[2 * count :]

    def place(axes, step):
        offsets = []
        for axis in reversed(axes):
            offsets.append(step % sizes[axis])
            step //= sizes[axis]
        coords = {}
        for axis, offset in zip(axes, offsets[::-1]):
            here = lax.axis_index(axis)
            coords[axis] = lax.rem(here + offset, sizes[axis]) if offset else here
        return coords

    def flat(axes, coords):
        index = 0
        for axis in axes:
            index = index * sizes[axis] + coords[axis]
        return index

    groups = {}
    for axes, _ in plan:
        for step in range(1, math.prod(sizes[a] for a in axes)):
            full, rest = {}, step
            for axis in reversed(axes):
                full[axis] = rest % sizes[axis]
                rest //= sizes[axis]
            key = tuple(sorted((a, o) for a, o in full.items() if o))
            groups[key] = (axes, step)
    barrier = pltpu.get_barrier_semaphore()
    for axes, step in groups.values():
        pl.semaphore_signal(barrier, inc=1, device_id=place(axes, step), device_id_type=MESH)
    pl.semaphore_wait(barrier, len(groups))

    copies = []
    for at, (axes, mode) in enumerate(plan):
        mine = flat(axes, place(axes, 0))
        for step in range(1, math.prod(sizes[a] for a in axes)):
            if mode == "f":
                peer = place(axes, offset(step, sizes[axes[0]]))
                source, slot = ins[at].at[step], step
            else:
                peer = place(axes, step)
                source = ins[at] if mode == "g" else ins[at].at[flat(axes, peer)]
                slot = mine
            copy = pltpu.make_async_remote_copy(
                src_ref=source,
                dst_ref=outs[at].at[slot],
                send_sem=send_sem.at[at, step],
                recv_sem=recv_sem.at[at, step],
                device_id=peer,
                device_id_type=MESH,
            )
            copy.start()
            copies.append(copy)
        if mode == "f":
            mine = 0
        own = pltpu.make_async_copy(
            ins[at] if mode == "g" else ins[at].at[mine], outs[at].at[mine], self_sem.at[at]
        )
        own.start()
        copies.append(own)
    for copy in copies:
        copy.wait()


def exchange(sizes, collective_id, *items):
    plan = [(axes, mode) for axes, mode, _ in items]
    arrays = [array for _, _, array in items]
    outs = []
    most = 1
    for axes, mode, array in items:
        n = math.prod(sizes[a] for a in axes)
        most = max(most, n)
        shape = (n,) + array.shape if mode == "g" else array.shape
        outs.append(jax.ShapeDtypeStruct(shape, array.dtype))
    count = len(items)
    moved = sum(math.prod(o.shape) * o.dtype.itemsize for o in outs)
    return pl.pallas_call(
        functools.partial(exchange_kernel, plan, sizes),
        out_shape=outs,
        in_specs=[pl.BlockSpec(memory_space=pl.ANY)] * count,
        out_specs=[pl.BlockSpec(memory_space=pl.ANY)] * count,
        scratch_shapes=[
            pltpu.SemaphoreType.DMA((count, most)),
            pltpu.SemaphoreType.DMA((count, most)),
            pltpu.SemaphoreType.DMA((count,)),
        ],
        compiler_params=pltpu.CompilerParams(collective_id=collective_id, has_side_effects=True),
        cost_estimate=pl.CostEstimate(flops=0, bytes_accessed=20 * moved, transcendentals=0),
        name="exchange_%d" % collective_id,
    )(*arrays)


def spread_kernel(pieces_ref, *out_refs):
    for which, out_ref in enumerate(out_refs):
        turned = jnp.swapaxes(pieces_ref[:, which].astype(f32), 0, 1)
        out_ref[...] = turned.reshape(out_ref.shape)


def spread(pieces):
    experts, count, depth, ff = pieces.shape
    block = 64
    outs = pl.pallas_call(
        spread_kernel,
        grid=(depth // block,),
        out_shape=[jax.ShapeDtypeStruct((depth * experts, ff), f32)] * count,
        in_specs=[pl.BlockSpec((experts, count, block, ff), lambda i: (0, 0, i, 0))],
        out_specs=[pl.BlockSpec((block * experts, ff), lambda i: (i, 0))] * count,
        compiler_params=pltpu.CompilerParams(vmem_limit_bytes=40 * 1024 * 1024),
        name="spread",
    )(pieces)
    return [out.reshape(depth, experts, ff) for out in outs]


def attention_kernel(groups, starts_ref, first_ref, queries_ref, pairs_ref, out_ref, probs):
    rows = queries_ref.shape[0]
    total, both = pairs_ref.shape
    pair_width = both // 2
    block = 512
    blocks = [slice(at, at + block) for at in range(0, total, block)]
    places = jnp.concatenate(
        [first_ref[0, 0] + lax.broadcasted_iota(jnp.int32, (rows, 1), 0)] * groups, axis=0
    )
    starts = jnp.concatenate([starts_ref[...]] * groups, axis=0)
    parts = []
    for head in range(pair_width // HEAD_SIZE):
        at = [(head * groups + g) * HEAD_SIZE for g in range(groups)]
        queries = jnp.concatenate([queries_ref[:, a : a + HEAD_SIZE] for a in at], axis=0)
        own = slice(head * HEAD_SIZE, (head + 1) * HEAD_SIZE)
        own_values = slice(pair_width + own.start, pair_width + own.stop)
        top = jnp.full((rows * groups, 1), -1e30, f32)
        for part in blocks:
            key_rows = part.start + lax.broadcasted_iota(jnp.int32, (1, block), 1)
            allowed = (key_rows >= starts) & (key_rows <= places)
            scores = contract_cols(queries, pairs_ref[part, own]) * HEAD_SIZE ** (-0.5)
            scores = jnp.where(allowed, scores, -1e30)
            probs[:, part] = scores
            top = jnp.maximum(top, jnp.max(scores, axis=1, keepdims=True))
        count = jnp.zeros((rows * groups, 1), f32)
        for part in blocks:
            raised = jnp.exp(probs[:, part] - top)
            probs[:, part] = raised
            count += jnp.sum(raised, axis=1, keepdims=True)
        share = 1.0 / count
        attended = jnp.zeros((rows * groups, HEAD_SIZE), f32)
        for part in blocks:
            attended += mm((probs[:, part] * share).astype(bf16), pairs_ref[part, own_values])
        parts += [attended[g * rows : (g + 1) * rows] for g in range(groups)]
    out_ref[...] = jnp.concatenate(parts, axis=1).astype(bf16)


def attention(starts, first_row, queries, pairs, pair_width):
    rows, q_width = queries.shape
    total = pairs.shape[0]
    groups = q_width // pair_width
    vmem = pl.BlockSpec(memory_space=pltpu.VMEM)
    return pl.pallas_call(
        functools.partial(attention_kernel, groups),
        out_shape=jax.ShapeDtypeStruct((rows, q_width), bf16),
        in_specs=[vmem, pl.BlockSpec(memory_space=pltpu.SMEM), vmem, vmem],
        out_specs=vmem,
        scratch_shapes=[pltpu.VMEM((rows * groups, total), f32)],
        compiler_params=pltpu.CompilerParams(vmem_limit_bytes=40 * 1024 * 1024),
        cost_estimate=pl.CostEstimate(
            flops=4 * rows * q_width * total, bytes_accessed=4 << 20, transcendentals=rows * total * 4
        ),
        name="attention",
    )(starts.reshape(rows, 1), first_row.reshape(1, 1), queries, pairs)


def attention_back_kernel(groups, starts_ref, first_ref, queries_ref, grads_ref, pairs_ref, query_out, pair_out, probs, back):
    rows = queries_ref.shape[0]
    total, both = pairs_ref.shape
    pair_width = both // 2
    block = 512
    blocks = [slice(at, at + block) for at in range(0, total, block)]
    scale = HEAD_SIZE ** (-0.5)
    places = jnp.concatenate([first_ref[0, 0] + lax.broadcasted_iota(jnp.int32, (rows, 1), 0)] * groups, axis=0)
    starts = jnp.concatenate([starts_ref[...]] * groups, axis=0)
    query_parts, key_parts, value_parts = [], [], []
    for head in range(pair_width // HEAD_SIZE):

        def heads_of(ref):
            at = [(head * groups + g) * HEAD_SIZE for g in range(groups)]
            return jnp.concatenate([ref[:, a : a + HEAD_SIZE] for a in at], axis=0)

        queries, grads = heads_of(queries_ref), heads_of(grads_ref)
        own = slice(head * HEAD_SIZE, (head + 1) * HEAD_SIZE)
        own_values = slice(pair_width + own.start, pair_width + own.stop)
        top = jnp.full((rows * groups, 1), -1e30, f32)
        for part in blocks:
            key_rows = part.start + lax.broadcasted_iota(jnp.int32, (1, block), 1)
            allowed = (key_rows >= starts) & (key_rows <= places)
            scores = contract_cols(queries, pairs_ref[part, own]) * scale
            scores = jnp.where(allowed, scores, -1e30)
            probs[:, part] = scores
            top = jnp.maximum(top, jnp.max(scores, axis=1, keepdims=True))
        count = jnp.zeros((rows * groups, 1), f32)
        for part in blocks:
            raised = jnp.exp(probs[:, part] - top)
            probs[:, part] = raised
            count += jnp.sum(raised, axis=1, keepdims=True)
        share = 1.0 / count
        mean = jnp.zeros((rows * groups, 1), f32)
        for part in blocks:
            weights = probs[:, part] * share
            probs[:, part] = weights
            prob_grad = contract_cols(grads, pairs_ref[part, own_values])
            back[:, part] = prob_grad
            mean += jnp.sum(weights * prob_grad, axis=1, keepdims=True)
        query_grad = jnp.zeros((rows * groups, HEAD_SIZE), f32)
        keys_here, values_here = [], []
        for part in blocks:
            weights = probs[:, part]
            score_grad = (weights * (back[:, part] - mean)).astype(bf16)
            query_grad += mm(score_grad, pairs_ref[part, own])
            keys_here.append((contract_rows(score_grad, queries) * scale).astype(bf16))
            values_here.append(contract_rows(weights.astype(bf16), grads).astype(bf16))
        query_grad = query_grad * scale
        query_parts += [query_grad[g * rows : (g + 1) * rows] for g in range(groups)]
        key_parts.append(jnp.concatenate(keys_here, axis=0))
        value_parts.append(jnp.concatenate(values_here, axis=0))
    query_out[...] = jnp.concatenate(query_parts, axis=1)
    pair_out[...] = jnp.concatenate(key_parts + value_parts, axis=1)


def attention_back(starts, first_row, queries, grads, pairs, pair_width):
    rows, q_width = queries.shape
    total = pairs.shape[0]
    groups = q_width // pair_width
    vmem = pl.BlockSpec(memory_space=pltpu.VMEM)
    return pl.pallas_call(
        functools.partial(attention_back_kernel, groups),
        out_shape=[
            jax.ShapeDtypeStruct((rows, q_width), f32),
            jax.ShapeDtypeStruct((total, 2 * pair_width), bf16),
        ],
        in_specs=[vmem, pl.BlockSpec(memory_space=pltpu.SMEM), vmem, vmem, vmem],
        out_specs=[vmem, vmem],
        scratch_shapes=[pltpu.VMEM((rows * groups, total), f32)] * 2,
        compiler_params=pltpu.CompilerParams(vmem_limit_bytes=48 * 1024 * 1024),
        cost_estimate=pl.CostEstimate(
            flops=10 * rows * q_width * total, bytes_accessed=8 << 20, transcendentals=rows * total * 4
        ),
        name="attention_back",
    )(starts.reshape(rows, 1), first_row.reshape(1, 1), queries, grads, pairs)


def expert_kernel(
    n,
    n_fsdp,
    part,
    rows_ref,
    probs_ref,
    grads_ref,
    w_ref,
    norm_got,
    mixed_got,
    gate_got,
    wgrad_ref,
    wgrad_buf,
    wgrad_got,
    norm_buf,
    probs_buf,
    both_buf,
    weighted_buf,
    back_buf,
    mixed_buf,
    gate_buf,
    send_sems,
    recv_sems,
    wgrad_send,
    wgrad_recv,
):
    me, fsdp_at = lax.axis_index("ctx"), lax.axis_index("fsdp")
    hidden = w_ref.shape[1] // 3

    def chunk(ref, k):
        return ref.at[pl.ds(pl.multiple_of(k * CAP, CAP), CAP)]

    def copy(which, k, source, target, place):
        return pltpu.make_async_remote_copy(
            src_ref=source,
            dst_ref=target,
            send_sem=send_sems.at[which, k],
            recv_sem=recv_sems.at[which, k],
            device_id={"ctx": lax.rem(place, n)},
            device_id_type=MESH,
        )

    def out_copies(k):
        place = me + offset(k, n)
        return (
            copy(0, k, chunk(rows_ref, k), chunk(norm_buf, k), place),
            copy(1, k, probs_ref.at[k], probs_buf.at[k], place),
        )

    def back_copies(k):
        place = me + n - offset(k, n)
        return (
            copy(2, k, chunk(back_buf, k), chunk(norm_got, k), place),
            copy(3, k, gate_buf.at[k], gate_got.at[k], place),
            copy(4, k, chunk(mixed_buf, k), chunk(mixed_got, k), place),
        )

    barrier = pltpu.get_barrier_semaphore()
    for k in range(1, n):
        pl.semaphore_signal(
            barrier, inc=1, device_id={"ctx": lax.rem(me + k, n)}, device_id_type=MESH
        )
    for k in range(1, n_fsdp):
        pl.semaphore_signal(
            barrier,
            inc=1,
            device_id={"fsdp": lax.rem(fsdp_at + k, n_fsdp)},
            device_id_type=MESH,
        )
    pl.semaphore_wait(barrier, n - 1 + n_fsdp - 1)
    for k in range(1, 4):
        for item in out_copies(k):
            item.start()
    norm_buf[:CAP] = rows_ref[:CAP]
    probs_buf[0] = probs_ref[0]
    same = lax.broadcasted_iota(jnp.int32, (CAP, CAP), 0) == lax.broadcasted_iota(
        jnp.int32, (CAP, CAP), 1
    )

    def pair(j, carry):
        @pl.when(j < n // 2 - 2)
        def _():
            for k in (2 * j + 4, 2 * j + 5):
                for item in out_copies(k):
                    item.start()

        for k in (2 * j, 2 * j + 1):

            @pl.when(k > 0)
            def _():
                for item in out_copies(k):
                    item.wait_recv()

        here = pl.ds(pl.multiple_of(j * 2 * CAP, 2 * CAP), 2 * CAP)
        gate_up = mm(norm_buf[here, :], w_ref[:, : 2 * hidden])
        down_back = mm(grads_ref[here, :], w_ref[:, 2 * hidden :])
        probs = jnp.concatenate(
            [
                jnp.sum(jnp.where(same, probs_buf[k][:1, :], 0.0), axis=1, keepdims=True)
                for k in (2 * j, 2 * j + 1)
            ],
            axis=0,
        )
        gate_pre, up_pre = gate_up[:, :hidden], gate_up[:, hidden:]
        sig = jax.nn.sigmoid(gate_pre)
        silu = gate_pre * sig
        activation = silu * up_pre
        gate_grad = branch_scale * jnp.sum(activation * down_back, axis=1, keepdims=True)
        act_grad = (branch_scale * probs) * down_back
        both_buf[here, :hidden] = (
            act_grad * up_pre * sig * (1.0 + gate_pre * (1.0 - sig))
        ).astype(bf16)
        both_buf[here, hidden:] = (act_grad * silu).astype(bf16)
        weighted_buf[here, :] = (probs * activation).astype(bf16)
        back_buf[here, :] = contract_cols(both_buf[here, :], w_ref[:, : 2 * hidden]).astype(bf16)
        for i in range(2):
            line = jnp.sum(
                jnp.where(same, gate_grad[i * CAP : (i + 1) * CAP], 0.0), axis=0, keepdims=True
            )
            gate_buf[2 * j + i] = jnp.broadcast_to(line, (8, CAP))
        mixed_buf[here, :] = contract_cols(weighted_buf[here, :], w_ref[:, 2 * hidden :]).astype(
            bf16
        )
        for k in (2 * j, 2 * j + 1):

            @pl.when(k > 0)
            def _():
                for item in back_copies(k):
                    item.start()

        return carry

    lax.fori_loop(0, n // 2, pair, 0)
    norm_got[:CAP] = back_buf[:CAP]
    mixed_got[:CAP] = mixed_buf[:CAP]
    gate_got[0] = gate_buf[0]

    slim = wgrad_ref.shape[1]

    def wgrad_copy(k):
        return pltpu.make_async_remote_copy(
            src_ref=wgrad_buf.at[k],
            dst_ref=wgrad_got.at[k],
            send_sem=wgrad_send.at[k],
            recv_sem=wgrad_recv.at[k],
            device_id={"fsdp": lax.rem(fsdp_at + k, n_fsdp)},
            device_id_type=MESH,
        )

    def weight_grads(j, carry):
        k = lax.rem(j + 1, n_fsdp)
        here = pl.ds(pl.multiple_of(lax.rem(fsdp_at + k, n_fsdp) * part, part), part)
        gate_up = contract_rows(norm_buf[:, here], both_buf[...]).astype(bf16)
        down = (contract_rows(grads_ref[:, here], weighted_buf[...]) * branch_scale).astype(bf16)
        for piece in range(hidden // slim):
            for which in range(3):
                row = (piece * 3 + which) * part
                if which < 2:
                    start = which * hidden + piece * slim
                    wgrad_buf[k, row : row + part, :] = gate_up[:, start : start + slim]
                else:
                    wgrad_buf[k, row : row + part, :] = down[:, piece * slim : (piece + 1) * slim]

        @pl.when(k > 0)
        def _():
            wgrad_copy(k).start()

        return carry

    lax.fori_loop(0, n_fsdp, weight_grads, 0)
    for k in range(1, n_fsdp):
        wgrad_copy(k).wait()

    def summed(j, carry):
        at = pl.ds(pl.multiple_of(j * part, part), part)
        total = wgrad_buf[0, at, :].astype(f32)
        for k in range(1, n_fsdp):
            total += wgrad_got[k, at, :].astype(f32)
        wgrad_ref[at, :] = total.astype(bf16)
        return carry

    lax.fori_loop(0, wgrad_buf.shape[1] // part, summed, 0)
    for k in range(1, n):
        for item in out_copies(k):
            item.wait_send()
        for item in back_copies(k):
            item.wait()


def expert_of_place(sizes, rows_sent, probs_sent, grad_rows, expert_w):
    n = sizes["ctx"]
    total, width = rows_sent.shape
    n_fsdp, n_tp = sizes["fsdp"], sizes["tp"]
    hidden, part = expert_w.shape[1] // 3, width // n_fsdp
    owned = (n_tp * 3 * part, hidden // n_tp)
    like = jax.ShapeDtypeStruct
    vmem = pl.BlockSpec(memory_space=pltpu.VMEM)
    return pl.pallas_call(
        functools.partial(expert_kernel, n, n_fsdp, part),
        out_shape=[
            like((total, width), bf16),
            like((total, width), bf16),
            like(probs_sent.shape, f32),
            like(owned, bf16),
        ],
        in_specs=[vmem] * 4,
        out_specs=[vmem] * 4,
        scratch_shapes=[
            pltpu.VMEM((n_fsdp,) + owned, bf16),
            pltpu.VMEM((n_fsdp,) + owned, bf16),
            pltpu.VMEM((total, width), bf16),
            pltpu.VMEM(probs_sent.shape, f32),
            pltpu.VMEM((total, 2 * hidden), bf16),
            pltpu.VMEM((total, hidden), bf16),
            pltpu.VMEM((total, width), bf16),
            pltpu.VMEM((total, width), bf16),
            pltpu.VMEM(probs_sent.shape, f32),
            pltpu.SemaphoreType.DMA((5, n)),
            pltpu.SemaphoreType.DMA((5, n)),
            pltpu.SemaphoreType.DMA((n_fsdp,)),
            pltpu.SemaphoreType.DMA((n_fsdp,)),
        ],
        compiler_params=pltpu.CompilerParams(
            collective_id=3, has_side_effects=True, vmem_limit_bytes=48 * 1024 * 1024
        ),
        cost_estimate=pl.CostEstimate(
            flops=6 * 2 * total * width * hidden * 3, bytes_accessed=100 << 20, transcendentals=0
        ),
        name="expert_of_place",
    )(rows_sent, probs_sent, grad_rows, expert_w)


def rope_tables(places, columns):
    column = jnp.arange(columns, dtype=jnp.int32)
    steps = (column % (HEAD_SIZE // 2)).astype(f32)
    frequencies = jnp.exp(steps * (-2.0 * math.log(rope_base) / HEAD_SIZE))
    angles = places.astype(f32)[:, None] * frequencies[None, :]
    first = (column % HEAD_SIZE < HEAD_SIZE // 2)[None, :]
    sine = jnp.sin(angles)
    return jnp.cos(angles), jnp.where(first, -sine, sine), first


def turn(values, cosine, sine, first):
    half = HEAD_SIZE // 2
    other = jnp.where(first, jnp.roll(values, -half, axis=1), jnp.roll(values, half, axis=1))
    return values * cosine + other * sine


def contract_rows(left, right, precision=None):
    return lax.dot_general(
        left, right, (((0,), (0,)), ((), ())), precision=precision, preferred_element_type=f32
    )


def contract_cols(left, right, precision=None):
    return lax.dot_general(
        left, right, (((1,), (1,)), ((), ())), precision=precision, preferred_element_type=f32
    )


def mm(left, right):
    return jnp.dot(left, right, preferred_element_type=f32)


def local(
    sizes,
    inputs,
    cotangent,
    lengths,
    expert_ids,
    attn_gain,
    w_query,
    key_weight,
    value_weight,
    w_output,
    ffn_gain,
    w_router,
    w_gate,
    w_up,
    w_down,
):
    rows, width = inputs.shape
    n_fsdp, n_ctx, n_tp = sizes["fsdp"], sizes["ctx"], sizes["tp"]
    experts = w_router.shape[1]
    depth, _, ff = w_gate.shape
    per_ctx = experts // n_ctx
    send = functools.partial(exchange, sizes)
    ctx_at, tp_at = lax.axis_index("ctx"), lax.axis_index("tp")

    chosen = jnp.any(
        expert_ids[:, :, None] == jnp.arange(experts, dtype=jnp.int32)[None, None, :], axis=1
    )
    offsets = [offset(slot, n_ctx) for slot in range(n_ctx)]
    ctx_order = lax.rem(ctx_at + jnp.array(offsets, dtype=jnp.int32), n_ctx)
    mine = ctx_order * per_ctx + tp_at
    chosen_mine = jnp.any(expert_ids[None, :, :] == mine[:, None, None], axis=2)
    earlier = jnp.arange(rows)[:, None] < jnp.arange(rows)[None, :]
    rank = mm(chosen_mine.astype(bf16), earlier.astype(bf16))
    slots = jnp.arange(CAP, dtype=f32)
    picks = (chosen_mine[:, None, :] & (rank[:, None, :] == slots[None, :, None])).astype(bf16)
    picks_flat = picks.reshape(n_ctx * CAP, rows)

    first = ctx_at * per_ctx
    own_slices = jnp.stack(
        [
            lax.dynamic_slice_in_dim(w, first, per_ctx, 1).transpose(1, 0, 2)
            for w in (w_gate, w_up, w_down)
        ],
        axis=1,
    )
    gains = jnp.concatenate(
        [
            attn_gain.reshape(-1, 128),
            ffn_gain.reshape(-1, 128),
            jnp.zeros((16 - 2 * depth // 128, 128), bf16),
        ],
        axis=0,
    )
    router_pad = jnp.pad(w_router, ((0, 0), (0, 128 - experts)))
    grads_sent = mm(picks_flat, cotangent).astype(bf16).reshape(n_ctx, CAP, width)
    qkv_w, gains_all, router_all, expert_slices, grad_rows = send(
        0,
        (("fsdp",), "g", jnp.concatenate([w_query, key_weight, value_weight], axis=1)),
        (("fsdp",), "g", gains),
        (("fsdp",), "g", router_pad),
        (("tp",), "a", own_slices),
        (("ctx",), "f", grads_sent),
    )
    qkv_w = qkv_w.reshape(width, -1)
    lines = depth // 128
    gain_one = gains_all[:, :lines].reshape(width).astype(f32)
    gain_two = gains_all[:, lines : 2 * lines].reshape(width).astype(f32)
    router_w = router_all.reshape(width, 128)[:, :experts]

    grad_rows = grad_rows.reshape(n_ctx * CAP, width)

    expert_cat = expert_slices.transpose(2, 1, 0, 3).reshape(depth, 3 * n_tp * ff)
    expert_w = lax.all_gather(expert_cat, "fsdp", axis=0, tiled=True)

    lengths_row = lengths[0]
    query_rows = ctx_at * rows + jnp.arange(rows, dtype=jnp.int32)
    seq_ends = jnp.cumsum(lengths_row)
    passed = (query_rows[:, None] >= seq_ends[None, :]).astype(jnp.int32)
    starts = jnp.sum(passed * lengths_row[None, :], axis=1)
    q_end, pair_width = w_query.shape[1], key_weight.shape[1]
    turned = q_end + pair_width
    cosine, sine, first_half = rope_tables(query_rows - starts, turned)
    hidden_in = inputs.astype(f32)
    scale_one = lax.rsqrt(jnp.mean(hidden_in * hidden_in, axis=-1, keepdims=True) + norm_eps)
    normed_one = (hidden_in * scale_one * gain_one).astype(bf16)
    qkv = mm(normed_one, qkv_w)
    queries_keys = turn(qkv[:, :turned], cosine, sine, first_half).astype(bf16)
    queries = queries_keys[:, :q_end]
    pairs_local = jnp.concatenate(
        [queries_keys[:, q_end:], qkv[:, turned:].astype(bf16)], axis=1
    )
    pairs_all, output_w = send(1, (("ctx",), "g", pairs_local), (("fsdp",), "g", w_output))
    output_w = output_w.reshape(width, -1)
    total_rows = n_ctx * rows
    pairs_all = pairs_all.reshape(total_rows, 2 * pair_width)
    attended = attention(starts, ctx_at * rows, queries, pairs_all, pair_width)
    quarter = rows // n_tp

    def quarter_of(array):
        return lax.dynamic_slice_in_dim(array, tp_at * quarter, quarter, 0)

    attn_part = contract_cols(attended, output_w).astype(bf16)
    (attn_parts,) = send(2, (("tp",), "a", attn_part.reshape(n_tp, quarter, width)))
    hidden_own, scale_one_own = quarter_of(hidden_in), quarter_of(scale_one)
    residual_own = hidden_own + branch_scale * jnp.sum(attn_parts.astype(f32), axis=0)

    scale_two_own = lax.rsqrt(jnp.mean(residual_own * residual_own, axis=-1, keepdims=True) + norm_eps)
    normed_two_own = (residual_own * scale_two_own * gain_two).astype(bf16)
    (normed_two,) = send(11, (("tp",), "g", normed_two_own))
    normed_two = normed_two.reshape(rows, width)
    logits = mm(normed_two, router_w)
    route_masked = jnp.where(chosen, logits, -1e30)
    route_exp = jnp.exp(route_masked - jnp.max(route_masked, axis=-1, keepdims=True))
    gate_probs = route_exp / jnp.sum(route_exp, axis=-1, keepdims=True)
    probs_mine = lax.dynamic_index_in_dim(
        gate_probs.T.reshape(n_ctx, per_ctx, rows), tp_at, 1, keepdims=False
    )
    probs_mine = jnp.take(probs_mine, ctx_order, axis=0)
    probs_sent = jnp.sum(picks.astype(f32) * probs_mine[:, None, :], axis=2)
    rows_sent = mm(picks_flat, normed_two).astype(bf16)
    probs_sent = jnp.broadcast_to(probs_sent[:, None, :], (n_ctx, 8, CAP))
    norm_grad_got, mixed_got, gate_grad_got, expert_grad = expert_of_place(
        sizes, rows_sent, probs_sent, grad_rows, expert_w
    )

    norm_grad_part = contract_rows(picks_flat, norm_grad_got)
    gate_grad_part = jnp.sum(picks.astype(f32) * gate_grad_got[:, 0, :, None], axis=1)
    norm_grad_parts, gate_grad_parts, pieces = send(
        5,
        (("tp",), "a", norm_grad_part.astype(bf16).reshape(n_tp, quarter, width)),
        (("tp",), "g", gate_grad_part),
        (("tp",), "a", expert_grad.reshape(n_tp, 3, depth, ff)),
    )

    pairs = [[2 * i, 2 * i + 1] for i in range(n_ctx // 2)]
    rings = [list(range(start, n_ctx, 2)) for start in range(2)]
    pieces = lax.all_gather(pieces, "ctx", axis=0, tiled=True, axis_index_groups=pairs)

    slot_of = jnp.array([offsets.index(k) for k in range(n_ctx)], dtype=jnp.int32)
    back_order = slot_of[lax.rem(jnp.arange(n_ctx, dtype=jnp.int32) + n_ctx - ctx_at, n_ctx)]
    gate_grads = jnp.take(gate_grad_parts, back_order, axis=1)
    gate_grads = gate_grads.transpose(2, 1, 0).reshape(rows, experts)
    route_grad = gate_probs * (
        gate_grads - jnp.sum(gate_probs * gate_grads, axis=-1, keepdims=True)
    )
    grad_router = contract_rows(normed_two.astype(f32), route_grad, highest)
    router_back = contract_cols(quarter_of(route_grad), router_w.astype(f32), highest)
    normed_grad = jnp.sum(norm_grad_parts.astype(f32), axis=0) + router_back
    weighted_two = normed_grad * gain_two
    grad_ffn_part = jnp.sum(normed_grad * residual_own * scale_two_own, axis=0)
    residual_grad = (
        quarter_of(cotangent).astype(f32)
        + scale_two_own * weighted_two
        - residual_own
        * scale_two_own**3
        * jnp.mean(weighted_two * residual_own, axis=-1, keepdims=True)
    )
    (attn_in,) = send(6, (("tp",), "g", (branch_scale * residual_grad).astype(bf16)))
    attn_in = attn_in.reshape(rows, width)

    side = jnp.pad(grad_router, ((0, 0), (0, 128 - experts)))
    early = jnp.concatenate([contract_rows(attn_in, attended), side], axis=1).astype(bf16)
    mixed_part = contract_rows(picks_flat, mixed_got).astype(bf16)
    attended_grad = mm(attn_in, output_w).astype(bf16)

    query_grad_rot, pair_grads = attention_back(
        starts, ctx_at * rows, queries, attended_grad, pairs_all, pair_width
    )
    pieces, pair_grads = lax.optimization_barrier((pieces, pair_grads))
    expert_all = lax.all_gather(pieces, "ctx", axis=0, tiled=True, axis_index_groups=rings)
    pair_got, mixed_parts, early_got = send(
        7,
        (("ctx",), "a", pair_grads.reshape(n_ctx, rows, 2 * pair_width)),
        (("tp",), "a", mixed_part.reshape(n_tp, quarter, width)),
        (("fsdp",), "a", early.reshape(n_fsdp, depth, -1)),
    )
    pair_owned = jnp.sum(pair_got.astype(f32), axis=0)
    turned_back = turn(
        jnp.concatenate([query_grad_rot, pair_owned[:, :pair_width]], axis=1),
        cosine,
        -sine,
        first_half,
    )
    qkv_grad = jnp.concatenate([turned_back, pair_owned[:, pair_width:]], axis=1).astype(bf16)
    normed_one_part = contract_cols(qkv_grad, qkv_w)
    grad_gain_part = jnp.sum(normed_one_part * hidden_in * scale_one, axis=0)
    grad_qkv = contract_rows(normed_one, qkv_grad).astype(bf16)
    output = residual_own + branch_scale * jnp.sum(mixed_parts.astype(f32), axis=0)

    gain_parts = jnp.stack([grad_gain_part, grad_ffn_part]).reshape(2, n_fsdp, depth)
    gain_chunks = jnp.pad(gain_parts.transpose(1, 0, 2), ((0, 0), (0, 6), (0, 0)))
    one_parts, qkv_got, gain_got, output = send(
        8,
        (("tp",), "a", normed_one_part.astype(bf16).reshape(n_tp, quarter, width)),
        (("fsdp",), "a", grad_qkv.reshape(n_fsdp, depth, -1)),
        (("fsdp",), "a", gain_chunks),
        (("tp",), "g", output.astype(bf16)),
    )
    small = jnp.concatenate(
        [
            jnp.sum(qkv_got.astype(f32), axis=0).astype(bf16),
            jnp.sum(early_got.astype(f32), axis=0).astype(bf16),
        ],
        axis=1,
    )
    gain_sum = jnp.sum(gain_got, axis=0)
    normed_one_grad = jnp.sum(one_parts.astype(f32), axis=0)
    weighted_one = normed_one_grad * gain_one
    input_grad = (
        residual_grad
        + scale_one_own * weighted_one
        - hidden_own
        * scale_one_own**3
        * jnp.mean(weighted_one * hidden_own, axis=-1, keepdims=True)
    )
    small_got, gain_all, input_grad = send(
        9,
        (("ctx",), "a", small.reshape(n_ctx, depth // n_ctx, -1)),
        (("ctx", "tp"), "g", gain_sum),
        (("tp",), "g", input_grad.astype(bf16)),
    )
    (small_all,) = send(10, (("ctx",), "g", jnp.sum(small_got.astype(f32), axis=0).astype(bf16)))
    small_all = small_all.reshape(depth, -1).astype(f32)
    gain_all = jnp.sum(gain_all, axis=0)
    grad_gate, grad_up, grad_down = spread(expert_all)
    k_end, v_end = q_end + pair_width, q_end + 2 * pair_width
    o_end = v_end + attended.shape[1]
    return (
        output.reshape(rows, width),
        input_grad.reshape(rows, width),
        gain_all[0],
        small_all[:, :q_end],
        small_all[:, q_end:k_end],
        small_all[:, k_end:v_end],
        small_all[:, v_end:o_end],
        gain_all[1],
        small_all[:, o_end : o_end + experts],
        grad_gate,
        grad_up,
        grad_down,
    )


def solution(mesh):
    sizes = dict(mesh.shape)
    return jax.shard_map(
        functools.partial(local, sizes),
        mesh=mesh,
        in_specs=(
            P(("fsdp", "ctx"), None),
            P(("fsdp", "ctx"), None),
            P("fsdp", None),
            P(("fsdp", "ctx"), None),
            P("fsdp"),
            P("fsdp", "tp"),
            P("fsdp", "tp"),
            P("fsdp", "tp"),
            P("fsdp", "tp"),
            P("fsdp"),
            P("fsdp", None),
            P("fsdp", None, "tp"),
            P("fsdp", None, "tp"),
            P("fsdp", None, "tp"),
        ),
        out_specs=(
            P(("fsdp", "ctx"), None),
            P(("fsdp", "ctx"), None),
            P("fsdp"),
            P("fsdp", "tp"),
            P("fsdp", "tp"),
            P("fsdp", "tp"),
            P("fsdp", "tp"),
            P("fsdp"),
            P("fsdp", None),
            P("fsdp", None, "tp"),
            P("fsdp", None, "tp"),
            P("fsdp", None, "tp"),
        ),
        check_vma=False,
    )
```

```python
import functools
import math

import jax
import jax.numpy as jnp
from jax import lax
from jax.experimental import pallas as pl
from jax.experimental.pallas import tpu as pltpu
from jax.sharding import PartitionSpec as P

HEAD_SIZE = 64
CAP = 128
MESH = pl.DeviceIdType.MESH

norm_eps = 1e-06
rope_base = 10000.0
branch_scale = 0.22
highest = lax.Precision.HIGHEST
bf16 = jnp.bfloat16
f32 = jnp.float32


def offset(slot, n):
    return slot // 2 + slot % 2 * (n // 2)


def exchange_kernel(plan, sizes, *refs):
    count = len(plan)
    ins, outs = refs[:count], refs[count : 2 * count]
    send_sem, recv_sem, self_sem = refs[2 * count :]

    def place(axes, step):
        offsets = []
        for axis in reversed(axes):
            offsets.append(step % sizes[axis])
            step //= sizes[axis]
        coords = {}
        for axis, offset in zip(axes, offsets[::-1]):
            here = lax.axis_index(axis)
            coords[axis] = lax.rem(here + offset, sizes[axis]) if offset else here
        return coords

    def flat(axes, coords):
        index = 0
        for axis in axes:
            index = index * sizes[axis] + coords[axis]
        return index

    groups = {}
    for axes, _ in plan:
        for step in range(1, math.prod(sizes[a] for a in axes)):
            full, rest = {}, step
            for axis in reversed(axes):
                full[axis] = rest % sizes[axis]
                rest //= sizes[axis]
            key = tuple(sorted((a, o) for a, o in full.items() if o))
            groups[key] = (axes, step)
    barrier = pltpu.get_barrier_semaphore()
    for axes, step in groups.values():
        pl.semaphore_signal(barrier, inc=1, device_id=place(axes, step), device_id_type=MESH)
    pl.semaphore_wait(barrier, len(groups))

    copies = []
    for at, (axes, mode) in enumerate(plan):
        mine = flat(axes, place(axes, 0))
        for step in range(1, math.prod(sizes[a] for a in axes)):
            if mode == "f":
                peer = place(axes, offset(step, sizes[axes[0]]))
                source, slot = ins[at].at[step], step
            else:
                peer = place(axes, step)
                source = ins[at] if mode == "g" else ins[at].at[flat(axes, peer)]
                slot = mine
            copy = pltpu.make_async_remote_copy(
                src_ref=source,
                dst_ref=outs[at].at[slot],
                send_sem=send_sem.at[at, step],
                recv_sem=recv_sem.at[at, step],
                device_id=peer,
                device_id_type=MESH,
            )
            copy.start()
            copies.append(copy)
        if mode == "f":
            mine = 0
        own = pltpu.make_async_copy(
            ins[at] if mode == "g" else ins[at].at[mine], outs[at].at[mine], self_sem.at[at]
        )
        own.start()
        copies.append(own)
    for copy in copies:
        copy.wait()


def exchange(sizes, collective_id, *items):
    plan = [(axes, mode) for axes, mode, _ in items]
    arrays = [array for _, _, array in items]
    outs = []
    most = 1
    for axes, mode, array in items:
        n = math.prod(sizes[a] for a in axes)
        most = max(most, n)
        shape = (n,) + array.shape if mode == "g" else array.shape
        outs.append(jax.ShapeDtypeStruct(shape, array.dtype))
    count = len(items)
    moved = sum(math.prod(o.shape) * o.dtype.itemsize for o in outs)
    return pl.pallas_call(
        functools.partial(exchange_kernel, plan, sizes),
        out_shape=outs,
        in_specs=[pl.BlockSpec(memory_space=pl.ANY)] * count,
        out_specs=[pl.BlockSpec(memory_space=pl.ANY)] * count,
        scratch_shapes=[
            pltpu.SemaphoreType.DMA((count, most)),
            pltpu.SemaphoreType.DMA((count, most)),
            pltpu.SemaphoreType.DMA((count,)),
        ],
        compiler_params=pltpu.CompilerParams(collective_id=collective_id, has_side_effects=True),
        cost_estimate=pl.CostEstimate(flops=0, bytes_accessed=20 * moved, transcendentals=0),
        name="exchange_%d" % collective_id,
    )(*arrays)


def spread_kernel(pieces_ref, *out_refs):
    for which, out_ref in enumerate(out_refs):
        turned = jnp.swapaxes(pieces_ref[:, which].astype(f32), 0, 1)
        out_ref[...] = turned.reshape(out_ref.shape)


def spread(pieces):
    experts, count, depth, ff = pieces.shape
    block = 64
    outs = pl.pallas_call(
        spread_kernel,
        grid=(depth // block,),
        out_shape=[jax.ShapeDtypeStruct((depth * experts, ff), f32)] * count,
        in_specs=[pl.BlockSpec((experts, count, block, ff), lambda i: (0, 0, i, 0))],
        out_specs=[pl.BlockSpec((block * experts, ff), lambda i: (i, 0))] * count,
        compiler_params=pltpu.CompilerParams(vmem_limit_bytes=40 * 1024 * 1024),
        name="spread",
    )(pieces)
    return [out.reshape(depth, experts, ff) for out in outs]


def attention_kernel(groups, starts_ref, first_ref, queries_ref, pairs_ref, out_ref, probs):
    rows = queries_ref.shape[0]
    total, both = pairs_ref.shape
    pair_width = both // 2
    block = 512
    blocks = [slice(at, at + block) for at in range(0, total, block)]
    places = jnp.concatenate(
        [first_ref[0, 0] + lax.broadcasted_iota(jnp.int32, (rows, 1), 0)] * groups, axis=0
    )
    starts = jnp.concatenate([starts_ref[...]] * groups, axis=0)
    parts = []
    for head in range(pair_width // HEAD_SIZE):
        at = [(head * groups + g) * HEAD_SIZE for g in range(groups)]
        queries = jnp.concatenate([queries_ref[:, a : a + HEAD_SIZE] for a in at], axis=0)
        own = slice(head * HEAD_SIZE, (head + 1) * HEAD_SIZE)
        own_values = slice(pair_width + own.start, pair_width + own.stop)
        top = jnp.full((rows * groups, 1), -1e30, f32)
        for part in blocks:
            key_rows = part.start + lax.broadcasted_iota(jnp.int32, (1, block), 1)
            allowed = (key_rows >= starts) & (key_rows <= places)
            scores = contract_cols(queries, pairs_ref[part, own]) * HEAD_SIZE ** (-0.5)
            scores = jnp.where(allowed, scores, -1e30)
            probs[:, part] = scores
            top = jnp.maximum(top, jnp.max(scores, axis=1, keepdims=True))
        count = jnp.zeros((rows * groups, 1), f32)
        for part in blocks:
            raised = jnp.exp(probs[:, part] - top)
            probs[:, part] = raised
            count += jnp.sum(raised, axis=1, keepdims=True)
        share = 1.0 / count
        attended = jnp.zeros((rows * groups, HEAD_SIZE), f32)
        for part in blocks:
            attended += mm((probs[:, part] * share).astype(bf16), pairs_ref[part, own_values])
        parts += [attended[g * rows : (g + 1) * rows] for g in range(groups)]
    out_ref[...] = jnp.concatenate(parts, axis=1).astype(bf16)


def attention(starts, first_row, queries, pairs, pair_width):
    rows, q_width = queries.shape
    total = pairs.shape[0]
    groups = q_width // pair_width
    vmem = pl.BlockSpec(memory_space=pltpu.VMEM)
    return pl.pallas_call(
        functools.partial(attention_kernel, groups),
        out_shape=jax.ShapeDtypeStruct((rows, q_width), bf16),
        in_specs=[vmem, pl.BlockSpec(memory_space=pltpu.SMEM), vmem, vmem],
        out_specs=vmem,
        scratch_shapes=[pltpu.VMEM((rows * groups, total), f32)],
        compiler_params=pltpu.CompilerParams(vmem_limit_bytes=40 * 1024 * 1024),
        cost_estimate=pl.CostEstimate(
            flops=4 * rows * q_width * total, bytes_accessed=4 << 20, transcendentals=rows * total * 4
        ),
        name="attention",
    )(starts.reshape(rows, 1), first_row.reshape(1, 1), queries, pairs)


def attention_back_kernel(groups, starts_ref, first_ref, queries_ref, grads_ref, pairs_ref, query_out, pair_out, probs, back):
    rows = queries_ref.shape[0]
    total, both = pairs_ref.shape
    pair_width = both // 2
    block = 512
    blocks = [slice(at, at + block) for at in range(0, total, block)]
    scale = HEAD_SIZE ** (-0.5)
    places = jnp.concatenate([first_ref[0, 0] + lax.broadcasted_iota(jnp.int32, (rows, 1), 0)] * groups, axis=0)
    starts = jnp.concatenate([starts_ref[...]] * groups, axis=0)
    query_parts, key_parts, value_parts = [], [], []
    for head in range(pair_width // HEAD_SIZE):

        def heads_of(ref):
            at = [(head * groups + g) * HEAD_SIZE for g in range(groups)]
            return jnp.concatenate([ref[:, a : a + HEAD_SIZE] for a in at], axis=0)

        queries, grads = heads_of(queries_ref), heads_of(grads_ref)
        own = slice(head * HEAD_SIZE, (head + 1) * HEAD_SIZE)
        own_values = slice(pair_width + own.start, pair_width + own.stop)
        top = jnp.full((rows * groups, 1), -1e30, f32)
        for part in blocks:
            key_rows = part.start + lax.broadcasted_iota(jnp.int32, (1, block), 1)
            allowed = (key_rows >= starts) & (key_rows <= places)
            scores = contract_cols(queries, pairs_ref[part, own]) * scale
            scores = jnp.where(allowed, scores, -1e30)
            probs[:, part] = scores
            top = jnp.maximum(top, jnp.max(scores, axis=1, keepdims=True))
        count = jnp.zeros((rows * groups, 1), f32)
        for part in blocks:
            raised = jnp.exp(probs[:, part] - top)
            probs[:, part] = raised
            count += jnp.sum(raised, axis=1, keepdims=True)
        share = 1.0 / count
        mean = jnp.zeros((rows * groups, 1), f32)
        for part in blocks:
            weights = probs[:, part] * share
            probs[:, part] = weights
            prob_grad = contract_cols(grads, pairs_ref[part, own_values])
            back[:, part] = prob_grad
            mean += jnp.sum(weights * prob_grad, axis=1, keepdims=True)
        query_grad = jnp.zeros((rows * groups, HEAD_SIZE), f32)
        keys_here, values_here = [], []
        for part in blocks:
            weights = probs[:, part]
            score_grad = (weights * (back[:, part] - mean)).astype(bf16)
            query_grad += mm(score_grad, pairs_ref[part, own])
            keys_here.append((contract_rows(score_grad, queries) * scale).astype(bf16))
            values_here.append(contract_rows(weights.astype(bf16), grads).astype(bf16))
        query_grad = query_grad * scale
        query_parts += [query_grad[g * rows : (g + 1) * rows] for g in range(groups)]
        key_parts.append(jnp.concatenate(keys_here, axis=0))
        value_parts.append(jnp.concatenate(values_here, axis=0))
    query_out[...] = jnp.concatenate(query_parts, axis=1)
    pair_out[...] = jnp.concatenate(key_parts + value_parts, axis=1)


def attention_back(starts, first_row, queries, grads, pairs, pair_width):
    rows, q_width = queries.shape
    total = pairs.shape[0]
    groups = q_width // pair_width
    vmem = pl.BlockSpec(memory_space=pltpu.VMEM)
    return pl.pallas_call(
        functools.partial(attention_back_kernel, groups),
        out_shape=[
            jax.ShapeDtypeStruct((rows, q_width), f32),
            jax.ShapeDtypeStruct((total, 2 * pair_width), bf16),
        ],
        in_specs=[vmem, pl.BlockSpec(memory_space=pltpu.SMEM), vmem, vmem, vmem],
        out_specs=[vmem, vmem],
        scratch_shapes=[pltpu.VMEM((rows * groups, total), f32)] * 2,
        compiler_params=pltpu.CompilerParams(vmem_limit_bytes=48 * 1024 * 1024),
        cost_estimate=pl.CostEstimate(
            flops=10 * rows * q_width * total, bytes_accessed=8 << 20, transcendentals=rows * total * 4
        ),
        name="attention_back",
    )(starts.reshape(rows, 1), first_row.reshape(1, 1), queries, grads, pairs)


def expert_kernel(
    n,
    n_fsdp,
    part,
    rows_ref,
    probs_ref,
    grads_ref,
    slices_ref,
    norm_got,
    mixed_got,
    gate_got,
    wgrad_ref,
    w_ref,
    wgrad_buf,
    wgrad_got,
    norm_buf,
    probs_buf,
    both_buf,
    weighted_buf,
    back_buf,
    mixed_buf,
    gate_buf,
    send_sems,
    recv_sems,
    wgrad_send,
    wgrad_recv,
):
    me, fsdp_at = lax.axis_index("ctx"), lax.axis_index("fsdp")
    hidden = w_ref.shape[1] // 3

    def chunk(ref, k):
        return ref.at[pl.ds(pl.multiple_of(k * CAP, CAP), CAP)]

    def copy(which, k, source, target, place):
        return pltpu.make_async_remote_copy(
            src_ref=source,
            dst_ref=target,
            send_sem=send_sems.at[which, k],
            recv_sem=recv_sems.at[which, k],
            device_id={"ctx": lax.rem(place, n)},
            device_id_type=MESH,
        )

    def out_copies(k):
        place = me + offset(k, n)
        return (
            copy(0, k, chunk(rows_ref, k), chunk(norm_buf, k), place),
            copy(1, k, probs_ref.at[k], probs_buf.at[k], place),
        )

    def back_copies(k):
        place = me + n - offset(k, n)
        return (
            copy(2, k, chunk(back_buf, k), chunk(norm_got, k), place),
            copy(3, k, gate_buf.at[k], gate_got.at[k], place),
            copy(4, k, chunk(mixed_buf, k), chunk(mixed_got, k), place),
        )

    barrier = pltpu.get_barrier_semaphore()
    for k in range(1, n):
        pl.semaphore_signal(
            barrier, inc=1, device_id={"ctx": lax.rem(me + k, n)}, device_id_type=MESH
        )
    for k in range(1, n_fsdp):
        pl.semaphore_signal(
            barrier,
            inc=1,
            device_id={"fsdp": lax.rem(fsdp_at + k, n_fsdp)},
            device_id_type=MESH,
        )
    pl.semaphore_wait(barrier, n - 1 + n_fsdp - 1)
    for k in range(1, 4):
        for item in out_copies(k):
            item.start()
    norm_buf[:CAP] = rows_ref[:CAP]
    probs_buf[0] = probs_ref[0]
    slim = wgrad_ref.shape[1]
    n_tp = hidden // slim
    for place in range(slices_ref.shape[0]):
        down = place // n_tp * part
        for which in range(3):
            start = which * hidden + place % n_tp * slim
            w_ref[down : down + part, start : start + slim] = slices_ref[place, which]
    same = lax.broadcasted_iota(jnp.int32, (CAP, CAP), 0) == lax.broadcasted_iota(
        jnp.int32, (CAP, CAP), 1
    )

    def pair(j, carry):
        @pl.when(j < n // 2 - 2)
        def _():
            for k in (2 * j + 4, 2 * j + 5):
                for item in out_copies(k):
                    item.start()

        for k in (2 * j, 2 * j + 1):

            @pl.when(k > 0)
            def _():
                for item in out_copies(k):
                    item.wait_recv()

        here = pl.ds(pl.multiple_of(j * 2 * CAP, 2 * CAP), 2 * CAP)
        gate_up = mm(norm_buf[here, :], w_ref[:, : 2 * hidden])
        down_back = mm(grads_ref[here, :], w_ref[:, 2 * hidden :])
        probs = jnp.concatenate(
            [
                jnp.sum(jnp.where(same, probs_buf[k][:1, :], 0.0), axis=1, keepdims=True)
                for k in (2 * j, 2 * j + 1)
            ],
            axis=0,
        )
        gate_pre, up_pre = gate_up[:, :hidden], gate_up[:, hidden:]
        sig = jax.nn.sigmoid(gate_pre)
        silu = gate_pre * sig
        activation = silu * up_pre
        gate_grad = branch_scale * jnp.sum(activation * down_back, axis=1, keepdims=True)
        act_grad = (branch_scale * probs) * down_back
        both_buf[here, :hidden] = (
            act_grad * up_pre * sig * (1.0 + gate_pre * (1.0 - sig))
        ).astype(bf16)
        both_buf[here, hidden:] = (act_grad * silu).astype(bf16)
        weighted_buf[here, :] = (probs * activation).astype(bf16)
        back_buf[here, :] = contract_cols(both_buf[here, :], w_ref[:, : 2 * hidden]).astype(bf16)
        for i in range(2):
            line = jnp.sum(
                jnp.where(same, gate_grad[i * CAP : (i + 1) * CAP], 0.0), axis=0, keepdims=True
            )
            gate_buf[2 * j + i] = jnp.broadcast_to(line, (8, CAP))
        mixed_buf[here, :] = contract_cols(weighted_buf[here, :], w_ref[:, 2 * hidden :]).astype(
            bf16
        )
        for k in (2 * j, 2 * j + 1):

            @pl.when(k > 0)
            def _():
                for item in back_copies(k):
                    item.start()

        return carry

    lax.fori_loop(0, n // 2, pair, 0)
    norm_got[:CAP] = back_buf[:CAP]
    mixed_got[:CAP] = mixed_buf[:CAP]
    gate_got[0] = gate_buf[0]

    def wgrad_copy(k):
        return pltpu.make_async_remote_copy(
            src_ref=wgrad_buf.at[k],
            dst_ref=wgrad_got.at[k],
            send_sem=wgrad_send.at[k],
            recv_sem=wgrad_recv.at[k],
            device_id={"fsdp": lax.rem(fsdp_at + k, n_fsdp)},
            device_id_type=MESH,
        )

    def weight_grads(j, carry):
        k = lax.rem(j + 1, n_fsdp)
        here = pl.ds(pl.multiple_of(lax.rem(fsdp_at + k, n_fsdp) * part, part), part)
        gate_up = contract_rows(norm_buf[:, here], both_buf[...]).astype(bf16)
        down = (contract_rows(grads_ref[:, here], weighted_buf[...]) * branch_scale).astype(bf16)
        for piece in range(hidden // slim):
            for which in range(3):
                row = (piece * 3 + which) * part
                if which < 2:
                    start = which * hidden + piece * slim
                    wgrad_buf[k, row : row + part, :] = gate_up[:, start : start + slim]
                else:
                    wgrad_buf[k, row : row + part, :] = down[:, piece * slim : (piece + 1) * slim]

        @pl.when(k > 0)
        def _():
            wgrad_copy(k).start()

        return carry

    lax.fori_loop(0, n_fsdp, weight_grads, 0)
    for k in range(1, n_fsdp):
        wgrad_copy(k).wait()

    def summed(j, carry):
        at = pl.ds(pl.multiple_of(j * part, part), part)
        total = wgrad_buf[0, at, :].astype(f32)
        for k in range(1, n_fsdp):
            total += wgrad_got[k, at, :].astype(f32)
        wgrad_ref[at, :] = total.astype(bf16)
        return carry

    lax.fori_loop(0, wgrad_buf.shape[1] // part, summed, 0)
    for k in range(1, n):
        for item in out_copies(k):
            item.wait_send()
        for item in back_copies(k):
            item.wait()


def expert_of_place(sizes, rows_sent, probs_sent, grad_rows, expert_w):
    n = sizes["ctx"]
    total, width = rows_sent.shape
    n_fsdp, n_tp = sizes["fsdp"], sizes["tp"]
    hidden, part = expert_w.shape[3] * n_tp, width // n_fsdp
    owned = (n_tp * 3 * part, hidden // n_tp)
    like = jax.ShapeDtypeStruct
    vmem = pl.BlockSpec(memory_space=pltpu.VMEM)
    return pl.pallas_call(
        functools.partial(expert_kernel, n, n_fsdp, part),
        out_shape=[
            like((total, width), bf16),
            like((total, width), bf16),
            like(probs_sent.shape, f32),
            like(owned, bf16),
        ],
        in_specs=[vmem] * 4,
        out_specs=[vmem] * 4,
        scratch_shapes=[
            pltpu.VMEM((width, 3 * hidden), bf16),
            pltpu.VMEM((n_fsdp,) + owned, bf16),
            pltpu.VMEM((n_fsdp,) + owned, bf16),
            pltpu.VMEM((total, width), bf16),
            pltpu.VMEM(probs_sent.shape, f32),
            pltpu.VMEM((total, 2 * hidden), bf16),
            pltpu.VMEM((total, hidden), bf16),
            pltpu.VMEM((total, width), bf16),
            pltpu.VMEM((total, width), bf16),
            pltpu.VMEM(probs_sent.shape, f32),
            pltpu.SemaphoreType.DMA((5, n)),
            pltpu.SemaphoreType.DMA((5, n)),
            pltpu.SemaphoreType.DMA((n_fsdp,)),
            pltpu.SemaphoreType.DMA((n_fsdp,)),
        ],
        compiler_params=pltpu.CompilerParams(
            collective_id=3, has_side_effects=True, vmem_limit_bytes=48 * 1024 * 1024
        ),
        cost_estimate=pl.CostEstimate(
            flops=6 * 2 * total * width * hidden * 3, bytes_accessed=100 << 20, transcendentals=0
        ),
        name="expert_of_place",
    )(rows_sent, probs_sent, grad_rows, expert_w)


def rope_tables(places, columns):
    column = jnp.arange(columns, dtype=jnp.int32)
    steps = (column % (HEAD_SIZE // 2)).astype(f32)
    frequencies = jnp.exp(steps * (-2.0 * math.log(rope_base) / HEAD_SIZE))
    angles = places.astype(f32)[:, None] * frequencies[None, :]
    first = (column % HEAD_SIZE < HEAD_SIZE // 2)[None, :]
    sine = jnp.sin(angles)
    return jnp.cos(angles), jnp.where(first, -sine, sine), first


def turn(values, cosine, sine, first):
    half = HEAD_SIZE // 2
    other = jnp.where(first, jnp.roll(values, -half, axis=1), jnp.roll(values, half, axis=1))
    return values * cosine + other * sine


def contract_rows(left, right, precision=None):
    return lax.dot_general(
        left, right, (((0,), (0,)), ((), ())), precision=precision, preferred_element_type=f32
    )


def contract_cols(left, right, precision=None):
    return lax.dot_general(
        left, right, (((1,), (1,)), ((), ())), precision=precision, preferred_element_type=f32
    )


def mm(left, right):
    return jnp.dot(left, right, preferred_element_type=f32)


def local(
    sizes,
    inputs,
    cotangent,
    lengths,
    expert_ids,
    attn_gain,
    w_query,
    key_weight,
    value_weight,
    w_output,
    ffn_gain,
    w_router,
    w_gate,
    w_up,
    w_down,
):
    rows, width = inputs.shape
    n_fsdp, n_ctx, n_tp = sizes["fsdp"], sizes["ctx"], sizes["tp"]
    experts = w_router.shape[1]
    depth, _, ff = w_gate.shape
    per_ctx = experts // n_ctx
    send = functools.partial(exchange, sizes)
    ctx_at, tp_at = lax.axis_index("ctx"), lax.axis_index("tp")

    first = ctx_at * per_ctx
    own_slices = jnp.stack(
        [
            lax.dynamic_slice_in_dim(w, first, per_ctx, 1).transpose(1, 0, 2)
            for w in (w_gate, w_up, w_down)
        ],
        axis=1,
    )
    lines = depth // 128

    def lined(gain):
        return jnp.pad(gain.reshape(lines, 128), ((0, 16 - lines), (0, 0)))

    qkv_w, gain_one, expert_slices = send(
        0,
        (("fsdp",), "g", jnp.concatenate([w_query, key_weight, value_weight], axis=1)),
        (("fsdp",), "g", lined(attn_gain)),
        (("tp",), "a", own_slices),
    )
    qkv_w = qkv_w.reshape(width, -1)
    gain_one = gain_one[:, :lines].reshape(width).astype(f32)
    expert_w = lax.all_gather(expert_slices, "fsdp", axis=0, tiled=True)

    chosen = jnp.any(
        expert_ids[:, :, None] == jnp.arange(experts, dtype=jnp.int32)[None, None, :], axis=1
    )
    offsets = [offset(slot, n_ctx) for slot in range(n_ctx)]
    ctx_order = lax.rem(ctx_at + jnp.array(offsets, dtype=jnp.int32), n_ctx)
    mine = ctx_order * per_ctx + tp_at
    chosen_mine = jnp.any(expert_ids[None, :, :] == mine[:, None, None], axis=2)
    earlier = jnp.arange(rows)[:, None] < jnp.arange(rows)[None, :]
    rank = mm(chosen_mine.astype(bf16), earlier.astype(bf16))
    slots = jnp.arange(CAP, dtype=f32)
    picks = (chosen_mine[:, None, :] & (rank[:, None, :] == slots[None, :, None])).astype(bf16)
    picks_flat = picks.reshape(n_ctx * CAP, rows)

    lengths_row = lengths[0]
    query_rows = ctx_at * rows + jnp.arange(rows, dtype=jnp.int32)
    seq_ends = jnp.cumsum(lengths_row)
    passed = (query_rows[:, None] >= seq_ends[None, :]).astype(jnp.int32)
    starts = jnp.sum(passed * lengths_row[None, :], axis=1)
    q_end, pair_width = w_query.shape[1], key_weight.shape[1]
    turned = q_end + pair_width
    cosine, sine, first_half = rope_tables(query_rows - starts, turned)
    hidden_in = inputs.astype(f32)
    scale_one = lax.rsqrt(jnp.mean(hidden_in * hidden_in, axis=-1, keepdims=True) + norm_eps)
    normed_one = (hidden_in * scale_one * gain_one).astype(bf16)
    qkv = mm(normed_one, qkv_w)
    queries_keys = turn(qkv[:, :turned], cosine, sine, first_half).astype(bf16)
    queries = queries_keys[:, :q_end]
    pairs_local = jnp.concatenate(
        [queries_keys[:, q_end:], qkv[:, turned:].astype(bf16)], axis=1
    )
    grads_sent = mm(picks_flat, cotangent).astype(bf16).reshape(n_ctx, CAP, width)
    pairs_all, output_w, gain_two, router_all, grad_rows = send(
        1,
        (("ctx",), "g", pairs_local),
        (("fsdp",), "g", w_output),
        (("fsdp",), "g", lined(ffn_gain)),
        (("fsdp",), "g", jnp.pad(w_router, ((0, 0), (0, 128 - experts)))),
        (("ctx",), "f", grads_sent),
    )
    output_w = output_w.reshape(width, -1)
    gain_two = gain_two[:, :lines].reshape(width).astype(f32)
    router_w = router_all.reshape(width, 128)[:, :experts]
    grad_rows = grad_rows.reshape(n_ctx * CAP, width)
    total_rows = n_ctx * rows
    pairs_all = pairs_all.reshape(total_rows, 2 * pair_width)
    attended = attention(starts, ctx_at * rows, queries, pairs_all, pair_width)
    quarter = rows // n_tp

    def quarter_of(array):
        return lax.dynamic_slice_in_dim(array, tp_at * quarter, quarter, 0)

    attn_part = contract_cols(attended, output_w).astype(bf16)
    (attn_parts,) = send(2, (("tp",), "a", attn_part.reshape(n_tp, quarter, width)))
    hidden_own, scale_one_own = quarter_of(hidden_in), quarter_of(scale_one)
    residual_own = hidden_own + branch_scale * jnp.sum(attn_parts.astype(f32), axis=0)

    scale_two_own = lax.rsqrt(jnp.mean(residual_own * residual_own, axis=-1, keepdims=True) + norm_eps)
    normed_two_own = (residual_own * scale_two_own * gain_two).astype(bf16)
    (normed_two,) = send(11, (("tp",), "g", normed_two_own))
    normed_two = normed_two.reshape(rows, width)
    logits = mm(normed_two, router_w)
    route_masked = jnp.where(chosen, logits, -1e30)
    route_exp = jnp.exp(route_masked - jnp.max(route_masked, axis=-1, keepdims=True))
    gate_probs = route_exp / jnp.sum(route_exp, axis=-1, keepdims=True)
    probs_mine = lax.dynamic_index_in_dim(
        gate_probs.T.reshape(n_ctx, per_ctx, rows), tp_at, 1, keepdims=False
    )
    probs_mine = jnp.take(probs_mine, ctx_order, axis=0)
    probs_sent = jnp.sum(picks.astype(f32) * probs_mine[:, None, :], axis=2)
    rows_sent = mm(picks_flat, normed_two).astype(bf16)
    probs_sent = jnp.broadcast_to(probs_sent[:, None, :], (n_ctx, 8, CAP))
    norm_grad_got, mixed_got, gate_grad_got, expert_grad = expert_of_place(
        sizes, rows_sent, probs_sent, grad_rows, expert_w
    )

    norm_grad_part = contract_rows(picks_flat, norm_grad_got)
    gate_grad_part = jnp.sum(picks.astype(f32) * gate_grad_got[:, 0, :, None], axis=1)
    norm_grad_parts, gate_grad_parts, pieces = send(
        5,
        (("tp",), "a", norm_grad_part.astype(bf16).reshape(n_tp, quarter, width)),
        (("tp",), "g", gate_grad_part),
        (("tp",), "a", expert_grad.reshape(n_tp, 3, depth, ff)),
    )

    pairs = [[2 * i, 2 * i + 1] for i in range(n_ctx // 2)]
    rings = [list(range(start, n_ctx, 2)) for start in range(2)]
    pieces = lax.all_gather(pieces, "ctx", axis=0, tiled=True, axis_index_groups=pairs)

    slot_of = jnp.array([offsets.index(k) for k in range(n_ctx)], dtype=jnp.int32)
    back_order = slot_of[lax.rem(jnp.arange(n_ctx, dtype=jnp.int32) + n_ctx - ctx_at, n_ctx)]
    gate_grads = jnp.take(gate_grad_parts, back_order, axis=1)
    gate_grads = gate_grads.transpose(2, 1, 0).reshape(rows, experts)
    route_grad = gate_probs * (
        gate_grads - jnp.sum(gate_probs * gate_grads, axis=-1, keepdims=True)
    )
    grad_router = contract_rows(normed_two.astype(f32), route_grad, highest)
    router_back = contract_cols(quarter_of(route_grad), router_w.astype(f32), highest)
    normed_grad = jnp.sum(norm_grad_parts.astype(f32), axis=0) + router_back
    weighted_two = normed_grad * gain_two
    grad_ffn_part = jnp.sum(normed_grad * residual_own * scale_two_own, axis=0)
    residual_grad = (
        quarter_of(cotangent).astype(f32)
        + scale_two_own * weighted_two
        - residual_own
        * scale_two_own**3
        * jnp.mean(weighted_two * residual_own, axis=-1, keepdims=True)
    )
    (attn_in,) = send(6, (("tp",), "g", (branch_scale * residual_grad).astype(bf16)))
    attn_in = attn_in.reshape(rows, width)

    side = jnp.pad(grad_router, ((0, 0), (0, 128 - experts)))
    early = jnp.concatenate([contract_rows(attn_in, attended), side], axis=1).astype(bf16)
    mixed_part = contract_rows(picks_flat, mixed_got).astype(bf16)
    attended_grad = mm(attn_in, output_w).astype(bf16)

    query_grad_rot, pair_grads = attention_back(
        starts, ctx_at * rows, queries, attended_grad, pairs_all, pair_width
    )
    pair_got, mixed_parts, early_got = send(
        7,
        (("ctx",), "a", pair_grads.reshape(n_ctx, rows, 2 * pair_width)),
        (("tp",), "a", mixed_part.reshape(n_tp, quarter, width)),
        (("fsdp",), "a", early.reshape(n_fsdp, depth, -1)),
    )
    pieces, pair_got = lax.optimization_barrier((pieces, pair_got))
    expert_all = lax.all_gather(pieces, "ctx", axis=0, tiled=True, axis_index_groups=rings)
    pair_owned = jnp.sum(pair_got.astype(f32), axis=0)
    turned_back = turn(
        jnp.concatenate([query_grad_rot, pair_owned[:, :pair_width]], axis=1),
        cosine,
        -sine,
        first_half,
    )
    qkv_grad = jnp.concatenate([turned_back, pair_owned[:, pair_width:]], axis=1).astype(bf16)
    normed_one_part = contract_cols(qkv_grad, qkv_w)
    grad_gain_part = jnp.sum(normed_one_part * hidden_in * scale_one, axis=0)
    grad_qkv = contract_rows(normed_one, qkv_grad).astype(bf16)
    output = residual_own + branch_scale * jnp.sum(mixed_parts.astype(f32), axis=0)

    gain_parts = jnp.stack([grad_gain_part, grad_ffn_part]).reshape(2, n_fsdp, depth)
    gain_chunks = jnp.pad(gain_parts.transpose(1, 0, 2), ((0, 0), (0, 6), (0, 0)))
    one_parts, qkv_got, gain_got, output = send(
        8,
        (("tp",), "a", normed_one_part.astype(bf16).reshape(n_tp, quarter, width)),
        (("fsdp",), "a", grad_qkv.reshape(n_fsdp, depth, -1)),
        (("fsdp",), "a", gain_chunks),
        (("tp",), "g", output.astype(bf16)),
    )
    small = jnp.concatenate(
        [
            jnp.sum(qkv_got.astype(f32), axis=0).astype(bf16),
            jnp.sum(early_got.astype(f32), axis=0).astype(bf16),
        ],
        axis=1,
    )
    gain_sum = jnp.sum(gain_got, axis=0)
    normed_one_grad = jnp.sum(one_parts.astype(f32), axis=0)
    weighted_one = normed_one_grad * gain_one
    input_grad = (
        residual_grad
        + scale_one_own * weighted_one
        - hidden_own
        * scale_one_own**3
        * jnp.mean(weighted_one * hidden_own, axis=-1, keepdims=True)
    )
    small_got, gain_all, input_grad = send(
        9,
        (("ctx",), "a", small.reshape(n_ctx, depth // n_ctx, -1)),
        (("ctx", "tp"), "g", gain_sum),
        (("tp",), "g", input_grad.astype(bf16)),
    )
    (small_all,) = send(10, (("ctx",), "g", jnp.sum(small_got.astype(f32), axis=0).astype(bf16)))
    small_all = small_all.reshape(depth, -1).astype(f32)
    gain_all = jnp.sum(gain_all, axis=0)
    grad_gate, grad_up, grad_down = spread(expert_all)
    k_end, v_end = q_end + pair_width, q_end + 2 * pair_width
    o_end = v_end + attended.shape[1]
    return (
        output.reshape(rows, width),
        input_grad.reshape(rows, width),
        gain_all[0],
        small_all[:, :q_end],
        small_all[:, q_end:k_end],
        small_all[:, k_end:v_end],
        small_all[:, v_end:o_end],
        gain_all[1],
        small_all[:, o_end : o_end + experts],
        grad_gate,
        grad_up,
        grad_down,
    )


def solution(mesh):
    sizes = dict(mesh.shape)
    return jax.shard_map(
        functools.partial(local, sizes),
        mesh=mesh,
        in_specs=(
            P(("fsdp", "ctx"), None),
            P(("fsdp", "ctx"), None),
            P("fsdp", None),
            P(("fsdp", "ctx"), None),
            P("fsdp"),
            P("fsdp", "tp"),
            P("fsdp", "tp"),
            P("fsdp", "tp"),
            P("fsdp", "tp"),
            P("fsdp"),
            P("fsdp", None),
            P("fsdp", None, "tp"),
            P("fsdp", None, "tp"),
            P("fsdp", None, "tp"),
        ),
        out_specs=(
            P(("fsdp", "ctx"), None),
            P(("fsdp", "ctx"), None),
            P("fsdp"),
            P("fsdp", "tp"),
            P("fsdp", "tp"),
            P("fsdp", "tp"),
            P("fsdp", "tp"),
            P("fsdp"),
            P("fsdp", None),
            P("fsdp", None, "tp"),
            P("fsdp", None, "tp"),
            P("fsdp", None, "tp"),
        ),
        check_vma=False,
    )
```

```python
import functools
import math

import jax
import jax.numpy as jnp
from jax import lax
from jax.experimental import pallas as pl
from jax.experimental.pallas import tpu as pltpu
from jax.sharding import PartitionSpec as P

HEAD_SIZE = 64
CAP = 128
MESH = pl.DeviceIdType.MESH

norm_eps = 1e-06
rope_base = 10000.0
branch_scale = 0.22
highest = lax.Precision.HIGHEST
bf16 = jnp.bfloat16
f32 = jnp.float32


def offset(slot, n):
    return slot // 2 + slot % 2 * (n // 2)


def exchange_kernel(plan, sizes, *refs):
    count = len(plan)
    ins, outs = refs[:count], refs[count : 2 * count]
    send_sem, recv_sem, self_sem = refs[2 * count :]

    def place(axes, step):
        offsets = []
        for axis in reversed(axes):
            offsets.append(step % sizes[axis])
            step //= sizes[axis]
        coords = {}
        for axis, offset in zip(axes, offsets[::-1]):
            here = lax.axis_index(axis)
            coords[axis] = lax.rem(here + offset, sizes[axis]) if offset else here
        return coords

    def flat(axes, coords):
        index = 0
        for axis in axes:
            index = index * sizes[axis] + coords[axis]
        return index

    groups = {}
    for axes, _ in plan:
        for step in range(1, math.prod(sizes[a] for a in axes)):
            full, rest = {}, step
            for axis in reversed(axes):
                full[axis] = rest % sizes[axis]
                rest //= sizes[axis]
            key = tuple(sorted((a, o) for a, o in full.items() if o))
            groups[key] = (axes, step)
    barrier = pltpu.get_barrier_semaphore()
    for axes, step in groups.values():
        pl.semaphore_signal(barrier, inc=1, device_id=place(axes, step), device_id_type=MESH)
    pl.semaphore_wait(barrier, len(groups))

    copies = []
    for at, (axes, mode) in enumerate(plan):
        mine = flat(axes, place(axes, 0))
        for step in range(1, math.prod(sizes[a] for a in axes)):
            if mode == "f":
                peer = place(axes, offset(step, sizes[axes[0]]))
                source, slot = ins[at].at[step], step
            else:
                peer = place(axes, step)
                source = ins[at] if mode == "g" else ins[at].at[flat(axes, peer)]
                slot = mine
            copy = pltpu.make_async_remote_copy(
                src_ref=source,
                dst_ref=outs[at].at[slot],
                send_sem=send_sem.at[at, step],
                recv_sem=recv_sem.at[at, step],
                device_id=peer,
                device_id_type=MESH,
            )
            copy.start()
            copies.append(copy)
        if mode == "f":
            mine = 0
        own = pltpu.make_async_copy(
            ins[at] if mode == "g" else ins[at].at[mine], outs[at].at[mine], self_sem.at[at]
        )
        own.start()
        copies.append(own)
    for copy in copies:
        copy.wait()


def exchange(sizes, collective_id, *items):
    plan = [(axes, mode) for axes, mode, _ in items]
    arrays = [array for _, _, array in items]
    outs = []
    most = 1
    for axes, mode, array in items:
        n = math.prod(sizes[a] for a in axes)
        most = max(most, n)
        shape = (n,) + array.shape if mode == "g" else array.shape
        outs.append(jax.ShapeDtypeStruct(shape, array.dtype))
    count = len(items)
    moved = sum(math.prod(o.shape) * o.dtype.itemsize for o in outs)
    return pl.pallas_call(
        functools.partial(exchange_kernel, plan, sizes),
        out_shape=outs,
        in_specs=[pl.BlockSpec(memory_space=pl.ANY)] * count,
        out_specs=[pl.BlockSpec(memory_space=pl.ANY)] * count,
        scratch_shapes=[
            pltpu.SemaphoreType.DMA((count, most)),
            pltpu.SemaphoreType.DMA((count, most)),
            pltpu.SemaphoreType.DMA((count,)),
        ],
        compiler_params=pltpu.CompilerParams(collective_id=collective_id, has_side_effects=True),
        cost_estimate=pl.CostEstimate(flops=0, bytes_accessed=20 * moved, transcendentals=0),
        name="exchange_%d" % collective_id,
    )(*arrays)


def spread_kernel(pieces_ref, *out_refs):
    for which, out_ref in enumerate(out_refs):
        turned = jnp.swapaxes(pieces_ref[:, which].astype(f32), 0, 1)
        out_ref[...] = turned.reshape(out_ref.shape)


def spread(pieces):
    experts, count, depth, ff = pieces.shape
    block = 64
    outs = pl.pallas_call(
        spread_kernel,
        grid=(depth // block,),
        out_shape=[jax.ShapeDtypeStruct((depth * experts, ff), f32)] * count,
        in_specs=[pl.BlockSpec((experts, count, block, ff), lambda i: (0, 0, i, 0))],
        out_specs=[pl.BlockSpec((block * experts, ff), lambda i: (i, 0))] * count,
        compiler_params=pltpu.CompilerParams(vmem_limit_bytes=40 * 1024 * 1024),
        name="spread",
    )(pieces)
    return [out.reshape(depth, experts, ff) for out in outs]


def attention_kernel(groups, starts_ref, first_ref, queries_ref, pairs_ref, out_ref, probs):
    rows = queries_ref.shape[0]
    total, both = pairs_ref.shape
    pair_width = both // 2
    block = 512
    blocks = [slice(at, at + block) for at in range(0, total, block)]
    places = jnp.concatenate(
        [first_ref[0, 0] + lax.broadcasted_iota(jnp.int32, (rows, 1), 0)] * groups, axis=0
    )
    starts = jnp.concatenate([starts_ref[...]] * groups, axis=0)
    parts = []
    for head in range(pair_width // HEAD_SIZE):
        at = [(head * groups + g) * HEAD_SIZE for g in range(groups)]
        queries = jnp.concatenate([queries_ref[:, a : a + HEAD_SIZE] for a in at], axis=0)
        own = slice(head * HEAD_SIZE, (head + 1) * HEAD_SIZE)
        own_values = slice(pair_width + own.start, pair_width + own.stop)
        top = jnp.full((rows * groups, 1), -1e30, f32)
        for part in blocks:
            key_rows = part.start + lax.broadcasted_iota(jnp.int32, (1, block), 1)
            allowed = (key_rows >= starts) & (key_rows <= places)
            scores = contract_cols(queries, pairs_ref[part, own]) * HEAD_SIZE ** (-0.5)
            scores = jnp.where(allowed, scores, -1e30)
            probs[:, part] = scores
            top = jnp.maximum(top, jnp.max(scores, axis=1, keepdims=True))
        count = jnp.zeros((rows * groups, 1), f32)
        for part in blocks:
            raised = jnp.exp(probs[:, part] - top)
            probs[:, part] = raised
            count += jnp.sum(raised, axis=1, keepdims=True)
        share = 1.0 / count
        attended = jnp.zeros((rows * groups, HEAD_SIZE), f32)
        for part in blocks:
            attended += mm((probs[:, part] * share).astype(bf16), pairs_ref[part, own_values])
        parts += [attended[g * rows : (g + 1) * rows] for g in range(groups)]
    out_ref[...] = jnp.concatenate(parts, axis=1).astype(bf16)


def attention(starts, first_row, queries, pairs, pair_width):
    rows, q_width = queries.shape
    total = pairs.shape[0]
    groups = q_width // pair_width
    vmem = pl.BlockSpec(memory_space=pltpu.VMEM)
    return pl.pallas_call(
        functools.partial(attention_kernel, groups),
        out_shape=jax.ShapeDtypeStruct((rows, q_width), bf16),
        in_specs=[vmem, pl.BlockSpec(memory_space=pltpu.SMEM), vmem, vmem],
        out_specs=vmem,
        scratch_shapes=[pltpu.VMEM((rows * groups, total), f32)],
        compiler_params=pltpu.CompilerParams(vmem_limit_bytes=40 * 1024 * 1024),
        cost_estimate=pl.CostEstimate(
            flops=4 * rows * q_width * total, bytes_accessed=4 << 20, transcendentals=rows * total * 4
        ),
        name="attention",
    )(starts.reshape(rows, 1), first_row.reshape(1, 1), queries, pairs)


def attention_back_kernel(groups, starts_ref, first_ref, queries_ref, grads_ref, pairs_ref, query_out, pair_out, probs, back):
    rows = queries_ref.shape[0]
    total, both = pairs_ref.shape
    pair_width = both // 2
    block = 512
    blocks = [slice(at, at + block) for at in range(0, total, block)]
    scale = HEAD_SIZE ** (-0.5)
    places = jnp.concatenate([first_ref[0, 0] + lax.broadcasted_iota(jnp.int32, (rows, 1), 0)] * groups, axis=0)
    starts = jnp.concatenate([starts_ref[...]] * groups, axis=0)
    query_parts, key_parts, value_parts = [], [], []
    for head in range(pair_width // HEAD_SIZE):

        def heads_of(ref):
            at = [(head * groups + g) * HEAD_SIZE for g in range(groups)]
            return jnp.concatenate([ref[:, a : a + HEAD_SIZE] for a in at], axis=0)

        queries, grads = heads_of(queries_ref), heads_of(grads_ref)
        own = slice(head * HEAD_SIZE, (head + 1) * HEAD_SIZE)
        own_values = slice(pair_width + own.start, pair_width + own.stop)
        top = jnp.full((rows * groups, 1), -1e30, f32)
        for part in blocks:
            key_rows = part.start + lax.broadcasted_iota(jnp.int32, (1, block), 1)
            allowed = (key_rows >= starts) & (key_rows <= places)
            scores = contract_cols(queries, pairs_ref[part, own]) * scale
            scores = jnp.where(allowed, scores, -1e30)
            probs[:, part] = scores
            top = jnp.maximum(top, jnp.max(scores, axis=1, keepdims=True))
        count = jnp.zeros((rows * groups, 1), f32)
        for part in blocks:
            raised = jnp.exp(probs[:, part] - top)
            probs[:, part] = raised
            count += jnp.sum(raised, axis=1, keepdims=True)
        share = 1.0 / count
        mean = jnp.zeros((rows * groups, 1), f32)
        for part in blocks:
            weights = probs[:, part] * share
            probs[:, part] = weights
            prob_grad = contract_cols(grads, pairs_ref[part, own_values])
            back[:, part] = prob_grad
            mean += jnp.sum(weights * prob_grad, axis=1, keepdims=True)
        query_grad = jnp.zeros((rows * groups, HEAD_SIZE), f32)
        keys_here, values_here = [], []
        for part in blocks:
            weights = probs[:, part]
            score_grad = (weights * (back[:, part] - mean)).astype(bf16)
            query_grad += mm(score_grad, pairs_ref[part, own])
            keys_here.append((contract_rows(score_grad, queries) * scale).astype(bf16))
            values_here.append(contract_rows(weights.astype(bf16), grads).astype(bf16))
        query_grad = query_grad * scale
        query_parts += [query_grad[g * rows : (g + 1) * rows] for g in range(groups)]
        key_parts.append(jnp.concatenate(keys_here, axis=0))
        value_parts.append(jnp.concatenate(values_here, axis=0))
    query_out[...] = jnp.concatenate(query_parts, axis=1)
    pair_out[...] = jnp.concatenate(key_parts + value_parts, axis=1)


def attention_back(starts, first_row, queries, grads, pairs, pair_width):
    rows, q_width = queries.shape
    total = pairs.shape[0]
    groups = q_width // pair_width
    vmem = pl.BlockSpec(memory_space=pltpu.VMEM)
    return pl.pallas_call(
        functools.partial(attention_back_kernel, groups),
        out_shape=[
            jax.ShapeDtypeStruct((rows, q_width), f32),
            jax.ShapeDtypeStruct((total, 2 * pair_width), bf16),
        ],
        in_specs=[vmem, pl.BlockSpec(memory_space=pltpu.SMEM), vmem, vmem, vmem],
        out_specs=[vmem, vmem],
        scratch_shapes=[pltpu.VMEM((rows * groups, total), f32)] * 2,
        compiler_params=pltpu.CompilerParams(vmem_limit_bytes=48 * 1024 * 1024),
        cost_estimate=pl.CostEstimate(
            flops=10 * rows * q_width * total, bytes_accessed=8 << 20, transcendentals=rows * total * 4
        ),
        name="attention_back",
    )(starts.reshape(rows, 1), first_row.reshape(1, 1), queries, grads, pairs)


def expert_kernel(
    n,
    n_fsdp,
    part,
    rows_ref,
    probs_ref,
    grads_ref,
    slices_ref,
    norm_got,
    mixed_got,
    gate_got,
    wgrad_ref,
    w_ref,
    wgrad_buf,
    wgrad_got,
    norm_buf,
    probs_buf,
    both_buf,
    weighted_buf,
    back_buf,
    mixed_buf,
    gate_buf,
    send_sems,
    recv_sems,
    wgrad_send,
    wgrad_recv,
):
    me, fsdp_at = lax.axis_index("ctx"), lax.axis_index("fsdp")
    hidden = w_ref.shape[1] // 3

    def chunk(ref, k):
        return ref.at[pl.ds(pl.multiple_of(k * CAP, CAP), CAP)]

    def copy(which, k, source, target, place):
        return pltpu.make_async_remote_copy(
            src_ref=source,
            dst_ref=target,
            send_sem=send_sems.at[which, k],
            recv_sem=recv_sems.at[which, k],
            device_id={"ctx": lax.rem(place, n)},
            device_id_type=MESH,
        )

    def out_copies(k):
        place = me + offset(k, n)
        return (
            copy(0, k, chunk(rows_ref, k), chunk(norm_buf, k), place),
            copy(1, k, probs_ref.at[k], probs_buf.at[k], place),
        )

    def back_copies(k):
        place = me + n - offset(k, n)
        return (
            copy(2, k, chunk(back_buf, k), chunk(norm_got, k), place),
            copy(3, k, gate_buf.at[k], gate_got.at[k], place),
            copy(4, k, chunk(mixed_buf, k), chunk(mixed_got, k), place),
        )

    barrier = pltpu.get_barrier_semaphore()
    for k in range(1, n):
        pl.semaphore_signal(
            barrier, inc=1, device_id={"ctx": lax.rem(me + k, n)}, device_id_type=MESH
        )
    for k in range(1, n_fsdp):
        pl.semaphore_signal(
            barrier,
            inc=1,
            device_id={"fsdp": lax.rem(fsdp_at + k, n_fsdp)},
            device_id_type=MESH,
        )
    pl.semaphore_wait(barrier, n - 1 + n_fsdp - 1)
    for k in range(1, 4):
        for item in out_copies(k):
            item.start()
    norm_buf[:CAP] = rows_ref[:CAP]
    probs_buf[0] = probs_ref[0]
    slim = wgrad_ref.shape[1]
    n_tp = hidden // slim
    for place in range(slices_ref.shape[0]):
        down = place // n_tp * part
        for which in range(3):
            start = which * hidden + place % n_tp * slim
            w_ref[down : down + part, start : start + slim] = slices_ref[place, which]
    same = lax.broadcasted_iota(jnp.int32, (CAP, CAP), 0) == lax.broadcasted_iota(
        jnp.int32, (CAP, CAP), 1
    )

    def pair(j, carry):
        @pl.when(j < n // 2 - 2)
        def _():
            for k in (2 * j + 4, 2 * j + 5):
                for item in out_copies(k):
                    item.start()

        for k in (2 * j, 2 * j + 1):

            @pl.when(k > 0)
            def _():
                for item in out_copies(k):
                    item.wait_recv()

        here = pl.ds(pl.multiple_of(j * 2 * CAP, 2 * CAP), 2 * CAP)
        gate_up = mm(norm_buf[here, :], w_ref[:, : 2 * hidden])
        down_back = mm(grads_ref[here, :], w_ref[:, 2 * hidden :])
        probs = jnp.concatenate(
            [
                jnp.sum(jnp.where(same, probs_buf[k][:1, :], 0.0), axis=1, keepdims=True)
                for k in (2 * j, 2 * j + 1)
            ],
            axis=0,
        )
        gate_pre, up_pre = gate_up[:, :hidden], gate_up[:, hidden:]
        sig = jax.nn.sigmoid(gate_pre)
        silu = gate_pre * sig
        activation = silu * up_pre
        gate_grad = branch_scale * jnp.sum(activation * down_back, axis=1, keepdims=True)
        act_grad = (branch_scale * probs) * down_back
        both_buf[here, :hidden] = (
            act_grad * up_pre * sig * (1.0 + gate_pre * (1.0 - sig))
        ).astype(bf16)
        both_buf[here, hidden:] = (act_grad * silu).astype(bf16)
        weighted_buf[here, :] = (probs * activation).astype(bf16)
        back_buf[here, :] = contract_cols(both_buf[here, :], w_ref[:, : 2 * hidden]).astype(bf16)
        for i in range(2):
            line = jnp.sum(
                jnp.where(same, gate_grad[i * CAP : (i + 1) * CAP], 0.0), axis=0, keepdims=True
            )
            gate_buf[2 * j + i] = jnp.broadcast_to(line, (8, CAP))
        mixed_buf[here, :] = contract_cols(weighted_buf[here, :], w_ref[:, 2 * hidden :]).astype(
            bf16
        )
        for k in (2 * j, 2 * j + 1):

            @pl.when(k > 0)
            def _():
                for item in back_copies(k):
                    item.start()

        return carry

    lax.fori_loop(0, n // 2, pair, 0)
    norm_got[:CAP] = back_buf[:CAP]
    mixed_got[:CAP] = mixed_buf[:CAP]
    gate_got[0] = gate_buf[0]

    def wgrad_copy(k):
        return pltpu.make_async_remote_copy(
            src_ref=wgrad_buf.at[k],
            dst_ref=wgrad_got.at[k],
            send_sem=wgrad_send.at[k],
            recv_sem=wgrad_recv.at[k],
            device_id={"fsdp": lax.rem(fsdp_at + k, n_fsdp)},
            device_id_type=MESH,
        )

    def weight_grads(j, carry):
        k = lax.rem(j + 1, n_fsdp)
        here = pl.ds(pl.multiple_of(lax.rem(fsdp_at + k, n_fsdp) * part, part), part)
        gate_up = contract_rows(norm_buf[:, here], both_buf[...]).astype(bf16)
        down = (contract_rows(grads_ref[:, here], weighted_buf[...]) * branch_scale).astype(bf16)
        for piece in range(hidden // slim):
            for which in range(3):
                row = (piece * 3 + which) * part
                if which < 2:
                    start = which * hidden + piece * slim
                    wgrad_buf[k, row : row + part, :] = gate_up[:, start : start + slim]
                else:
                    wgrad_buf[k, row : row + part, :] = down[:, piece * slim : (piece + 1) * slim]

        @pl.when(k > 0)
        def _():
            wgrad_copy(k).start()

        return carry

    lax.fori_loop(0, n_fsdp, weight_grads, 0)
    for k in range(1, n_fsdp):
        wgrad_copy(k).wait()

    def summed(j, carry):
        at = pl.ds(pl.multiple_of(j * part, part), part)
        total = wgrad_buf[0, at, :].astype(f32)
        for k in range(1, n_fsdp):
            total += wgrad_got[k, at, :].astype(f32)
        wgrad_ref[at, :] = total.astype(bf16)
        return carry

    lax.fori_loop(0, wgrad_buf.shape[1] // part, summed, 0)
    for k in range(1, n):
        for item in out_copies(k):
            item.wait_send()
        for item in back_copies(k):
            item.wait()


def expert_of_place(sizes, rows_sent, probs_sent, grad_rows, expert_w):
    n = sizes["ctx"]
    total, width = rows_sent.shape
    n_fsdp, n_tp = sizes["fsdp"], sizes["tp"]
    hidden, part = expert_w.shape[3] * n_tp, width // n_fsdp
    owned = (n_tp * 3 * part, hidden // n_tp)
    like = jax.ShapeDtypeStruct
    vmem = pl.BlockSpec(memory_space=pltpu.VMEM)
    return pl.pallas_call(
        functools.partial(expert_kernel, n, n_fsdp, part),
        out_shape=[
            like((total, width), bf16),
            like((total, width), bf16),
            like(probs_sent.shape, f32),
            like(owned, bf16),
        ],
        in_specs=[vmem] * 4,
        out_specs=[vmem] * 4,
        scratch_shapes=[
            pltpu.VMEM((width, 3 * hidden), bf16),
            pltpu.VMEM((n_fsdp,) + owned, bf16),
            pltpu.VMEM((n_fsdp,) + owned, bf16),
            pltpu.VMEM((total, width), bf16),
            pltpu.VMEM(probs_sent.shape, f32),
            pltpu.VMEM((total, 2 * hidden), bf16),
            pltpu.VMEM((total, hidden), bf16),
            pltpu.VMEM((total, width), bf16),
            pltpu.VMEM((total, width), bf16),
            pltpu.VMEM(probs_sent.shape, f32),
            pltpu.SemaphoreType.DMA((5, n)),
            pltpu.SemaphoreType.DMA((5, n)),
            pltpu.SemaphoreType.DMA((n_fsdp,)),
            pltpu.SemaphoreType.DMA((n_fsdp,)),
        ],
        compiler_params=pltpu.CompilerParams(
            collective_id=3, has_side_effects=True, vmem_limit_bytes=48 * 1024 * 1024
        ),
        cost_estimate=pl.CostEstimate(
            flops=6 * 2 * total * width * hidden * 3, bytes_accessed=100 << 20, transcendentals=0
        ),
        name="expert_of_place",
    )(rows_sent, probs_sent, grad_rows, expert_w)


def rope_tables(places, columns):
    column = jnp.arange(columns, dtype=jnp.int32)
    steps = (column % (HEAD_SIZE // 2)).astype(f32)
    frequencies = jnp.exp(steps * (-2.0 * math.log(rope_base) / HEAD_SIZE))
    angles = places.astype(f32)[:, None] * frequencies[None, :]
    first = (column % HEAD_SIZE < HEAD_SIZE // 2)[None, :]
    sine = jnp.sin(angles)
    return jnp.cos(angles), jnp.where(first, -sine, sine), first


def turn(values, cosine, sine, first):
    half = HEAD_SIZE // 2
    other = jnp.where(first, jnp.roll(values, -half, axis=1), jnp.roll(values, half, axis=1))
    return values * cosine + other * sine


def contract_rows(left, right, precision=None):
    return lax.dot_general(
        left, right, (((0,), (0,)), ((), ())), precision=precision, preferred_element_type=f32
    )


def contract_cols(left, right, precision=None):
    return lax.dot_general(
        left, right, (((1,), (1,)), ((), ())), precision=precision, preferred_element_type=f32
    )


def mm(left, right):
    return jnp.dot(left, right, preferred_element_type=f32)


def local(
    sizes,
    inputs,
    cotangent,
    lengths,
    expert_ids,
    attn_gain,
    w_query,
    key_weight,
    value_weight,
    w_output,
    ffn_gain,
    w_router,
    w_gate,
    w_up,
    w_down,
):
    rows, width = inputs.shape
    n_fsdp, n_ctx, n_tp = sizes["fsdp"], sizes["ctx"], sizes["tp"]
    experts = w_router.shape[1]
    depth, _, ff = w_gate.shape
    per_ctx = experts // n_ctx
    send = functools.partial(exchange, sizes)
    ctx_at, tp_at = lax.axis_index("ctx"), lax.axis_index("tp")

    first = ctx_at * per_ctx
    own_slices = jnp.stack(
        [
            lax.dynamic_slice_in_dim(w, first, per_ctx, 1).transpose(1, 0, 2)
            for w in (w_gate, w_up, w_down)
        ],
        axis=1,
    )
    lines = depth // 128

    def lined(gain):
        return jnp.pad(gain.reshape(lines, 128), ((0, 16 - lines), (0, 0)))

    qkv_w, gain_one, expert_slices = send(
        0,
        (("fsdp",), "g", jnp.concatenate([w_query, key_weight, value_weight], axis=1)),
        (("fsdp",), "g", lined(attn_gain)),
        (("tp",), "a", own_slices),
    )
    qkv_w = qkv_w.reshape(width, -1)
    gain_one = gain_one[:, :lines].reshape(width).astype(f32)
    expert_w = lax.all_gather(expert_slices, "fsdp", axis=0, tiled=True)

    chosen = jnp.any(
        expert_ids[:, :, None] == jnp.arange(experts, dtype=jnp.int32)[None, None, :], axis=1
    )
    offsets = [offset(slot, n_ctx) for slot in range(n_ctx)]
    ctx_order = lax.rem(ctx_at + jnp.array(offsets, dtype=jnp.int32), n_ctx)
    mine = ctx_order * per_ctx + tp_at
    chosen_mine = jnp.any(expert_ids[None, :, :] == mine[:, None, None], axis=2)
    earlier = jnp.arange(rows)[:, None] < jnp.arange(rows)[None, :]
    rank = mm(chosen_mine.astype(bf16), earlier.astype(bf16))
    slots = jnp.arange(CAP, dtype=f32)
    picks = (chosen_mine[:, None, :] & (rank[:, None, :] == slots[None, :, None])).astype(bf16)
    picks_flat = picks.reshape(n_ctx * CAP, rows)

    lengths_row = lengths[0]
    query_rows = ctx_at * rows + jnp.arange(rows, dtype=jnp.int32)
    seq_ends = jnp.cumsum(lengths_row)
    passed = (query_rows[:, None] >= seq_ends[None, :]).astype(jnp.int32)
    starts = jnp.sum(passed * lengths_row[None, :], axis=1)
    q_end, pair_width = w_query.shape[1], key_weight.shape[1]
    turned = q_end + pair_width
    cosine, sine, first_half = rope_tables(query_rows - starts, turned)
    hidden_in = inputs.astype(f32)
    scale_one = lax.rsqrt(jnp.mean(hidden_in * hidden_in, axis=-1, keepdims=True) + norm_eps)
    normed_one = (hidden_in * scale_one * gain_one).astype(bf16)
    qkv = mm(normed_one, qkv_w)
    queries_keys = turn(qkv[:, :turned], cosine, sine, first_half).astype(bf16)
    queries = queries_keys[:, :q_end]
    pairs_local = jnp.concatenate(
        [queries_keys[:, q_end:], qkv[:, turned:].astype(bf16)], axis=1
    )
    grads_sent = mm(picks_flat, cotangent).astype(bf16).reshape(n_ctx, CAP, width)
    pairs_all, output_w, gain_two, router_all, grad_rows = send(
        1,
        (("ctx",), "g", pairs_local),
        (("fsdp",), "g", w_output),
        (("fsdp",), "g", lined(ffn_gain)),
        (("fsdp",), "g", jnp.pad(w_router, ((0, 0), (0, 128 - experts)))),
        (("ctx",), "f", grads_sent),
    )
    output_w = output_w.reshape(width, -1)
    gain_two = gain_two[:, :lines].reshape(width).astype(f32)
    router_w = router_all.reshape(width, 128)[:, :experts]
    grad_rows = grad_rows.reshape(n_ctx * CAP, width)
    total_rows = n_ctx * rows
    pairs_all = pairs_all.reshape(total_rows, 2 * pair_width)
    attended = attention(starts, ctx_at * rows, queries, pairs_all, pair_width)
    quarter = rows // n_tp

    def quarter_of(array):
        return lax.dynamic_slice_in_dim(array, tp_at * quarter, quarter, 0)

    attn_part = contract_cols(attended, output_w).astype(bf16)
    (attn_parts,) = send(2, (("tp",), "a", attn_part.reshape(n_tp, quarter, width)))
    hidden_own, scale_one_own = quarter_of(hidden_in), quarter_of(scale_one)
    residual_own = hidden_own + branch_scale * jnp.sum(attn_parts.astype(f32), axis=0)

    scale_two_own = lax.rsqrt(jnp.mean(residual_own * residual_own, axis=-1, keepdims=True) + norm_eps)
    normed_two_own = (residual_own * scale_two_own * gain_two).astype(bf16)
    (normed_two,) = send(11, (("tp",), "g", normed_two_own))
    normed_two = normed_two.reshape(rows, width)
    logits = mm(normed_two, router_w)
    route_masked = jnp.where(chosen, logits, -1e30)
    route_exp = jnp.exp(route_masked - jnp.max(route_masked, axis=-1, keepdims=True))
    gate_probs = route_exp / jnp.sum(route_exp, axis=-1, keepdims=True)
    probs_mine = lax.dynamic_index_in_dim(
        gate_probs.T.reshape(n_ctx, per_ctx, rows), tp_at, 1, keepdims=False
    )
    probs_mine = jnp.take(probs_mine, ctx_order, axis=0)
    probs_sent = jnp.sum(picks.astype(f32) * probs_mine[:, None, :], axis=2)
    rows_sent = mm(picks_flat, normed_two).astype(bf16)
    probs_sent = jnp.broadcast_to(probs_sent[:, None, :], (n_ctx, 8, CAP))
    norm_grad_got, mixed_got, gate_grad_got, expert_grad = expert_of_place(
        sizes, rows_sent, probs_sent, grad_rows, expert_w
    )

    norm_grad_part = contract_rows(picks_flat, norm_grad_got)
    gate_grad_part = jnp.sum(picks.astype(f32) * gate_grad_got[:, 0, :, None], axis=1)
    norm_grad_parts, gate_grad_parts, pieces = send(
        5,
        (("tp",), "a", norm_grad_part.astype(bf16).reshape(n_tp, quarter, width)),
        (("tp",), "g", gate_grad_part),
        (("tp",), "a", expert_grad.reshape(n_tp, 3, depth, ff)),
    )

    rings = [list(range(start, n_ctx, 2)) for start in range(2)]
    partner = lax.ppermute(pieces, "ctx", [(i, i + 1 - 2 * (i % 2)) for i in range(n_ctx)])

    slot_of = jnp.array([offsets.index(k) for k in range(n_ctx)], dtype=jnp.int32)
    back_order = slot_of[lax.rem(jnp.arange(n_ctx, dtype=jnp.int32) + n_ctx - ctx_at, n_ctx)]
    gate_grads = jnp.take(gate_grad_parts, back_order, axis=1)
    gate_grads = gate_grads.transpose(2, 1, 0).reshape(rows, experts)
    route_grad = gate_probs * (
        gate_grads - jnp.sum(gate_probs * gate_grads, axis=-1, keepdims=True)
    )
    grad_router = contract_rows(normed_two.astype(f32), route_grad, highest)
    router_back = contract_cols(quarter_of(route_grad), router_w.astype(f32), highest)
    normed_grad = jnp.sum(norm_grad_parts.astype(f32), axis=0) + router_back
    weighted_two = normed_grad * gain_two
    grad_ffn_part = jnp.sum(normed_grad * residual_own * scale_two_own, axis=0)
    residual_grad = (
        quarter_of(cotangent).astype(f32)
        + scale_two_own * weighted_two
        - residual_own
        * scale_two_own**3
        * jnp.mean(weighted_two * residual_own, axis=-1, keepdims=True)
    )
    (attn_in,) = send(6, (("tp",), "g", (branch_scale * residual_grad).astype(bf16)))
    attn_in = attn_in.reshape(rows, width)

    side = jnp.pad(grad_router, ((0, 0), (0, 128 - experts)))
    early = jnp.concatenate([contract_rows(attn_in, attended), side], axis=1).astype(bf16)
    mixed_part = contract_rows(picks_flat, mixed_got).astype(bf16)
    attended_grad = mm(attn_in, output_w).astype(bf16)

    query_grad_rot, pair_grads = attention_back(
        starts, ctx_at * rows, queries, attended_grad, pairs_all, pair_width
    )
    partner, pair_grads = lax.optimization_barrier((partner, pair_grads))
    pieces = jnp.where(
        lax.rem(ctx_at, 2) == 0,
        jnp.concatenate([pieces, partner]),
        jnp.concatenate([partner, pieces]),
    )
    expert_all = lax.all_gather(pieces, "ctx", axis=0, tiled=True, axis_index_groups=rings)
    pair_got, mixed_parts, early_got = send(
        7,
        (("ctx",), "a", pair_grads.reshape(n_ctx, rows, 2 * pair_width)),
        (("tp",), "a", mixed_part.reshape(n_tp, quarter, width)),
        (("fsdp",), "a", early.reshape(n_fsdp, depth, -1)),
    )
    pair_owned = jnp.sum(pair_got.astype(f32), axis=0)
    turned_back = turn(
        jnp.concatenate([query_grad_rot, pair_owned[:, :pair_width]], axis=1),
        cosine,
        -sine,
        first_half,
    )
    qkv_grad = jnp.concatenate([turned_back, pair_owned[:, pair_width:]], axis=1).astype(bf16)
    normed_one_part = contract_cols(qkv_grad, qkv_w)
    grad_gain_part = jnp.sum(normed_one_part * hidden_in * scale_one, axis=0)
    grad_qkv = contract_rows(normed_one, qkv_grad).astype(bf16)
    output = residual_own + branch_scale * jnp.sum(mixed_parts.astype(f32), axis=0)

    gain_parts = jnp.stack([grad_gain_part, grad_ffn_part]).reshape(2, n_fsdp, depth)
    gain_chunks = jnp.pad(gain_parts.transpose(1, 0, 2), ((0, 0), (0, 6), (0, 0)))
    one_parts, qkv_got, gain_got, output = send(
        8,
        (("tp",), "a", normed_one_part.astype(bf16).reshape(n_tp, quarter, width)),
        (("fsdp",), "a", grad_qkv.reshape(n_fsdp, depth, -1)),
        (("fsdp",), "a", gain_chunks),
        (("tp",), "g", output.astype(bf16)),
    )
    small = jnp.concatenate(
        [
            jnp.sum(qkv_got.astype(f32), axis=0).astype(bf16),
            jnp.sum(early_got.astype(f32), axis=0).astype(bf16),
        ],
        axis=1,
    )
    gain_sum = jnp.sum(gain_got, axis=0)
    normed_one_grad = jnp.sum(one_parts.astype(f32), axis=0)
    weighted_one = normed_one_grad * gain_one
    input_grad = (
        residual_grad
        + scale_one_own * weighted_one
        - hidden_own
        * scale_one_own**3
        * jnp.mean(weighted_one * hidden_own, axis=-1, keepdims=True)
    )
    small_got, gain_all, input_grad = send(
        9,
        (("ctx",), "a", small.reshape(n_ctx, depth // n_ctx, -1)),
        (("ctx", "tp"), "g", gain_sum),
        (("tp",), "g", input_grad.astype(bf16)),
    )
    (small_all,) = send(10, (("ctx",), "g", jnp.sum(small_got.astype(f32), axis=0).astype(bf16)))
    small_all = small_all.reshape(depth, -1).astype(f32)
    gain_all = jnp.sum(gain_all, axis=0)
    grad_gate, grad_up, grad_down = spread(expert_all)
    k_end, v_end = q_end + pair_width, q_end + 2 * pair_width
    o_end = v_end + attended.shape[1]
    return (
        output.reshape(rows, width),
        input_grad.reshape(rows, width),
        gain_all[0],
        small_all[:, :q_end],
        small_all[:, q_end:k_end],
        small_all[:, k_end:v_end],
        small_all[:, v_end:o_end],
        gain_all[1],
        small_all[:, o_end : o_end + experts],
        grad_gate,
        grad_up,
        grad_down,
    )


def solution(mesh):
    sizes = dict(mesh.shape)
    return jax.shard_map(
        functools.partial(local, sizes),
        mesh=mesh,
        in_specs=(
            P(("fsdp", "ctx"), None),
            P(("fsdp", "ctx"), None),
            P("fsdp", None),
            P(("fsdp", "ctx"), None),
            P("fsdp"),
            P("fsdp", "tp"),
            P("fsdp", "tp"),
            P("fsdp", "tp"),
            P("fsdp", "tp"),
            P("fsdp"),
            P("fsdp", None),
            P("fsdp", None, "tp"),
            P("fsdp", None, "tp"),
            P("fsdp", None, "tp"),
        ),
        out_specs=(
            P(("fsdp", "ctx"), None),
            P(("fsdp", "ctx"), None),
            P("fsdp"),
            P("fsdp", "tp"),
            P("fsdp", "tp"),
            P("fsdp", "tp"),
            P("fsdp", "tp"),
            P("fsdp"),
            P("fsdp", None),
            P("fsdp", None, "tp"),
            P("fsdp", None, "tp"),
            P("fsdp", None, "tp"),
        ),
        check_vma=False,
    )
```

```python
import functools
import math

import jax
import jax.numpy as jnp
from jax import lax
from jax.experimental import pallas as pl
from jax.experimental.pallas import tpu as pltpu
from jax.sharding import PartitionSpec as P

HEAD_SIZE = 64
CAP = 128
MESH = pl.DeviceIdType.MESH

norm_eps = 1e-06
rope_base = 10000.0
branch_scale = 0.22
highest = lax.Precision.HIGHEST
bf16 = jnp.bfloat16
f32 = jnp.float32


def offset(slot, n):
    return slot // 2 + slot % 2 * (n // 2)


def exchange_kernel(plan, sizes, *refs):
    count = len(plan)
    ins, outs = refs[:count], refs[count : 2 * count]
    send_sem, recv_sem, self_sem = refs[2 * count :]

    def place(axes, step):
        offsets = []
        for axis in reversed(axes):
            offsets.append(step % sizes[axis])
            step //= sizes[axis]
        coords = {}
        for axis, offset in zip(axes, offsets[::-1]):
            here = lax.axis_index(axis)
            coords[axis] = lax.rem(here + offset, sizes[axis]) if offset else here
        return coords

    def flat(axes, coords):
        index = 0
        for axis in axes:
            index = index * sizes[axis] + coords[axis]
        return index

    groups = {}
    for axes, _ in plan:
        for step in range(1, math.prod(sizes[a] for a in axes)):
            full, rest = {}, step
            for axis in reversed(axes):
                full[axis] = rest % sizes[axis]
                rest //= sizes[axis]
            key = tuple(sorted((a, o) for a, o in full.items() if o))
            groups[key] = (axes, step)
    barrier = pltpu.get_barrier_semaphore()
    for axes, step in groups.values():
        pl.semaphore_signal(barrier, inc=1, device_id=place(axes, step), device_id_type=MESH)
    pl.semaphore_wait(barrier, len(groups))

    copies = []
    for at, (axes, mode) in enumerate(plan):
        mine = flat(axes, place(axes, 0))
        for step in range(1, math.prod(sizes[a] for a in axes)):
            if mode == "f":
                peer = place(axes, offset(step, sizes[axes[0]]))
                source, slot = ins[at].at[step], step
            else:
                peer = place(axes, step)
                source = ins[at] if mode == "g" else ins[at].at[flat(axes, peer)]
                slot = mine
            copy = pltpu.make_async_remote_copy(
                src_ref=source,
                dst_ref=outs[at].at[slot],
                send_sem=send_sem.at[at, step],
                recv_sem=recv_sem.at[at, step],
                device_id=peer,
                device_id_type=MESH,
            )
            copy.start()
            copies.append(copy)
        if mode == "f":
            mine = 0
        own = pltpu.make_async_copy(
            ins[at] if mode == "g" else ins[at].at[mine], outs[at].at[mine], self_sem.at[at]
        )
        own.start()
        copies.append(own)
    for copy in copies:
        copy.wait()


def exchange(sizes, collective_id, *items):
    plan = [(axes, mode) for axes, mode, _ in items]
    arrays = [array for _, _, array in items]
    outs = []
    most = 1
    for axes, mode, array in items:
        n = math.prod(sizes[a] for a in axes)
        most = max(most, n)
        shape = (n,) + array.shape if mode == "g" else array.shape
        outs.append(jax.ShapeDtypeStruct(shape, array.dtype))
    count = len(items)
    moved = sum(math.prod(o.shape) * o.dtype.itemsize for o in outs)
    return pl.pallas_call(
        functools.partial(exchange_kernel, plan, sizes),
        out_shape=outs,
        in_specs=[pl.BlockSpec(memory_space=pl.ANY)] * count,
        out_specs=[pl.BlockSpec(memory_space=pl.ANY)] * count,
        scratch_shapes=[
            pltpu.SemaphoreType.DMA((count, most)),
            pltpu.SemaphoreType.DMA((count, most)),
            pltpu.SemaphoreType.DMA((count,)),
        ],
        compiler_params=pltpu.CompilerParams(collective_id=collective_id, has_side_effects=True),
        cost_estimate=pl.CostEstimate(flops=0, bytes_accessed=20 * moved, transcendentals=0),
        name="exchange_%d" % collective_id,
    )(*arrays)


def spread_kernel(pieces_ref, *out_refs):
    for which, out_ref in enumerate(out_refs):
        turned = jnp.swapaxes(pieces_ref[:, which].astype(f32), 0, 1)
        out_ref[...] = turned.reshape(out_ref.shape)


def spread(pieces):
    experts, count, depth, ff = pieces.shape
    block = 64
    outs = pl.pallas_call(
        spread_kernel,
        grid=(depth // block,),
        out_shape=[jax.ShapeDtypeStruct((depth * experts, ff), f32)] * count,
        in_specs=[pl.BlockSpec((experts, count, block, ff), lambda i: (0, 0, i, 0))],
        out_specs=[pl.BlockSpec((block * experts, ff), lambda i: (i, 0))] * count,
        compiler_params=pltpu.CompilerParams(vmem_limit_bytes=40 * 1024 * 1024),
        name="spread",
    )(pieces)
    return [out.reshape(depth, experts, ff) for out in outs]


def attention_kernel(groups, starts_ref, first_ref, queries_ref, pairs_ref, out_ref, probs):
    rows = queries_ref.shape[0]
    total, both = pairs_ref.shape
    pair_width = both // 2
    block = 512
    blocks = [slice(at, at + block) for at in range(0, total, block)]
    places = jnp.concatenate(
        [first_ref[0, 0] + lax.broadcasted_iota(jnp.int32, (rows, 1), 0)] * groups, axis=0
    )
    starts = jnp.concatenate([starts_ref[...]] * groups, axis=0)
    parts = []
    for head in range(pair_width // HEAD_SIZE):
        at = [(head * groups + g) * HEAD_SIZE for g in range(groups)]
        queries = jnp.concatenate([queries_ref[:, a : a + HEAD_SIZE] for a in at], axis=0)
        own = slice(head * HEAD_SIZE, (head + 1) * HEAD_SIZE)
        own_values = slice(pair_width + own.start, pair_width + own.stop)
        top = jnp.full((rows * groups, 1), -1e30, f32)
        for part in blocks:
            key_rows = part.start + lax.broadcasted_iota(jnp.int32, (1, block), 1)
            allowed = (key_rows >= starts) & (key_rows <= places)
            scores = contract_cols(queries, pairs_ref[part, own]) * HEAD_SIZE ** (-0.5)
            scores = jnp.where(allowed, scores, -1e30)
            probs[:, part] = scores
            top = jnp.maximum(top, jnp.max(scores, axis=1, keepdims=True))
        count = jnp.zeros((rows * groups, 1), f32)
        for part in blocks:
            raised = jnp.exp(probs[:, part] - top)
            probs[:, part] = raised
            count += jnp.sum(raised, axis=1, keepdims=True)
        share = 1.0 / count
        attended = jnp.zeros((rows * groups, HEAD_SIZE), f32)
        for part in blocks:
            attended += mm((probs[:, part] * share).astype(bf16), pairs_ref[part, own_values])
        parts += [attended[g * rows : (g + 1) * rows] for g in range(groups)]
    out_ref[...] = jnp.concatenate(parts, axis=1).astype(bf16)


def attention(starts, first_row, queries, pairs, pair_width):
    rows, q_width = queries.shape
    total = pairs.shape[0]
    groups = q_width // pair_width
    vmem = pl.BlockSpec(memory_space=pltpu.VMEM)
    return pl.pallas_call(
        functools.partial(attention_kernel, groups),
        out_shape=jax.ShapeDtypeStruct((rows, q_width), bf16),
        in_specs=[vmem, pl.BlockSpec(memory_space=pltpu.SMEM), vmem, vmem],
        out_specs=vmem,
        scratch_shapes=[pltpu.VMEM((rows * groups, total), f32)],
        compiler_params=pltpu.CompilerParams(vmem_limit_bytes=40 * 1024 * 1024),
        cost_estimate=pl.CostEstimate(
            flops=4 * rows * q_width * total, bytes_accessed=4 << 20, transcendentals=rows * total * 4
        ),
        name="attention",
    )(starts.reshape(rows, 1), first_row.reshape(1, 1), queries, pairs)


def attention_back_kernel(groups, starts_ref, first_ref, queries_ref, grads_ref, pairs_ref, query_out, pair_out, probs, back):
    rows = queries_ref.shape[0]
    total, both = pairs_ref.shape
    pair_width = both // 2
    block = 512
    blocks = [slice(at, at + block) for at in range(0, total, block)]
    scale = HEAD_SIZE ** (-0.5)
    places = jnp.concatenate([first_ref[0, 0] + lax.broadcasted_iota(jnp.int32, (rows, 1), 0)] * groups, axis=0)
    starts = jnp.concatenate([starts_ref[...]] * groups, axis=0)
    query_parts, key_parts, value_parts = [], [], []
    for head in range(pair_width // HEAD_SIZE):

        def heads_of(ref):
            at = [(head * groups + g) * HEAD_SIZE for g in range(groups)]
            return jnp.concatenate([ref[:, a : a + HEAD_SIZE] for a in at], axis=0)

        queries, grads = heads_of(queries_ref), heads_of(grads_ref)
        own = slice(head * HEAD_SIZE, (head + 1) * HEAD_SIZE)
        own_values = slice(pair_width + own.start, pair_width + own.stop)
        top = jnp.full((rows * groups, 1), -1e30, f32)
        for part in blocks:
            key_rows = part.start + lax.broadcasted_iota(jnp.int32, (1, block), 1)
            allowed = (key_rows >= starts) & (key_rows <= places)
            scores = contract_cols(queries, pairs_ref[part, own]) * scale
            scores = jnp.where(allowed, scores, -1e30)
            probs[:, part] = scores
            top = jnp.maximum(top, jnp.max(scores, axis=1, keepdims=True))
        count = jnp.zeros((rows * groups, 1), f32)
        for part in blocks:
            raised = jnp.exp(probs[:, part] - top)
            probs[:, part] = raised
            count += jnp.sum(raised, axis=1, keepdims=True)
        share = 1.0 / count
        mean = jnp.zeros((rows * groups, 1), f32)
        for part in blocks:
            weights = probs[:, part] * share
            probs[:, part] = weights
            prob_grad = contract_cols(grads, pairs_ref[part, own_values])
            back[:, part] = prob_grad
            mean += jnp.sum(weights * prob_grad, axis=1, keepdims=True)
        query_grad = jnp.zeros((rows * groups, HEAD_SIZE), f32)
        keys_here, values_here = [], []
        for part in blocks:
            weights = probs[:, part]
            score_grad = (weights * (back[:, part] - mean)).astype(bf16)
            query_grad += mm(score_grad, pairs_ref[part, own])
            keys_here.append((contract_rows(score_grad, queries) * scale).astype(bf16))
            values_here.append(contract_rows(weights.astype(bf16), grads).astype(bf16))
        query_grad = query_grad * scale
        query_parts += [query_grad[g * rows : (g + 1) * rows] for g in range(groups)]
        key_parts.append(jnp.concatenate(keys_here, axis=0))
        value_parts.append(jnp.concatenate(values_here, axis=0))
    query_out[...] = jnp.concatenate(query_parts, axis=1)
    pair_out[...] = jnp.concatenate(key_parts + value_parts, axis=1)


def attention_back(starts, first_row, queries, grads, pairs, pair_width):
    rows, q_width = queries.shape
    total = pairs.shape[0]
    groups = q_width // pair_width
    vmem = pl.BlockSpec(memory_space=pltpu.VMEM)
    return pl.pallas_call(
        functools.partial(attention_back_kernel, groups),
        out_shape=[
            jax.ShapeDtypeStruct((rows, q_width), f32),
            jax.ShapeDtypeStruct((total, 2 * pair_width), bf16),
        ],
        in_specs=[vmem, pl.BlockSpec(memory_space=pltpu.SMEM), vmem, vmem, vmem],
        out_specs=[vmem, vmem],
        scratch_shapes=[pltpu.VMEM((rows * groups, total), f32)] * 2,
        compiler_params=pltpu.CompilerParams(vmem_limit_bytes=48 * 1024 * 1024),
        cost_estimate=pl.CostEstimate(
            flops=10 * rows * q_width * total, bytes_accessed=8 << 20, transcendentals=rows * total * 4
        ),
        name="attention_back",
    )(starts.reshape(rows, 1), first_row.reshape(1, 1), queries, grads, pairs)


def expert_kernel(
    n,
    n_fsdp,
    part,
    rows_ref,
    probs_ref,
    grads_ref,
    slices_ref,
    norm_got,
    mixed_got,
    gate_got,
    wgrad_ref,
    w_ref,
    wgrad_buf,
    wgrad_got,
    norm_buf,
    probs_buf,
    both_buf,
    weighted_buf,
    back_buf,
    mixed_buf,
    gate_buf,
    send_sems,
    recv_sems,
    wgrad_send,
    wgrad_recv,
):
    me, fsdp_at = lax.axis_index("ctx"), lax.axis_index("fsdp")
    hidden = w_ref.shape[1] // 3

    def chunk(ref, k):
        return ref.at[pl.ds(pl.multiple_of(k * CAP, CAP), CAP)]

    def copy(which, k, source, target, place):
        return pltpu.make_async_remote_copy(
            src_ref=source,
            dst_ref=target,
            send_sem=send_sems.at[which, k],
            recv_sem=recv_sems.at[which, k],
            device_id={"ctx": lax.rem(place, n)},
            device_id_type=MESH,
        )

    def out_copies(k):
        place = me + offset(k, n)
        return (
            copy(0, k, chunk(rows_ref, k), chunk(norm_buf, k), place),
            copy(1, k, probs_ref.at[k], probs_buf.at[k], place),
        )

    def back_copies(k):
        place = me + n - offset(k, n)
        return (
            copy(2, k, chunk(back_buf, k), chunk(norm_got, k), place),
            copy(3, k, gate_buf.at[k], gate_got.at[k], place),
            copy(4, k, chunk(mixed_buf, k), chunk(mixed_got, k), place),
        )

    barrier = pltpu.get_barrier_semaphore()
    for k in range(1, n):
        pl.semaphore_signal(
            barrier, inc=1, device_id={"ctx": lax.rem(me + k, n)}, device_id_type=MESH
        )
    for k in range(1, n_fsdp):
        pl.semaphore_signal(
            barrier,
            inc=1,
            device_id={"fsdp": lax.rem(fsdp_at + k, n_fsdp)},
            device_id_type=MESH,
        )
    pl.semaphore_wait(barrier, n - 1 + n_fsdp - 1)
    for k in range(1, 4):
        for item in out_copies(k):
            item.start()
    norm_buf[:CAP] = rows_ref[:CAP]
    probs_buf[0] = probs_ref[0]
    slim = wgrad_ref.shape[1]
    n_tp = hidden // slim
    for place in range(slices_ref.shape[0]):
        down = place // n_tp * part
        for which in range(3):
            start = which * hidden + place % n_tp * slim
            w_ref[down : down + part, start : start + slim] = slices_ref[place, which]
    same = lax.broadcasted_iota(jnp.int32, (CAP, CAP), 0) == lax.broadcasted_iota(
        jnp.int32, (CAP, CAP), 1
    )

    def pair(j, carry):
        @pl.when(j < n // 2 - 2)
        def _():
            for k in (2 * j + 4, 2 * j + 5):
                for item in out_copies(k):
                    item.start()

        for k in (2 * j, 2 * j + 1):

            @pl.when(k > 0)
            def _():
                for item in out_copies(k):
                    item.wait_recv()

        here = pl.ds(pl.multiple_of(j * 2 * CAP, 2 * CAP), 2 * CAP)
        gate_up = mm(norm_buf[here, :], w_ref[:, : 2 * hidden])
        down_back = mm(grads_ref[here, :], w_ref[:, 2 * hidden :])
        probs = jnp.concatenate(
            [
                jnp.sum(jnp.where(same, probs_buf[k][:1, :], 0.0), axis=1, keepdims=True)
                for k in (2 * j, 2 * j + 1)
            ],
            axis=0,
        )
        gate_pre, up_pre = gate_up[:, :hidden], gate_up[:, hidden:]
        sig = jax.nn.sigmoid(gate_pre)
        silu = gate_pre * sig
        activation = silu * up_pre
        gate_grad = branch_scale * jnp.sum(activation * down_back, axis=1, keepdims=True)
        act_grad = (branch_scale * probs) * down_back
        both_buf[here, :hidden] = (
            act_grad * up_pre * sig * (1.0 + gate_pre * (1.0 - sig))
        ).astype(bf16)
        both_buf[here, hidden:] = (act_grad * silu).astype(bf16)
        weighted_buf[here, :] = (probs * activation).astype(bf16)
        back_buf[here, :] = contract_cols(both_buf[here, :], w_ref[:, : 2 * hidden]).astype(bf16)
        for i in range(2):
            line = jnp.sum(
                jnp.where(same, gate_grad[i * CAP : (i + 1) * CAP], 0.0), axis=0, keepdims=True
            )
            gate_buf[2 * j + i] = jnp.broadcast_to(line, (8, CAP))
        mixed_buf[here, :] = contract_cols(weighted_buf[here, :], w_ref[:, 2 * hidden :]).astype(
            bf16
        )
        for k in (2 * j, 2 * j + 1):

            @pl.when(k > 0)
            def _():
                for item in back_copies(k):
                    item.start()

        return carry

    lax.fori_loop(0, n // 2, pair, 0)
    norm_got[:CAP] = back_buf[:CAP]
    mixed_got[:CAP] = mixed_buf[:CAP]
    gate_got[0] = gate_buf[0]

    def wgrad_copy(k):
        return pltpu.make_async_remote_copy(
            src_ref=wgrad_buf.at[k],
            dst_ref=wgrad_got.at[k],
            send_sem=wgrad_send.at[k],
            recv_sem=wgrad_recv.at[k],
            device_id={"fsdp": lax.rem(fsdp_at + k, n_fsdp)},
            device_id_type=MESH,
        )

    def weight_grads(j, carry):
        k = lax.rem(j + 1, n_fsdp)
        here = pl.ds(pl.multiple_of(lax.rem(fsdp_at + k, n_fsdp) * part, part), part)
        gate_up = contract_rows(norm_buf[:, here], both_buf[...]).astype(bf16)
        down = (contract_rows(grads_ref[:, here], weighted_buf[...]) * branch_scale).astype(bf16)
        for piece in range(hidden // slim):
            for which in range(3):
                row = (piece * 3 + which) * part
                if which < 2:
                    start = which * hidden + piece * slim
                    wgrad_buf[k, row : row + part, :] = gate_up[:, start : start + slim]
                else:
                    wgrad_buf[k, row : row + part, :] = down[:, piece * slim : (piece + 1) * slim]

        @pl.when(k > 0)
        def _():
            wgrad_copy(k).start()

        return carry

    lax.fori_loop(0, n_fsdp, weight_grads, 0)
    for k in range(1, n_fsdp):
        wgrad_copy(k).wait()

    def summed(j, carry):
        at = pl.ds(pl.multiple_of(j * part, part), part)
        total = wgrad_buf[0, at, :].astype(f32)
        for k in range(1, n_fsdp):
            total += wgrad_got[k, at, :].astype(f32)
        wgrad_ref[at, :] = total.astype(bf16)
        return carry

    lax.fori_loop(0, wgrad_buf.shape[1] // part, summed, 0)
    for k in range(1, n):
        for item in out_copies(k):
            item.wait_send()
        for item in back_copies(k):
            item.wait()


def expert_of_place(sizes, rows_sent, probs_sent, grad_rows, expert_w):
    n = sizes["ctx"]
    total, width = rows_sent.shape
    n_fsdp, n_tp = sizes["fsdp"], sizes["tp"]
    hidden, part = expert_w.shape[3] * n_tp, width // n_fsdp
    owned = (n_tp * 3 * part, hidden // n_tp)
    like = jax.ShapeDtypeStruct
    vmem = pl.BlockSpec(memory_space=pltpu.VMEM)
    return pl.pallas_call(
        functools.partial(expert_kernel, n, n_fsdp, part),
        out_shape=[
            like((total, width), bf16),
            like((total, width), bf16),
            like(probs_sent.shape, f32),
            like(owned, bf16),
        ],
        in_specs=[vmem] * 4,
        out_specs=[vmem] * 4,
        scratch_shapes=[
            pltpu.VMEM((width, 3 * hidden), bf16),
            pltpu.VMEM((n_fsdp,) + owned, bf16),
            pltpu.VMEM((n_fsdp,) + owned, bf16),
            pltpu.VMEM((total, width), bf16),
            pltpu.VMEM(probs_sent.shape, f32),
            pltpu.VMEM((total, 2 * hidden), bf16),
            pltpu.VMEM((total, hidden), bf16),
            pltpu.VMEM((total, width), bf16),
            pltpu.VMEM((total, width), bf16),
            pltpu.VMEM(probs_sent.shape, f32),
            pltpu.SemaphoreType.DMA((5, n)),
            pltpu.SemaphoreType.DMA((5, n)),
            pltpu.SemaphoreType.DMA((n_fsdp,)),
            pltpu.SemaphoreType.DMA((n_fsdp,)),
        ],
        compiler_params=pltpu.CompilerParams(
            collective_id=3, has_side_effects=True, vmem_limit_bytes=48 * 1024 * 1024
        ),
        cost_estimate=pl.CostEstimate(
            flops=6 * 2 * total * width * hidden * 3, bytes_accessed=100 << 20, transcendentals=0
        ),
        name="expert_of_place",
    )(rows_sent, probs_sent, grad_rows, expert_w)


def rope_tables(places, columns):
    column = jnp.arange(columns, dtype=jnp.int32)
    steps = (column % (HEAD_SIZE // 2)).astype(f32)
    frequencies = jnp.exp(steps * (-2.0 * math.log(rope_base) / HEAD_SIZE))
    angles = places.astype(f32)[:, None] * frequencies[None, :]
    first = (column % HEAD_SIZE < HEAD_SIZE // 2)[None, :]
    sine = jnp.sin(angles)
    return jnp.cos(angles), jnp.where(first, -sine, sine), first


def turn(values, cosine, sine, first):
    half = HEAD_SIZE // 2
    other = jnp.where(first, jnp.roll(values, -half, axis=1), jnp.roll(values, half, axis=1))
    return values * cosine + other * sine


def contract_rows(left, right, precision=None):
    return lax.dot_general(
        left, right, (((0,), (0,)), ((), ())), precision=precision, preferred_element_type=f32
    )


def contract_cols(left, right, precision=None):
    return lax.dot_general(
        left, right, (((1,), (1,)), ((), ())), precision=precision, preferred_element_type=f32
    )


def mm(left, right):
    return jnp.dot(left, right, preferred_element_type=f32)


def local(
    sizes,
    inputs,
    cotangent,
    lengths,
    expert_ids,
    attn_gain,
    w_query,
    key_weight,
    value_weight,
    w_output,
    ffn_gain,
    w_router,
    w_gate,
    w_up,
    w_down,
):
    rows, width = inputs.shape
    n_fsdp, n_ctx, n_tp = sizes["fsdp"], sizes["ctx"], sizes["tp"]
    experts = w_router.shape[1]
    depth, _, ff = w_gate.shape
    per_ctx = experts // n_ctx
    send = functools.partial(exchange, sizes)
    ctx_at, tp_at = lax.axis_index("ctx"), lax.axis_index("tp")

    first = ctx_at * per_ctx
    own_slices = jnp.stack(
        [
            lax.dynamic_slice_in_dim(w, first, per_ctx, 1).transpose(1, 0, 2)
            for w in (w_gate, w_up, w_down)
        ],
        axis=1,
    )
    lines = depth // 128

    def lined(gain):
        return jnp.pad(gain.reshape(lines, 128), ((0, 16 - lines), (0, 0)))

    qkv_w, gain_one, expert_slices = send(
        0,
        (("fsdp",), "g", jnp.concatenate([w_query, key_weight, value_weight], axis=1)),
        (("fsdp",), "g", lined(attn_gain)),
        (("tp",), "a", own_slices),
    )
    qkv_w = qkv_w.reshape(width, -1)
    gain_one = gain_one[:, :lines].reshape(width).astype(f32)
    expert_w = lax.all_gather(expert_slices, "fsdp", axis=0, tiled=True)

    chosen = jnp.any(
        expert_ids[:, :, None] == jnp.arange(experts, dtype=jnp.int32)[None, None, :], axis=1
    )
    offsets = [offset(slot, n_ctx) for slot in range(n_ctx)]
    ctx_order = lax.rem(ctx_at + jnp.array(offsets, dtype=jnp.int32), n_ctx)
    mine = ctx_order * per_ctx + tp_at
    chosen_mine = jnp.any(expert_ids[None, :, :] == mine[:, None, None], axis=2)
    earlier = jnp.arange(rows)[:, None] < jnp.arange(rows)[None, :]
    rank = mm(chosen_mine.astype(bf16), earlier.astype(bf16))
    slots = jnp.arange(CAP, dtype=f32)
    picks = (chosen_mine[:, None, :] & (rank[:, None, :] == slots[None, :, None])).astype(bf16)
    picks_flat = picks.reshape(n_ctx * CAP, rows)

    lengths_row = lengths[0]
    query_rows = ctx_at * rows + jnp.arange(rows, dtype=jnp.int32)
    seq_ends = jnp.cumsum(lengths_row)
    passed = (query_rows[:, None] >= seq_ends[None, :]).astype(jnp.int32)
    starts = jnp.sum(passed * lengths_row[None, :], axis=1)
    q_end, pair_width = w_query.shape[1], key_weight.shape[1]
    turned = q_end + pair_width
    cosine, sine, first_half = rope_tables(query_rows - starts, turned)
    hidden_in = inputs.astype(f32)
    scale_one = lax.rsqrt(jnp.mean(hidden_in * hidden_in, axis=-1, keepdims=True) + norm_eps)
    normed_one = (hidden_in * scale_one * gain_one).astype(bf16)
    qkv = mm(normed_one, qkv_w)
    queries_keys = turn(qkv[:, :turned], cosine, sine, first_half).astype(bf16)
    queries = queries_keys[:, :q_end]
    pairs_local = jnp.concatenate(
        [queries_keys[:, q_end:], qkv[:, turned:].astype(bf16)], axis=1
    )
    grads_sent = mm(picks_flat, cotangent).astype(bf16).reshape(n_ctx, CAP, width)
    pairs_all, output_w, gain_two, router_all, grad_rows = send(
        1,
        (("ctx",), "g", pairs_local),
        (("fsdp",), "g", w_output),
        (("fsdp",), "g", lined(ffn_gain)),
        (("fsdp",), "g", jnp.pad(w_router, ((0, 0), (0, 128 - experts)))),
        (("ctx",), "f", grads_sent),
    )
    output_w = output_w.reshape(width, -1)
    gain_two = gain_two[:, :lines].reshape(width).astype(f32)
    router_w = router_all.reshape(width, 128)[:, :experts]
    grad_rows = grad_rows.reshape(n_ctx * CAP, width)
    total_rows = n_ctx * rows
    pairs_all = pairs_all.reshape(total_rows, 2 * pair_width)
    attended = attention(starts, ctx_at * rows, queries, pairs_all, pair_width)
    quarter = rows // n_tp

    def quarter_of(array):
        return lax.dynamic_slice_in_dim(array, tp_at * quarter, quarter, 0)

    attn_part = contract_cols(attended, output_w).astype(bf16)
    (attn_parts,) = send(2, (("tp",), "a", attn_part.reshape(n_tp, quarter, width)))
    hidden_own, scale_one_own = quarter_of(hidden_in), quarter_of(scale_one)
    residual_own = hidden_own + branch_scale * jnp.sum(attn_parts.astype(f32), axis=0)

    scale_two_own = lax.rsqrt(jnp.mean(residual_own * residual_own, axis=-1, keepdims=True) + norm_eps)
    normed_two_own = (residual_own * scale_two_own * gain_two).astype(bf16)
    (normed_two,) = send(11, (("tp",), "g", normed_two_own))
    normed_two = normed_two.reshape(rows, width)
    logits = mm(normed_two, router_w)
    route_masked = jnp.where(chosen, logits, -1e30)
    route_exp = jnp.exp(route_masked - jnp.max(route_masked, axis=-1, keepdims=True))
    gate_probs = route_exp / jnp.sum(route_exp, axis=-1, keepdims=True)
    probs_mine = lax.dynamic_index_in_dim(
        gate_probs.T.reshape(n_ctx, per_ctx, rows), tp_at, 1, keepdims=False
    )
    probs_mine = jnp.take(probs_mine, ctx_order, axis=0)
    probs_sent = jnp.sum(picks.astype(f32) * probs_mine[:, None, :], axis=2)
    rows_sent = mm(picks_flat, normed_two).astype(bf16)
    probs_sent = jnp.broadcast_to(probs_sent[:, None, :], (n_ctx, 8, CAP))
    norm_grad_got, mixed_got, gate_grad_got, expert_grad = expert_of_place(
        sizes, rows_sent, probs_sent, grad_rows, expert_w
    )

    norm_grad_part = contract_rows(picks_flat, norm_grad_got)
    gate_grad_part = jnp.sum(picks.astype(f32) * gate_grad_got[:, 0, :, None], axis=1)
    norm_grad_parts, gate_grad_parts, pieces = send(
        5,
        (("tp",), "a", norm_grad_part.astype(bf16).reshape(n_tp, quarter, width)),
        (("tp",), "g", gate_grad_part),
        (("tp",), "a", expert_grad.reshape(n_tp, 3, depth, ff)),
    )

    pairs = [[2 * i, 2 * i + 1] for i in range(n_ctx // 2)]
    rings = [list(range(start, n_ctx, 2)) for start in range(2)]
    pieces = lax.all_gather(pieces, "ctx", axis=0, tiled=True, axis_index_groups=pairs)

    slot_of = jnp.array([offsets.index(k) for k in range(n_ctx)], dtype=jnp.int32)
    back_order = slot_of[lax.rem(jnp.arange(n_ctx, dtype=jnp.int32) + n_ctx - ctx_at, n_ctx)]
    gate_grads = jnp.take(gate_grad_parts, back_order, axis=1)
    gate_grads = gate_grads.transpose(2, 1, 0).reshape(rows, experts)
    route_grad = gate_probs * (
        gate_grads - jnp.sum(gate_probs * gate_grads, axis=-1, keepdims=True)
    )
    grad_router = contract_rows(normed_two.astype(f32), route_grad, highest)
    router_back = contract_cols(quarter_of(route_grad), router_w.astype(f32), highest)
    normed_grad = jnp.sum(norm_grad_parts.astype(f32), axis=0) + router_back
    weighted_two = normed_grad * gain_two
    grad_ffn_part = jnp.sum(normed_grad * residual_own * scale_two_own, axis=0)
    residual_grad = (
        quarter_of(cotangent).astype(f32)
        + scale_two_own * weighted_two
        - residual_own
        * scale_two_own**3
        * jnp.mean(weighted_two * residual_own, axis=-1, keepdims=True)
    )
    (attn_in,) = send(6, (("tp",), "g", (branch_scale * residual_grad).astype(bf16)))
    attn_in = attn_in.reshape(rows, width)

    side = jnp.pad(grad_router, ((0, 0), (0, 128 - experts)))
    early = jnp.concatenate([contract_rows(attn_in, attended), side], axis=1).astype(bf16)
    mixed_part = contract_rows(picks_flat, mixed_got).astype(bf16)
    attended_grad = mm(attn_in, output_w).astype(bf16)

    query_grad_rot, pair_grads = attention_back(
        starts, ctx_at * rows, queries, attended_grad, pairs_all, pair_width
    )
    pieces, pair_grads, mixed_part, early = lax.optimization_barrier(
        (pieces, pair_grads, mixed_part, early)
    )
    expert_all = lax.all_gather(pieces, "ctx", axis=0, tiled=True, axis_index_groups=rings)
    pair_got, mixed_parts, early_got = send(
        7,
        (("ctx",), "a", pair_grads.reshape(n_ctx, rows, 2 * pair_width)),
        (("tp",), "a", mixed_part.reshape(n_tp, quarter, width)),
        (("fsdp",), "a", early.reshape(n_fsdp, depth, -1)),
    )
    pair_owned = jnp.sum(pair_got.astype(f32), axis=0)
    turned_back = turn(
        jnp.concatenate([query_grad_rot, pair_owned[:, :pair_width]], axis=1),
        cosine,
        -sine,
        first_half,
    )
    qkv_grad = jnp.concatenate([turned_back, pair_owned[:, pair_width:]], axis=1).astype(bf16)
    normed_one_part = contract_cols(qkv_grad, qkv_w)
    grad_gain_part = jnp.sum(normed_one_part * hidden_in * scale_one, axis=0)
    grad_qkv = contract_rows(normed_one, qkv_grad).astype(bf16)
    output = residual_own + branch_scale * jnp.sum(mixed_parts.astype(f32), axis=0)

    gain_parts = jnp.stack([grad_gain_part, grad_ffn_part]).reshape(2, n_fsdp, depth)
    gain_chunks = jnp.pad(gain_parts.transpose(1, 0, 2), ((0, 0), (0, 6), (0, 0)))
    one_parts, qkv_got, gain_got, output = send(
        8,
        (("tp",), "a", normed_one_part.astype(bf16).reshape(n_tp, quarter, width)),
        (("fsdp",), "a", grad_qkv.reshape(n_fsdp, depth, -1)),
        (("fsdp",), "a", gain_chunks),
        (("tp",), "g", output.astype(bf16)),
    )
    small = jnp.concatenate(
        [
            jnp.sum(qkv_got.astype(f32), axis=0).astype(bf16),
            jnp.sum(early_got.astype(f32), axis=0).astype(bf16),
        ],
        axis=1,
    )
    gain_sum = jnp.sum(gain_got, axis=0)
    normed_one_grad = jnp.sum(one_parts.astype(f32), axis=0)
    weighted_one = normed_one_grad * gain_one
    input_grad = (
        residual_grad
        + scale_one_own * weighted_one
        - hidden_own
        * scale_one_own**3
        * jnp.mean(weighted_one * hidden_own, axis=-1, keepdims=True)
    )
    small_got, gain_all, input_grad = send(
        9,
        (("ctx",), "a", small.reshape(n_ctx, depth // n_ctx, -1)),
        (("ctx", "tp"), "g", gain_sum),
        (("tp",), "g", input_grad.astype(bf16)),
    )
    (small_all,) = send(10, (("ctx",), "g", jnp.sum(small_got.astype(f32), axis=0).astype(bf16)))
    small_all = small_all.reshape(depth, -1).astype(f32)
    gain_all = jnp.sum(gain_all, axis=0)
    grad_gate, grad_up, grad_down = spread(expert_all)
    k_end, v_end = q_end + pair_width, q_end + 2 * pair_width
    o_end = v_end + attended.shape[1]
    return (
        output.reshape(rows, width),
        input_grad.reshape(rows, width),
        gain_all[0],
        small_all[:, :q_end],
        small_all[:, q_end:k_end],
        small_all[:, k_end:v_end],
        small_all[:, v_end:o_end],
        gain_all[1],
        small_all[:, o_end : o_end + experts],
        grad_gate,
        grad_up,
        grad_down,
    )


def solution(mesh):
    sizes = dict(mesh.shape)
    return jax.shard_map(
        functools.partial(local, sizes),
        mesh=mesh,
        in_specs=(
            P(("fsdp", "ctx"), None),
            P(("fsdp", "ctx"), None),
            P("fsdp", None),
            P(("fsdp", "ctx"), None),
            P("fsdp"),
            P("fsdp", "tp"),
            P("fsdp", "tp"),
            P("fsdp", "tp"),
            P("fsdp", "tp"),
            P("fsdp"),
            P("fsdp", None),
            P("fsdp", None, "tp"),
            P("fsdp", None, "tp"),
            P("fsdp", None, "tp"),
        ),
        out_specs=(
            P(("fsdp", "ctx"), None),
            P(("fsdp", "ctx"), None),
            P("fsdp"),
            P("fsdp", "tp"),
            P("fsdp", "tp"),
            P("fsdp", "tp"),
            P("fsdp", "tp"),
            P("fsdp"),
            P("fsdp", None),
            P("fsdp", None, "tp"),
            P("fsdp", None, "tp"),
            P("fsdp", None, "tp"),
        ),
        check_vma=False,
    )
```
